32 devices in a mesh: noise: 4 (over y, x), nodes: 8 (over z, core).
Axes of the slice: x: 2, y: 2, z: 4, core: 2. Of those that a mesh axis runs over, the one named last changes fastest.
Arguments:
- inputs: bfloat16 [4, 8192, 512], P('noise', 'nodes'), may hold values from -6 to 6
- sigma: float32 [4], P('noise'), may hold values from 0.02 to 80
- neighbours: int32 [4, 8192, 16], P('noise', 'nodes'), may hold values from 0 to 8191, as said below
- cotangent: bfloat16 [4, 8192, 512], P('noise', 'nodes'), may hold values from -6 to 6
- inward_weight: float32 [512, 1536], P('nodes'), may hold values from -0.25 to 0.25
- inward_first: float32 [512, 1536], P('nodes'), may hold values from -512 to 512
- inward_second: float32 [512, 1536], P('nodes'), may hold values from 2730 to 10922
- outward_weight: float32 [512, 512], P('nodes'), may hold values from -0.5 to 0.5
- outward_first: float32 [512, 512], P('nodes'), may hold values from -512 to 512
- outward_second: float32 [512, 512], P('nodes'), may hold values from 2730 to 10922
- expand_weight: float32 [512, 2048], P('nodes'), may hold values from -0.25 to 0.25
- expand_first: float32 [512, 2048], P('nodes'), may hold values from -512 to 512
- expand_second: float32 [512, 2048], P('nodes'), may hold values from 2730 to 10922
- contract_weight: float32 [2048, 512], P('nodes'), may hold values from -0.25 to 0.25
- contract_first: float32 [2048, 512], P('nodes'), may hold values from -512 to 512
- contract_second: float32 [2048, 512], P('nodes'), may hold values from 2730 to 10922
- modulate_weight: float32 [512, 2048], P('nodes'), may hold values from -0.25 to 0.25
- modulate_first: float32 [512, 2048], P('nodes'), may hold values from -512 to 512
- modulate_second: float32 [512, 2048], P('nodes'), may hold values from 2730 to 10922
Outputs:
- outputs: bfloat16 [4, 8192, 512], P('noise', 'nodes')
- input_grad: float32 [4, 8192, 512], P('noise', 'nodes')
- inward_moment: float32 [512, 1536], P('nodes')
- inward_square: float32 [512, 1536], P('nodes')
- inward_fresh: float32 [512, 1536], P('nodes')
- outward_moment: float32 [512, 512], P('nodes')
- outward_square: float32 [512, 512], P('nodes')
- outward_fresh: float32 [512, 512], P('nodes')
- expand_moment: float32 [512, 2048], P('nodes')
- expand_square: float32 [512, 2048], P('nodes')
- expand_fresh: float32 [512, 2048], P('nodes')
- contract_moment: float32 [2048, 512], P('nodes')
- contract_square: float32 [2048, 512], P('nodes')
- contract_fresh: float32 [2048, 512], P('nodes')
- modulate_moment: float32 [512, 2048], P('nodes')
- modulate_square: float32 [512, 2048], P('nodes')
- modulate_fresh: float32 [512, 2048], P('nodes')
The draws below stay inside these ranges and needn't reach their ends.
Inputs may be any that keep to these rules, and one draw needn't show every extreme that they name: `neighbours`: column 0 of node i is i itself, column 1 is (i + 64) mod 8192, column 2 is (i - 64) mod 8192; every neighbour of node i is (i + t) mod 8192 for some t with |t| <= 64.
All inputs are finite; a program needn't handle non-finite values.
Results may differ from the reference program's by a relative error of at most 0.017.
Values may be sent and summed in bfloat16 or wider, within the bound.
No kernel may reach another device: no remote copies, remote signals or barrier semaphores. Data moves between devices by JAX's collectives and lax.ppermute only.
A program may use at most 128 MiB of HBM per device.

```python
import math
import jax
import jax.numpy as jnp
from jax import lax

D = 512
HEADS = 4
FF = 2048
NEIGH = 16
RIM = 64
STEP = 10
HEAD_DIM = 128
NODES = 8192
COPIES = 4
N_NOISE = 4


def draw_neighbours(key, part):
    key = jax.random.fold_in(key, 7)
    offsets = jax.random.randint(key, (COPIES, NODES, NEIGH - 3), -RIM, RIM + 1)
    fixed = jnp.array([0, RIM, -RIM], dtype=jnp.int32)
    fixed = jnp.broadcast_to(fixed[None, None, :], (COPIES, NODES, 3))
    shifts = jnp.concatenate([fixed, offsets.astype(jnp.int32)], axis=-1)
    anchor = jnp.arange(NODES, dtype=jnp.int32)[None, :, None]
    return ((anchor + shifts) % NODES).astype(jnp.int32)


def steps_of(stream_key, shape, cuts, least, top_value):
    level = 1.0
    for position, blocks in cuts:
        draws = jax.random.uniform(jax.random.fold_in(jax.random.fold_in(stream_key, 6), position), (blocks,), jnp.float32, least / len(cuts), top_value / len(cuts))
        level = level * jnp.repeat(jnp.exp(draws), shape[position] // blocks).reshape((-1,) + (1,) * (len(shape) - 1 - position))
    return level


def bell_draw(stream_key, extent, scale, most, cuts=(), kind=jnp.bfloat16):
    factor_of = steps_of(stream_key, extent, cuts, -0.22, 0.18) if cuts else 1.0
    entries = jax.random.normal(stream_key, extent, jnp.float32) * scale * factor_of
    return jnp.minimum(jnp.maximum(entries, -most), most).astype(kind)


def setup_inputs(seed: int = 0) -> dict:
    splits = jax.random.split(jax.random.key(seed), 20)
    return {
        "inputs": bell_draw(splits[0], (COPIES, NODES, D), 1.0, 6.0, ((0, 4), (1, 8))),
        "sigma": jnp.clip(jnp.exp(math.log(80.0) - 8.2940497 * jax.random.uniform(splits[1], (COPIES,), jnp.float32) ** steps_of(splits[1], (COPIES,), ((0, 4),), -0.2, 0.2)), 0.02, 80.0),
        "neighbours": draw_neighbours(jax.random.fold_in(splits[19], 71), 0),
        "cotangent": bell_draw(splits[3], (COPIES, NODES, D), 1.0, 6.0, ((0, 4), (1, 8))),
        "inward_weight": bell_draw(splits[4], (D, 3 * D), D ** -0.5, 0.25, ((0, 8),), jnp.float32),
        "inward_first": bell_draw(splits[5], (D, 3 * D), ((N_NOISE * NODES // 4) ** 0.5), 512.0, ((0, 8),), jnp.float32),
        "inward_second": jnp.clip(jnp.exp(math.log(10922.0) - 1.3864775 * jax.random.uniform(splits[6], (D, 3 * D), jnp.float32) ** steps_of(splits[6], (D, 3 * D), ((0, 8),), -0.2, 0.2)), 2730.0, 10922.0),
        "outward_weight": bell_draw(splits[7], (D, D), (D // 4) ** -0.5, 0.5, ((0, 8),), jnp.float32),
        "outward_first": bell_draw(splits[8], (D, D), ((N_NOISE * NODES // 4) ** 0.5), 512.0, ((0, 8),), jnp.float32),
        "outward_second": jnp.clip(jnp.exp(math.log(10922.0) - 1.3864775 * jax.random.uniform(splits[9], (D, D), jnp.float32) ** steps_of(splits[9], (D, D), ((0, 8),), -0.2, 0.2)), 2730.0, 10922.0),
        "expand_weight": bell_draw(splits[10], (D, FF), D ** -0.5, 0.25, ((0, 8),), jnp.float32),
        "expand_first": bell_draw(splits[11], (D, FF), ((N_NOISE * NODES // 4) ** 0.5), 512.0, ((0, 8),), jnp.float32),
        "expand_second": jnp.clip(jnp.exp(math.log(10922.0) - 1.3864775 * jax.random.uniform(splits[12], (D, FF), jnp.float32) ** steps_of(splits[12], (D, FF), ((0, 8),), -0.2, 0.2)), 2730.0, 10922.0),
        "contract_weight": bell_draw(splits[13], (FF, D), (FF // 4) ** -0.5, 0.25, ((0, 8),), jnp.float32),
        "contract_first": bell_draw(splits[14], (FF, D), ((N_NOISE * NODES // 4) ** 0.5), 512.0, ((0, 8),), jnp.float32),
        "contract_second": jnp.clip(jnp.exp(math.log(10922.0) - 1.3864775 * jax.random.uniform(splits[15], (FF, D), jnp.float32) ** steps_of(splits[15], (FF, D), ((0, 8),), -0.2, 0.2)), 2730.0, 10922.0),
        "modulate_weight": bell_draw(splits[16], (D, 4 * D), D ** -0.5, 0.25, ((0, 8),), jnp.float32),
        "modulate_first": bell_draw(splits[17], (D, 4 * D), ((N_NOISE * NODES // 4) ** 0.5), 512.0, ((0, 8),), jnp.float32),
        "modulate_second": jnp.clip(jnp.exp(math.log(10922.0) - 1.3864775 * jax.random.uniform(splits[18], (D, 4 * D), jnp.float32) ** steps_of(splits[18], (D, 4 * D), ((0, 8),), -0.2, 0.2)), 2730.0, 10922.0),
    }


@jax.custom_vjp
def low(v):
    return lax.optimization_barrier(v.astype(jnp.bfloat16)).astype(jnp.float32)

@jax.custom_vjp
def low_back(v):
    return v

def low_keep(v):
    return (low(v), None)

def low_pass(kept, grad):
    return (grad,)

def back_keep(v):
    return (v, None)

def back_low(kept, grad):
    return (low(grad),)
low.defvjp(low_keep, low_pass)
low_back.defvjp(back_keep, back_low)

def normalize(values):
    center = values - lax.optimization_barrier(jnp.mean(values, axis=-1, keepdims=True))
    spread = lax.optimization_barrier(jnp.mean(center * center, axis=-1, keepdims=True))
    return center * lax.rsqrt(spread + 1e-06)

def fourier(sigma):
    half = D // 2
    counter = jnp.arange(half).astype(jnp.float32)
    freqs = jnp.exp(counter * (math.log(64.0) / (half - 1)))
    phase = jnp.log(sigma)[:, None] * freqs[None, :]
    return jnp.concatenate([jnp.sin(phase), jnp.cos(phase)], axis=-1)

def attend_copy(queries, keys, values, neighbours):
    block = math.gcd(NODES, 512)
    count = NODES // block
    qblocks = queries.reshape(count, block, HEADS, HEAD_DIM)
    nblocks = neighbours.reshape(count, block, NEIGH)

    def one_block(pieces):
        qpart, npart = pieces
        kpart = keys[npart].reshape(block, NEIGH, HEADS, HEAD_DIM)
        vpart = values[npart].reshape(block, NEIGH, HEADS, HEAD_DIM)
        scores = jnp.einsum('bhd,bkhd->bkh', qpart, kpart, precision=lax.Precision.HIGHEST) / math.sqrt(HEAD_DIM)
        top = lax.optimization_barrier(jnp.max(scores, axis=1, keepdims=True))
        expo = jnp.exp(scores - top)
        probs = low(expo / lax.optimization_barrier(jnp.sum(expo, axis=1, keepdims=True)))
        mixed = jnp.einsum('bkh,bkhd->bhd', probs, vpart, precision=lax.Precision.HIGHEST)
        return mixed.reshape(block, D)
    return lax.map(jax.checkpoint(one_block), (qblocks, nblocks)).reshape(NODES, D)

def project(left, right):
    return jnp.einsum('cnd,de->cne', left, right, precision=lax.Precision.HIGHEST)

def layer(states, inward, outward, expand, contract, modulate, sigma, neighbours):
    w_in = low(inward)
    w_out = low(outward)
    w_exp = low(expand)
    w_con = low(contract)
    w_mod = low(modulate)
    cond = low(fourier(sigma))
    modulation = jnp.dot(cond, w_mod, precision=lax.Precision.HIGHEST)[:, None, :]
    scale_one = modulation[..., :D]
    shift_one = modulation[..., D:2 * D]
    scale_two = modulation[..., 2 * D:3 * D]
    shift_two = modulation[..., 3 * D:]
    first_in = low(normalize(states) * (1.0 + scale_one) + shift_one)
    joint = low(low_back(project(first_in, w_in)))
    attended = jax.vmap(attend_copy)(joint[..., :D], joint[..., D:2 * D], joint[..., 2 * D:], neighbours)
    attended = low(low_back(attended))
    mixed = states + low_back(project(attended, w_out))
    second_in = low(normalize(mixed) * (1.0 + scale_two) + shift_two)
    up_act = low_back(project(second_in, w_exp))
    swished = low(up_act * jax.nn.sigmoid(up_act))
    return mixed + low_back(project(swished, w_con))

def adamw(weight, first, second, grads):
    moment = 0.5 * first + 0.5 * grads
    square = 0.75 * second + 0.25 * grads * grads
    ratio = moment / (1.0 - 0.5 ** STEP) / (jnp.sqrt(square / (1.0 - 0.75 ** STEP)) + 1e-08)
    return (moment, square, weight - 0.02 * (ratio + 0.1 * weight))

def reference(inputs, sigma, neighbours, cotangent, inward_weight, inward_first, inward_second, outward_weight, outward_first, outward_second, expand_weight, expand_first, expand_second, contract_weight, contract_first, contract_second, modulate_weight, modulate_first, modulate_second):
    states = inputs.astype(jnp.float32)

    def wrapped(values, inward, outward, expand, contract, modulate):
        return layer(values, inward, outward, expand, contract, modulate, sigma, neighbours)
    final, pull = jax.vjp(wrapped, states, inward_weight, outward_weight, expand_weight, contract_weight, modulate_weight)
    grads = pull(cotangent.astype(jnp.float32))
    inward_new = adamw(inward_weight, inward_first, inward_second, grads[1])
    outward_new = adamw(outward_weight, outward_first, outward_second, grads[2])
    expand_new = adamw(expand_weight, expand_first, expand_second, grads[3])
    contract_new = adamw(contract_weight, contract_first, contract_second, grads[4])
    modulate_new = adamw(modulate_weight, modulate_first, modulate_second, grads[5])
    return (final.astype(jnp.bfloat16), grads[0], inward_new[0], inward_new[1], inward_new[2], outward_new[0], outward_new[1], outward_new[2], expand_new[0], expand_new[1], expand_new[2], contract_new[0], contract_new[1], contract_new[2], modulate_new[0], modulate_new[1], modulate_new[2])
```

```python
import functools
import math

import jax
import jax.numpy as jnp
from jax import lax
from jax.experimental import pallas as pl
from jax.experimental.pallas import tpu as pltpu
from jax.sharding import PartitionSpec as P

D = 512
HEADS = 4
NEIGH = 16
RIM = 64
STEP = 10
HEAD_DIM = 128
BLOCK = 128
WINDOW = BLOCK + 2 * RIM
AXES = ("noise", "nodes")
BF16 = jnp.bfloat16
F32 = jnp.float32
NONE = -1e30


def dot(left, right, left_dim, right_dim):
    return lax.dot_general(
        left, right, (((left_dim,), (right_dim,)), ((), ())), preferred_element_type=F32
    )


def fourier(sigma):
    half = D // 2
    counter = jnp.arange(half).astype(F32)
    freqs = jnp.exp(counter * (math.log(64.0) / (half - 1)))
    phase = jnp.log(sigma)[:, None] * freqs[None, :]
    return jnp.concatenate([jnp.sin(phase), jnp.cos(phase)], axis=-1)


def normalize_parts(values):
    center = values - jnp.mean(values, axis=-1, keepdims=True)
    inverse = lax.rsqrt(jnp.mean(center * center, axis=-1, keepdims=True) + 1e-06)
    return (center * inverse, inverse)


def norm_back(normed, inverse, grads):
    average = jnp.mean(grads, axis=-1, keepdims=True)
    along = jnp.mean(grads * normed, axis=-1, keepdims=True)
    return inverse * (grads - average - normed * along)


def adamw(weight, first, second, grads):
    moment = 0.5 * first + 0.5 * grads
    square = 0.75 * second + 0.25 * grads * grads
    ratio = moment / (1.0 - 0.5**STEP) / (jnp.sqrt(square / (1.0 - 0.75**STEP)) + 1e-08)
    return (moment, square, weight - 0.02 * (ratio + 0.1 * weight))


def params(mib, grid=1):
    return pltpu.CompilerParams(
        vmem_limit_bytes=mib * 2**20, dimension_semantics=("arbitrary",) * grid
    )


def cost(flops, moved):
    return pl.CostEstimate(flops=flops, bytes_accessed=moved, transcendentals=0)


def count_kernel(places_ref, bias_ref):
    places = places_ref[...]
    lanes = lax.broadcasted_iota(jnp.int32, (BLOCK, WINDOW), 1)
    count = jnp.zeros((BLOCK, WINDOW), F32)
    for k in range(NEIGH):
        count = count + (places[:, k : k + 1] == lanes).astype(F32)
    bias_ref[...] = jnp.where(count > 0.0, jnp.log(count), NONE)


def count_call(places):
    rows = places.shape[0]
    return pl.pallas_call(
        count_kernel,
        grid=(rows // BLOCK,),
        in_specs=[pl.BlockSpec((BLOCK, NEIGH), lambda i: (i, 0))],
        out_specs=pl.BlockSpec((BLOCK, WINDOW), lambda i: (i, 0)),
        out_shape=jax.ShapeDtypeStruct((rows, WINDOW), F32),
        compiler_params=params(32),
        cost_estimate=cost(rows * WINDOW * 48, rows * WINDOW * 4),
        name="neighbour_counts",
    )(places)


def attend_kernel(q_ref, low_ref, high_ref, bias_ref, out_ref, probs_ref):
    bias = bias_ref[...]
    scale = 1.0 / math.sqrt(HEAD_DIM)
    for h in range(HEADS):
        cols = slice(h * HEAD_DIM, (h + 1) * HEAD_DIM)
        vals = slice(D + h * HEAD_DIM, D + (h + 1) * HEAD_DIM)
        keys = jnp.concatenate([low_ref[:, cols], high_ref[:, cols]], axis=0)
        values = jnp.concatenate([low_ref[:, vals], high_ref[:, vals]], axis=0)
        scores = dot(q_ref[:, cols], keys, 1, 1) * scale + bias
        top = jnp.max(scores, axis=1, keepdims=True)
        expo = jnp.exp(scores - top)
        probs = (expo * (1.0 / jnp.sum(expo, axis=1, keepdims=True))).astype(BF16)
        probs_ref[:, h * WINDOW : (h + 1) * WINDOW] = probs
        out_ref[:, cols] = dot(probs, values, 1, 0).astype(BF16)


def attend_call(queries, keyvals, bias):
    rows = queries.shape[0]
    return pl.pallas_call(
        attend_kernel,
        grid=(rows // BLOCK,),
        in_specs=[
            pl.BlockSpec((BLOCK, D), lambda i: (i, 0)),
            pl.BlockSpec((BLOCK, 2 * D), lambda i: (i, 0)),
            pl.BlockSpec((BLOCK, 2 * D), lambda i: (i + 1, 0)),
            pl.BlockSpec((BLOCK, WINDOW), lambda i: (i, 0)),
        ],
        out_specs=[
            pl.BlockSpec((BLOCK, D), lambda i: (i, 0)),
            pl.BlockSpec((BLOCK, HEADS * WINDOW), lambda i: (i, 0)),
        ],
        out_shape=[
            jax.ShapeDtypeStruct((rows, D), BF16),
            jax.ShapeDtypeStruct((rows, HEADS * WINDOW), BF16),
        ],
        compiler_params=params(32),
        cost_estimate=cost(4 * rows * WINDOW * D, 6 * 2**20),
        name="attention_forward",
    )(queries, keyvals, keyvals, bias)


def attend_back_kernel(
    q_ref, low_ref, high_ref, probs_ref, grad_ref, dq_ref, dkv_ref, carry_ref
):
    step = pl.program_id(0)
    last = pl.num_programs(0) - 1
    scale = 1.0 / math.sqrt(HEAD_DIM)

    @pl.when(step == 0)
    def _():
        carry_ref[...] = jnp.zeros_like(carry_ref)

    @pl.when(step == last)
    def _():
        dkv_ref[...] = carry_ref[...].astype(BF16)

    @pl.when(step < last)
    def _():
        for h in range(HEADS):
            cols = slice(h * HEAD_DIM, (h + 1) * HEAD_DIM)
            vals = slice(D + h * HEAD_DIM, D + (h + 1) * HEAD_DIM)
            keys = jnp.concatenate([low_ref[:, cols], high_ref[:, cols]], axis=0)
            values = jnp.concatenate([low_ref[:, vals], high_ref[:, vals]], axis=0)
            grads = grad_ref[:, cols]
            probs = probs_ref[:, h * WINDOW : (h + 1) * WINDOW]
            wide = probs.astype(F32)
            d_probs = dot(grads, values, 1, 1)
            weighted = wide * d_probs
            total = jnp.sum(weighted, axis=1, keepdims=True)
            d_scores = ((weighted - wide * total) * scale).astype(BF16)
            dq_ref[:, cols] = dot(d_scores, keys, 1, 0).astype(BF16)
            d_keys = dot(d_scores, q_ref[:, cols], 0, 0)
            d_values = dot(probs, grads, 0, 0)
            dkv_ref[:, cols] = (carry_ref[:, cols] + d_keys[:BLOCK]).astype(BF16)
            dkv_ref[:, vals] = (carry_ref[:, vals] + d_values[:BLOCK]).astype(BF16)
            carry_ref[:, cols] = d_keys[BLOCK:]
            carry_ref[:, vals] = d_values[BLOCK:]


def attend_back_call(queries, keyvals, probs, grads):
    rows = queries.shape[0]
    count = rows // BLOCK
    here = lambda i: (jnp.minimum(i, count - 1), 0)
    return pl.pallas_call(
        attend_back_kernel,
        grid=(count + 1,),
        in_specs=[
            pl.BlockSpec((BLOCK, D), here),
            pl.BlockSpec((BLOCK, 2 * D), here),
            pl.BlockSpec((BLOCK, 2 * D), lambda i: (jnp.minimum(i + 1, count), 0)),
            pl.BlockSpec((BLOCK, HEADS * WINDOW), here),
            pl.BlockSpec((BLOCK, D), here),
        ],
        out_specs=[
            pl.BlockSpec((BLOCK, D), here),
            pl.BlockSpec((BLOCK, 2 * D), lambda i: (i, 0)),
        ],
        out_shape=[
            jax.ShapeDtypeStruct((rows, D), BF16),
            jax.ShapeDtypeStruct((rows + 2 * RIM, 2 * D), BF16),
        ],
        scratch_shapes=[pltpu.VMEM((BLOCK, 2 * D), F32)],
        compiler_params=params(32),
        cost_estimate=cost(8 * rows * WINDOW * D, 10 * 2**20),
        name="attention_backward",
    )(queries, keyvals, keyvals, probs, grads)


ROWS_MLP = 256
CHUNK = 512


def mlp_kernel(
    attended_ref, states_ref, cot_ref, mod_ref, w_out_ref, w_exp_ref, w_con_ref,
    final_ref, second_ref, swished_ref, d_up_ref, d_mixed_ref, d_att_ref, sums_ref,
):
    scale_two = mod_ref[2:3, :]
    shift_two = mod_ref[3:4, :]
    cot = cot_ref[...]
    mixed = states_ref[...].astype(F32) + dot(attended_ref[...], w_out_ref[...], 1, 0)
    normed, inverse = normalize_parts(mixed)
    second_in = (normed * (1.0 + scale_two) + shift_two).astype(BF16)
    second_ref[...] = second_in
    hidden = w_exp_ref.shape[1]
    final = mixed
    d_second = jnp.zeros_like(mixed)
    for start in range(0, hidden, CHUNK):
        part = slice(start, start + CHUNK)
        up = dot(second_in, w_exp_ref[:, part], 1, 0)
        gate = 0.5 + 0.5 * jnp.tanh(0.5 * up)
        product = up * gate
        swished = product.astype(BF16)
        swished_ref[:, part] = swished
        final = final + dot(swished, w_con_ref[part, :], 1, 0)
        d_swished = dot(cot, w_con_ref[part, :], 1, 1)
        d_up = (d_swished * (gate + product * (1.0 - gate))).astype(BF16)
        d_up_ref[:, part] = d_up
        d_second = d_second + dot(d_up, w_exp_ref[:, part], 1, 1)
    final_ref[...] = final.astype(BF16)

    @pl.when(pl.program_id(0) == 0)
    def _():
        sums_ref[...] = jnp.zeros_like(sums_ref)

    sums_ref[0:1, :] += jnp.sum(d_second * normed, axis=0, keepdims=True)
    sums_ref[1:2, :] += jnp.sum(d_second, axis=0, keepdims=True)
    d_mixed = cot.astype(F32) + norm_back(normed, inverse, d_second * (1.0 + scale_two))
    d_mixed_ref[...] = d_mixed
    d_att_ref[...] = dot(d_mixed.astype(BF16), w_out_ref[...], 1, 1).astype(BF16)


def mlp_call(attended, states, cot, mod, w_out, w_exp, w_con):
    rows = states.shape[0]
    hidden = w_exp.shape[1]
    some = lambda width: pl.BlockSpec((ROWS_MLP, width), lambda i: (i, 0))
    whole = lambda array: pl.BlockSpec(array.shape, lambda i: (0, 0))
    return pl.pallas_call(
        mlp_kernel,
        grid=(rows // ROWS_MLP,),
        in_specs=[some(D), some(D), some(D), whole(mod), whole(w_out), whole(w_exp), whole(w_con)],
        out_specs=[
            some(D), some(D), some(hidden), some(hidden), some(D), some(D),
            pl.BlockSpec((8, D), lambda i: (0, 0)),
        ],
        out_shape=[
            jax.ShapeDtypeStruct((rows, D), BF16),
            jax.ShapeDtypeStruct((rows, D), BF16),
            jax.ShapeDtypeStruct((rows, hidden), BF16),
            jax.ShapeDtypeStruct((rows, hidden), BF16),
            jax.ShapeDtypeStruct((rows, D), F32),
            jax.ShapeDtypeStruct((rows, D), BF16),
            jax.ShapeDtypeStruct((8, D), F32),
        ],
        compiler_params=params(48),
        cost_estimate=cost(rows * D * (8 * hidden + 4 * D), 22 * 2**20),
        name="mlp",
    )(attended, states, cot, mod, w_out, w_exp, w_con)


def first_kernel(dq_ref, dkv_ref, states_ref, d_mixed_ref, mod_ref, w_in_ref, grad_ref, sums_ref):
    scale_one = mod_ref[0:1, :]
    normed, inverse = normalize_parts(states_ref[...].astype(F32))
    d_first = dot(dq_ref[...], w_in_ref[:, :D], 1, 1) + dot(dkv_ref[...], w_in_ref[:, D:], 1, 1)

    @pl.when(pl.program_id(0) == 0)
    def _():
        sums_ref[...] = jnp.zeros_like(sums_ref)

    sums_ref[0:1, :] += jnp.sum(d_first * normed, axis=0, keepdims=True)
    sums_ref[1:2, :] += jnp.sum(d_first, axis=0, keepdims=True)
    grad_ref[...] = d_mixed_ref[...] + norm_back(normed, inverse, d_first * (1.0 + scale_one))


def first_call(dq, dkv, states, d_mixed, mod, w_in):
    rows = states.shape[0]
    some = lambda width: pl.BlockSpec((ROWS_MLP, width), lambda i: (i, 0))
    whole = lambda array: pl.BlockSpec(array.shape, lambda i: (0, 0))
    return pl.pallas_call(
        first_kernel,
        grid=(rows // ROWS_MLP,),
        in_specs=[some(D), some(2 * D), some(D), some(D), whole(mod), whole(w_in)],
        out_specs=[some(D), pl.BlockSpec((8, D), lambda i: (0, 0))],
        out_shape=[jax.ShapeDtypeStruct((rows, D), F32), jax.ShapeDtypeStruct((8, D), F32)],
        compiler_params=params(32),
        cost_estimate=cost(2 * rows * D * 3 * D, 10 * 2**20),
        name="input_gradient",
    )(dq, dkv, states, d_mixed, mod, w_in)


class Layout:
    def __init__(self):
        self.noise = lax.axis_size("noise")
        self.nodes = lax.axis_size("nodes")
        self.chips = self.nodes // 2

    def permute(self, value, move):
        pairs = []
        for n in range(self.noise):
            for z in range(self.chips):
                for c in range(2):
                    n2, z2, c2 = move(n, z % self.chips, c)
                    source = (n * self.chips + z) * 2 + c
                    target = (n2 * self.chips + z2 % self.chips) * 2 + c2
                    pairs.append((source, target))
        return lax.ppermute(value, AXES, pairs)

    def along(self, value, steps):
        count = self.nodes
        return lax.ppermute(value, "nodes", [(i, (i + steps) % count) for i in range(count)])

    def sum_nodes(self, value):
        value = value + self.permute(value, lambda n, z, c: (n, z, 1 - c))
        bit = 1
        while bit < self.chips:
            value = value + self.permute(value, lambda n, z, c: (n, z ^ bit, c))
            bit *= 2
        return value

    def gather_noise(self, value):
        n = lax.axis_index("noise")
        held = value[None]
        bit = 1
        while bit < self.noise:
            held = jnp.concatenate(
                [held, self.permute(held, lambda m, z, c: (m ^ bit, z, c))], axis=0
            )
            bit *= 2
        order = jnp.arange(self.noise) ^ n
        return held[order]

    def reduce_rows(self, grads):
        rows, cols = grads.shape
        own = rows // self.nodes
        part = cols // self.noise
        me = lax.axis_index("nodes")
        c = me % 2
        z = me // 2
        n = lax.axis_index("noise")
        blocks = grads.astype(BF16).reshape(self.chips, 2, own, cols)
        mine = lax.dynamic_index_in_dim(blocks, c, 1, keepdims=False)
        theirs = lax.dynamic_index_in_dim(blocks, 1 - c, 1, keepdims=False)
        got = self.permute(theirs, lambda n, z, c: (n, z, 1 - c))
        held = (mine.astype(F32) + got.astype(F32)).astype(BF16)
        held = held.reshape(self.chips, own, self.noise, part).transpose(2, 0, 1, 3)
        low, high = n % 2, n // 2
        slots = []
        for i in range(2):
            for j in range(2):
                at_zero = ((high ^ j) * 2) + (low ^ i)
                at_one = ((high ^ i) * 2) + (low ^ j)
                slots.append(held[jnp.where(c == 0, at_zero, at_one)])
        first_move = lambda n, z, c: (n ^ (1 if c == 0 else 2), z, c)
        second_move = lambda n, z, c: (n ^ (2 if c == 0 else 1), z, c)
        kept = jnp.stack(slots[:2]).astype(F32)
        kept = kept + self.permute(jnp.stack(slots[2:]), first_move).astype(F32)
        total = kept[0] + self.permute(kept[1].astype(BF16), second_move).astype(F32)
        total = jnp.roll(total, -z, axis=0)
        result = total[0]
        for s in range(1, self.chips):
            piece = total[s].astype(BF16)
            result = result + self.permute(piece, lambda n, z, c: (n, z + s, c)).astype(F32)
        result = result.astype(BF16)
        pair = jnp.stack([result, self.permute(result, second_move)])
        other = self.permute(pair, first_move)
        quarters = [pair[0], pair[1], other[0], other[1]]
        stacked = jnp.stack(quarters)
        order = []
        for q in range(4):
            x, y = q % 2, q // 2
            i = jnp.where(c == 0, x ^ low, y ^ high)
            j = jnp.where(c == 0, y ^ high, x ^ low)
            order.append(stacked[i * 2 + j])
        return jnp.concatenate(order, axis=-1).astype(F32)


def per_device(
    inputs, sigma, neighbours, cotangent,
    inward_weight, inward_first, inward_second,
    outward_weight, outward_first, outward_second,
    expand_weight, expand_first, expand_second,
    contract_weight, contract_first, contract_second,
    modulate_weight, modulate_first, modulate_second,
):
    net = Layout()
    states_low = inputs[0]
    cot = cotangent[0]
    rows = states_low.shape[0]
    device = lax.axis_index("nodes")
    own = modulate_weight.shape[0]

    w_in = lax.all_gather(inward_weight.astype(BF16), "nodes", axis=0, tiled=True)
    w_out = lax.all_gather(outward_weight.astype(BF16), "nodes", axis=0, tiled=True)
    w_exp = lax.all_gather(expand_weight.astype(BF16), "nodes", axis=0, tiled=True)
    w_con = lax.all_gather(contract_weight.astype(BF16), "nodes", axis=0, tiled=True)

    before = net.along(states_low[rows - RIM :], 1)
    after = net.along(states_low[:RIM], -1)

    cond_low = fourier(sigma).astype(BF16)
    cond_part = lax.dynamic_slice_in_dim(cond_low, device * own, own, 1)
    partial = jnp.dot(cond_part, modulate_weight.astype(BF16), preferred_element_type=F32)
    mod = net.sum_nodes(partial.reshape(4, D))

    total = rows * net.nodes
    place = (neighbours[0] - (device * rows - RIM)) % total
    place = place - (jnp.arange(rows, dtype=jnp.int32) // BLOCK * BLOCK)[:, None]
    bias = count_call(place)

    wide = jnp.concatenate([before, states_low, after], axis=0).astype(F32)
    normed, _ = normalize_parts(wide)
    first_in = (normed * (1.0 + mod[0:1]) + mod[1:2]).astype(BF16)
    queries = dot(first_in[RIM : RIM + rows], w_in[:, :D], 1, 0).astype(BF16)
    keyvals = dot(first_in, w_in[:, D:], 1, 0).astype(BF16)

    attended, probs = attend_call(queries, keyvals, bias)
    final, second_in, swished, d_up, d_mixed, d_attended, sums_two = mlp_call(
        attended, states_low, cot, mod, w_out, w_exp, w_con
    )
    grad_con = dot(swished, cot, 0, 0)
    grad_exp = dot(second_in, d_up, 0, 0)
    grad_out = dot(attended, d_mixed.astype(BF16), 0, 0)
    dq, dkv_wide = attend_back_call(queries, keyvals, probs, d_attended)
    grad_in = jnp.concatenate(
        [dot(first_in[RIM : RIM + rows], dq, 0, 0), dot(first_in, dkv_wide, 0, 0)], axis=1
    )
    from_next = net.along(dkv_wide[:RIM], -1)
    from_prev = net.along(dkv_wide[rows + RIM :], 1)
    dkv = dkv_wide[RIM : RIM + rows]
    dkv = jnp.concatenate(
        [dkv[:RIM] + from_prev, dkv[RIM : rows - RIM], dkv[rows - RIM :] + from_next], axis=0
    )
    input_grad, sums_one = first_call(dq, dkv, states_low, d_mixed, mod, w_in)

    d_mod = jnp.concatenate([sums_one[:2], sums_two[:2]], axis=0).reshape(1, 4 * D)
    d_mod = net.sum_nodes(d_mod)[0]
    everyone = net.gather_noise(jnp.concatenate([d_mod, cond_low[0].astype(F32)]))
    conds = lax.dynamic_slice_in_dim(everyone[:, 4 * D :], device * own, own, 1)
    grad_mod = lax.dot_general(
        conds, everyone[:, : 4 * D], (((0,), (0,)), ((), ())), precision=lax.Precision.HIGHEST
    )

    results = [final[None], input_grad[None]]
    for weight, first, second, grads in (
        (inward_weight, inward_first, inward_second, net.reduce_rows(grad_in)),
        (outward_weight, outward_first, outward_second, net.reduce_rows(grad_out)),
        (expand_weight, expand_first, expand_second, net.reduce_rows(grad_exp)),
        (contract_weight, contract_first, contract_second, net.reduce_rows(grad_con)),
        (modulate_weight, modulate_first, modulate_second, grad_mod),
    ):
        results.extend(adamw(weight, first, second, grads))
    return tuple(results)


def solution(mesh):
    grid = P("noise", "nodes", None)
    shard = P("nodes", None)
    return jax.shard_map(
        per_device,
        mesh=mesh,
        in_specs=(grid, P("noise"), grid, grid) + (shard,) * 15,
        out_specs=(grid, grid) + (shard,) * 15,
        check_vma=False,
    )
```

```python
import functools
import math

import jax
import jax.numpy as jnp
from jax import lax
from jax.experimental import pallas as pl
from jax.experimental.pallas import tpu as pltpu
from jax.sharding import PartitionSpec as P

D = 512
HEADS = 4
NEIGH = 16
RIM = 64
STEP = 10
HEAD_DIM = 128
BLOCK = 128
WINDOW = BLOCK + 2 * RIM
GROUP = 4
HALF = 512
CHUNK = 1024
LANES = 128
RIDER_ROWS = 8
NOISE, NODES = AXES = ("noise", "nodes")
BF16 = jnp.bfloat16
F32 = jnp.float32
NONE = -1e30
SMALL = 1.0 / math.sqrt(HEAD_DIM)

VMEM = pl.BlockSpec(memory_space=pltpu.VMEM)
HBM = pl.BlockSpec(memory_space=pltpu.HBM)


def dot(left, right, left_dim, right_dim):
    return lax.dot_general(
        left, right, (((left_dim,), (right_dim,)), ((), ())), preferred_element_type=F32
    )


def fourier(sigma):
    half = D // 2
    counter = jnp.arange(half).astype(F32)
    freqs = jnp.exp(counter * (math.log(64.0) / (half - 1)))
    phase = jnp.log(sigma)[:, None] * freqs[None, :]
    return jnp.concatenate([jnp.sin(phase), jnp.cos(phase)], axis=-1)


def normalize_parts(values):
    center = values - jnp.mean(values, axis=-1, keepdims=True)
    inverse = lax.rsqrt(jnp.mean(center * center, axis=-1, keepdims=True) + 1e-06)
    return (center * inverse, inverse)


def norm_back(normed, inverse, grads):
    average = jnp.mean(grads, axis=-1, keepdims=True)
    along = jnp.mean(grads * normed, axis=-1, keepdims=True)
    return inverse * (grads - average - normed * along)


def adamw(weight, first, second, grads):
    moment = 0.5 * first + 0.5 * grads
    square = 0.75 * second + 0.25 * grads * grads
    ratio = moment / (1.0 - 0.5**STEP) / (jnp.sqrt(square / (1.0 - 0.75**STEP)) + 1e-08)
    return (moment, square, weight - 0.02 * (ratio + 0.1 * weight))


def pinned(shape, dtype):
    return pltpu.VMEM(tuple(shape), dtype)


class Order:
    def __init__(self):
        self.tick = None
        self.tenths = 0

    def __call__(self, kernel, ins, outs, scratch=(), mib=8, free=(), loose=(), whole=()):
        before = [] if self.tick is None else [self.tick]

        def body(*refs):
            first = len(ins) + len(before)
            last = first + len(outs)
            kernel(*refs[: len(ins)], *refs[first:last], *refs[last + 1 :])
            refs[last][...] = jnp.zeros((8, LANES), F32)

        keep = lambda array: pltpu.with_memory_space_constraint(array, pltpu.VMEM)
        stay = lambda array: pltpu.with_memory_space_constraint(array, pltpu.HBM)
        arrays = [
            a if k in free else stay(a) if k in loose else keep(a) for k, a in enumerate(ins)
        ]
        specs = [HBM if k in loose else VMEM for k in range(len(ins))]
        named = kernel.func if isinstance(kernel, functools.partial) else kernel
        *results, self.tick = pl.pallas_call(
            body,
            in_specs=specs + [VMEM] * len(before),
            out_specs=[HBM if k in whole else VMEM for k in range(len(outs))] + [VMEM],
            out_shape=list(outs) + [pinned((8, LANES), F32)],
            scratch_shapes=list(scratch),
            compiler_params=pltpu.CompilerParams(vmem_limit_bytes=mib * 2**20),
            cost_estimate=pl.CostEstimate(
                flops=self.tenths * 10**8, bytes_accessed=1, transcendentals=0
            ),
            name=named.__name__,
        )(*arrays, *map(keep, before))
        return results


class Place:
    def __init__(self):
        self.device = lax.axis_index(NODES)
        self.n = lax.axis_index(NOISE)
        self.core = lax.rem(self.device, 2)
        self.chip = lax.div(self.device, 2)
        swapped = lax.rem(self.n, 2) * 2 + lax.div(self.n, 2)
        self.role = jnp.where(self.core == 0, self.n, swapped)
        self.other = jnp.where(self.core == 0, swapped, self.n)


def load_kernel(*refs):
    count, sems = len(refs) // 2, refs[-1]
    copies = [
        pltpu.make_async_copy(refs[k], refs[count + k], sems.at[k]) for k in range(count)
    ]
    for copy in copies:
        copy.start()
    for copy in copies:
        copy.wait()


def count_kernel(total, near_ref, bias_ref):
    rows = bias_ref.shape[0]
    base = Place().device * rows - RIM
    window = lax.broadcasted_iota(jnp.int32, (WINDOW, BLOCK), 0)
    for start in range(0, rows, BLOCK):
        place = near_ref[:, start : start + BLOCK] - (base + start)
        place = jnp.where(place < 0, place + total, place)
        place = jnp.where(place >= total, place - total, place)
        count = jnp.zeros((WINDOW, BLOCK), F32)
        for k in range(NEIGH):
            count = count + jnp.where(place[k : k + 1, :] == window, 1.0, 0.0)
        bias = jnp.where(count > 0.0, jnp.log(count), NONE)
        bias_ref[start : start + BLOCK, :] = bias.T


def pack_inward_kernel(inward_ref, halves_ref):
    wide = halves_ref.shape[2]
    for half in range(2):
        halves_ref[half] = inward_ref[:, half * wide : (half + 1) * wide].astype(BF16)


def pack_expand_kernel(expand_ref, outward_ref, halves_ref):
    wide = expand_ref.shape[1] // 2
    for half in range(2):
        left = expand_ref[:, half * wide : (half + 1) * wide].astype(BF16)
        right = outward_ref[:, half * D // 2 : (half + 1) * D // 2].astype(BF16)
        halves_ref[half, :, :wide] = left
        halves_ref[half, :, wide:] = right


def pack_contract_kernel(contract_ref, halves_ref):
    own = halves_ref.shape[1]
    for k in range(4):
        rows = contract_ref[k * own : (k + 1) * own, :].astype(BF16)
        halves_ref[k // 2, :, k % 2 * D : (k % 2 + 1) * D] = rows


def near_kernel(halves_ref, fetched_ref, got_ref, near_ref, every_ref):
    place = Place()
    mine = jnp.where(place.core == 0, lax.rem(place.n, 2), 1 - lax.div(place.n, 2))
    for half in range(2):
        near_ref[2 * mine + half] = fetched_ref[half]
        near_ref[2 * (1 - mine) + half] = got_ref[half]
        every_ref[4 + half] = halves_ref[half]
    for k in range(4):
        every_ref[k] = near_ref[k]


def take_kernel(value_ref, out_ref):
    out_ref[...] = value_ref[...]


def edges_kernel(states_ref, core_ref, chip_ref):
    core = Place().core
    rows = states_ref.shape[0]
    head, tail = states_ref[:RIM, :], states_ref[rows - RIM :, :]

    @pl.when(core == 0)
    def _():
        core_ref[...] = tail
        chip_ref[...] = head

    @pl.when(core == 1)
    def _():
        core_ref[...] = head
        chip_ref[...] = tail


def modulation_kernel(cond_ref, weight_ref, out_ref):
    own = weight_ref.shape[0]
    first = Place().device * own
    rows = lax.broadcasted_iota(jnp.int32, (D, own), 0)
    cols = lax.broadcasted_iota(jnp.int32, (D, own), 1)
    chosen = jnp.where(rows == cols + first, 1.0, 0.0).astype(BF16)
    mine = dot(cond_ref[...], chosen, 1, 0).astype(BF16)
    out_ref[...] = dot(mine, weight_ref[...].astype(BF16), 1, 0)


def sum_kernel(left_ref, right_ref, out_ref):
    out_ref[...] = left_ref[...] + right_ref[...]


def first_kernel(states_ref, core_ref, chip_ref, sum_ref, first_ref, mod_ref):
    core = Place().core
    mod_ref[...] = sum_ref[...]
    scale = 1.0 + mod_ref[0:1, :D]
    shift = mod_ref[0:1, D : 2 * D]
    rows = states_ref.shape[0]

    def put(at, values):
        normed, _ = normalize_parts(values.astype(F32))
        first_ref[at : at + values.shape[0], :] = (normed * scale + shift).astype(BF16)

    put(RIM, states_ref[...])

    @pl.when(core == 0)
    def _():
        put(0, chip_ref[...])
        put(RIM + rows, core_ref[...])

    @pl.when(core == 1)
    def _():
        put(0, core_ref[...])
        put(RIM + rows, chip_ref[...])


def heads(array_ref, start, rows, base):
    return [
        array_ref[start : start + rows, base + h * HEAD_DIM : base + (h + 1) * HEAD_DIM]
        for h in range(HEADS)
    ]


def joint_kernel(first_ref, bias_ref, *refs):
    parts = refs[:-5]
    q_ref, kv_ref, w_ref, out_ref, probs_ref = refs[-5:]
    rows = q_ref.shape[0]
    deep, width = parts[0].shape[1:]

    def put(ref, block, half):
        span = pl.ds(pl.multiple_of(block * deep, deep), deep)
        w_ref[span, half * width : (half + 1) * width] = ref[...]

    assemble(parts, put)
    q_ref[...] = dot(first_ref[RIM : RIM + rows, :], w_ref[:, :D], 1, 0).astype(BF16)
    kv_ref[...] = dot(first_ref[...], w_ref[:, D:], 1, 0).astype(BF16)
    for group in range(0, rows, GROUP * BLOCK):
        starts = range(group, min(group + GROUP * BLOCK, rows), BLOCK)
        jobs = [(s, h) for s in starts for h in range(HEADS)]
        queries = [x for s in starts for x in heads(q_ref, s, BLOCK, 0)]
        keys = [x for s in starts for x in heads(kv_ref, s, WINDOW, 0)]
        values = [x for s in starts for x in heads(kv_ref, s, WINDOW, D)]
        scores = [dot(q, k, 1, 1) for q, k in zip(queries, keys)]
        scores = [x * SMALL + bias_ref[s : s + BLOCK, :] for x, (s, _) in zip(scores, jobs)]
        tops = [jnp.max(x, axis=1, keepdims=True) for x in scores]
        expos = [jnp.exp(x - t) for x, t in zip(scores, tops)]
        sums = [jnp.sum(x, axis=1, keepdims=True) for x in expos]
        probs = [(x * (1.0 / t)).astype(BF16) for x, t in zip(expos, sums)]
        outs = [dot(p, v, 1, 0).astype(BF16) for p, v in zip(probs, values)]
        for p, o, (s, h) in zip(probs, outs, jobs):
            probs_ref[s : s + BLOCK, h * WINDOW : (h + 1) * WINDOW] = p
            out_ref[s : s + BLOCK, h * HEAD_DIM : (h + 1) * HEAD_DIM] = o


def attend_back_kernel(
    q_ref, kv_ref, probs_ref, grad_ref, dq_ref, dkv_ref, core_ref, chip_ref
):
    rows = q_ref.shape[0]
    carry = [jnp.zeros((BLOCK, HEAD_DIM), F32)] * (2 * HEADS)
    for group in range(0, rows, GROUP * BLOCK):
        starts = range(group, min(group + GROUP * BLOCK, rows), BLOCK)
        jobs = [(s, h) for s in starts for h in range(HEADS)]
        queries = [x for s in starts for x in heads(q_ref, s, BLOCK, 0)]
        grads = [x for s in starts for x in heads(grad_ref, s, BLOCK, 0)]
        keys = [x for s in starts for x in heads(kv_ref, s, WINDOW, 0)]
        values = [x for s in starts for x in heads(kv_ref, s, WINDOW, D)]
        probs = [probs_ref[s : s + BLOCK, h * WINDOW : (h + 1) * WINDOW] for s, h in jobs]
        d_probs = [dot(g, v, 1, 1) for g, v in zip(grads, values)]
        weighted = [p.astype(F32) * d for p, d in zip(probs, d_probs)]
        totals = [jnp.sum(w, axis=1, keepdims=True) for w in weighted]
        d_scores = [
            ((w - p.astype(F32) * t) * SMALL).astype(BF16)
            for w, p, t in zip(weighted, probs, totals)
        ]
        d_queries = [dot(d, k, 1, 0).astype(BF16) for d, k in zip(d_scores, keys)]
        d_keys = [dot(d, q, 0, 0) for d, q in zip(d_scores, queries)]
        d_values = [dot(p, g, 0, 0) for p, g in zip(probs, grads)]
        for x, (s, h) in zip(d_queries, jobs):
            dq_ref[s : s + BLOCK, h * HEAD_DIM : (h + 1) * HEAD_DIM] = x
        for column in range(2 * HEADS):
            parts = (d_keys if column < HEADS else d_values)[column % HEADS :: HEADS]
            cols = slice(column * HEAD_DIM, (column + 1) * HEAD_DIM)
            for s, part in zip(starts, parts):
                dkv_ref[s : s + BLOCK, cols] = (carry[column] + part[:BLOCK]).astype(BF16)
                carry[column] = part[BLOCK:]
    for column, part in enumerate(carry):
        cols = slice(column * HEAD_DIM, (column + 1) * HEAD_DIM)
        dkv_ref[rows : rows + BLOCK, cols] = part.astype(BF16)
    core = Place().core
    low, high = dkv_ref[:RIM, :], dkv_ref[rows + RIM :, :]

    @pl.when(core == 0)
    def _():
        core_ref[...] = high
        chip_ref[...] = low

    @pl.when(core == 1)
    def _():
        core_ref[...] = low
        chip_ref[...] = high


def assemble(parts, put):
    if len(parts) == 1:
        for half in range(2):
            put(parts[0].at[half], 0, half)
        return
    place = Place()
    for p in range(2):
        near, far = parts[2 * p : 2 * p + 2]
        owner = place.core if p == 0 else 1 - place.core

        def put_all(next_one, second, third):
            for half in range(2):
                for s, ref in enumerate((near.at[4 + half], next_one, second, third)):
                    part = ref if s == 0 else ref[0].at[ref[1] + half]
                    put(part, lax.rem(place.chip + s, 4) * 2 + owner, half)

        for core, bit in ((0, lax.div(place.n, 2)), (1, lax.rem(place.n, 2))):
            for turn in range(2):
                low, high = (near, far) if turn == 0 else (far, near)

                @pl.when(jnp.logical_and(owner == core, bit == turn))
                def _():
                    put_all((low, 2) if core == 0 else (high, 0), (low, 0), (high, 2))


def copy_rows(source, target, rows, sem):
    copy = pltpu.make_async_copy(source.at[rows], target.at[rows], sem)
    copy.start()
    return copy


def write_slots(targets, block_of):
    place = Place()
    owners = (place.core, 1 - place.core)
    for target, owner, role in zip(targets, owners, (place.role, place.other)):
        for slot in range(4):
            quarter = role ^ ((slot // 2) + 2 * (slot % 2))
            for s in range(target.shape[1]):
                target[slot, s] = block_of((place.chip ^ s) * 2 + owner, quarter).astype(BF16)


def mlp_forward_kernel(attended_ref, states_ref, cot_ref, mod_ref, *refs):
    parts = refs[:-9]
    (mixed_ref, second_ref, swished_ref, slope_ref, w_out_ref, w_exp_ref,
     keep_ref, send_ref, grad_ref) = refs[-9:]
    own = keep_ref.shape[2]
    hidden = w_exp_ref.shape[1]
    deep = parts[0].shape[1]

    def put(ref, block, half):
        rows = pl.ds(pl.multiple_of(block * deep, deep), deep)
        wide, thin = hidden // 2, D // 2
        w_exp_ref[rows, half * wide : (half + 1) * wide] = ref[:, :wide]
        w_out_ref[rows, half * thin : (half + 1) * thin] = ref[:, wide:]

    assemble(parts, put)
    scale = 1.0 + mod_ref[0:1, 2 * D : 3 * D]
    shift = mod_ref[0:1, 3 * D :]
    for start in range(0, states_ref.shape[0], HALF):
        rows = slice(start, start + HALF)
        mixed = states_ref[rows].astype(F32) + dot(attended_ref[rows], w_out_ref[...], 1, 0)
        mixed_ref[rows] = mixed
        normed, _ = normalize_parts(mixed)
        second_in = (normed * scale + shift).astype(BF16)
        second_ref[rows] = second_in
        for at in range(0, hidden, CHUNK):
            cols = slice(at, at + CHUNK)
            up = dot(second_in, w_exp_ref[:, cols], 1, 0)
            gate = 0.5 + 0.5 * jnp.tanh(0.5 * up)
            product = up * gate
            swished_ref[rows, cols] = product.astype(BF16)
            slope_ref[rows, cols] = (gate + product * (1.0 - gate)).astype(BF16)
    grad_ref[...] = dot(swished_ref[...], cot_ref[...], 0, 0)
    write_slots(
        (keep_ref, send_ref),
        lambda block, quarter: grad_ref[
            pl.ds(pl.multiple_of((block * 4 + quarter) * own, own), own), :
        ],
    )


def mlp_backward(rows, slope_ref, cot_ref, w_exp_ref, w_con_ref, d_up_ref, d_second_ref):
    hidden = w_exp_ref.shape[1]
    cot = cot_ref[rows]
    d_second = jnp.zeros(d_second_ref.shape, F32)
    for at in range(0, hidden, CHUNK):
        cols = slice(at, at + CHUNK)
        d_swished = dot(cot, w_con_ref[cols, :], 1, 1)
        d_up = (d_swished * slope_ref[rows, cols].astype(F32)).astype(BF16)
        d_up_ref[:, cols] = d_up
        d_second = d_second + dot(d_up, w_exp_ref[:, cols], 1, 1)
    d_second_ref[...] = d_second


def mlp_backward_low_kernel(slope_ref, cot_ref, w_exp_ref, *refs):
    parts = refs[:-3]
    d_up_ref, d_second_ref, w_con_ref = refs[-3:]
    deep = parts[0].shape[1]

    def put(ref, block, half):
        for k in range(2):
            start = pl.multiple_of((block * 4 + half * 2 + k) * deep, deep)
            w_con_ref[pl.ds(start, deep), :] = ref[:, k * D : (k + 1) * D]

    assemble(parts, put)
    rows = slice(0, d_up_ref.shape[0])
    mlp_backward(rows, slope_ref, cot_ref, w_exp_ref, w_con_ref, d_up_ref, d_second_ref)


def mlp_backward_high_kernel(slope_ref, cot_ref, w_exp_ref, w_con_ref, d_up_ref, d_second_ref):
    half = d_up_ref.shape[0]
    rows = slice(half, 2 * half)
    mlp_backward(rows, slope_ref, cot_ref, w_exp_ref, w_con_ref, d_up_ref, d_second_ref)


def final_kernel(mixed_ref, swished_ref, w_con_ref, final_ref, done_ref, sems):
    sends = []
    for start in range(0, mixed_ref.shape[0], HALF):
        rows = slice(start, start + HALF)
        final = mixed_ref[rows] + dot(swished_ref[rows], w_con_ref[...], 1, 0)
        done_ref[rows] = final.astype(BF16)
        sends.append(copy_rows(done_ref, final_ref, rows, sems.at[len(sends)]))
    for send in sends:
        send.wait()


def norm_backward_kernel(
    mixed_ref, low_ref, high_ref, cot_ref, mod_ref, w_out_ref,
    d_mixed_ref, d_low_ref, d_att_ref, sums_ref,
):
    scale = 1.0 + mod_ref[0:1, 2 * D : 3 * D]
    sums_ref[...] = jnp.zeros_like(sums_ref)
    half = low_ref.shape[0]
    for k, d_second_ref in enumerate((low_ref, high_ref)):
        rows = slice(k * half, (k + 1) * half)
        normed, inverse = normalize_parts(mixed_ref[rows])
        d_second = d_second_ref[...]
        sums_ref[0:1, :] += jnp.sum(d_second * normed, axis=0, keepdims=True)
        sums_ref[1:2, :] += jnp.sum(d_second, axis=0, keepdims=True)
        d_mixed = cot_ref[rows].astype(F32) + norm_back(normed, inverse, d_second * scale)
        d_mixed_ref[rows] = d_mixed
        d_low_ref[rows] = d_mixed.astype(BF16)
        d_att_ref[rows] = dot(d_mixed.astype(BF16), w_out_ref[...], 1, 1).astype(BF16)


def expand_grads_kernel(
    second_ref, low_ref, high_ref, attended_ref, d_low_ref, keep_ref, send_ref, exp_ref, out_ref
):
    own, unit = keep_ref.shape[2:]
    wide = unit - D // 4
    half = low_ref.shape[0]
    exp_ref[...] = dot(second_ref[:half, :], low_ref[...], 0, 0)
    exp_ref[...] += dot(second_ref[half:, :], high_ref[...], 0, 0)
    out_ref[...] = dot(attended_ref[...], d_low_ref[...], 0, 0)

    def block_of(block, quarter):
        rows = pl.ds(pl.multiple_of(block * own, own), own)
        first = exp_ref[rows, pl.ds(pl.multiple_of(quarter * wide, wide), wide)]
        second = out_ref[rows, pl.ds(pl.multiple_of(quarter * (D // 4), D // 4), D // 4)]
        return jnp.concatenate([first, second], axis=1)

    write_slots((keep_ref, send_ref), block_of)


def in_grads_kernel(first_ref, dq_ref, dkv_ref, keep_ref, send_ref, in_ref):
    own, unit = keep_ref.shape[2:]
    rows = dq_ref.shape[0]
    in_ref[:, :D] = dot(first_ref[RIM : RIM + rows, :], dq_ref[...], 0, 0)
    in_ref[:, D:] = dot(first_ref[...], dkv_ref[...], 0, 0)
    write_slots(
        (keep_ref, send_ref),
        lambda block, quarter: in_ref[
            pl.ds(pl.multiple_of(block * own, own), own),
            pl.ds(pl.multiple_of(quarter * unit, unit), unit),
        ],
    )


def rider_spots(copy, own):
    for group in range(5 * D // LANES):
        row = copy * RIDER_ROWS + group // 3
        at = (group % 3) * LANES
        yield group, row // own, row % own, slice(at, at + LANES)


def input_grad_kernel(
    copies, nodes, dq_ref, dkv_ref, core_ref, chip_ref, states_ref, d_mixed_ref, mod_ref, w_in_ref,
    sums_two_ref, cond_ref, grad_ref, rider_ref, wide_ref, row_ref, slab_ref, done_ref, out_sems,
):
    place = Place()
    rows = states_ref.shape[0]
    wide_ref[...] = dkv_ref[...]

    def join(at, ref):
        part = slice(at, at + RIM)
        wide_ref[part, :] = (wide_ref[part, :].astype(F32) + ref[...].astype(F32)).astype(BF16)

    @pl.when(place.core == 0)
    def _():
        join(RIM, chip_ref)
        join(rows, core_ref)

    @pl.when(place.core == 1)
    def _():
        join(RIM, core_ref)
        join(rows, chip_ref)

    scale = 1.0 + mod_ref[0:1, :D]
    d_scale = jnp.zeros((1, D), F32)
    d_shift = jnp.zeros((1, D), F32)
    sends = []
    for start in range(0, rows, HALF):
        part = slice(start, start + HALF)
        normed, inverse = normalize_parts(states_ref[part].astype(F32))
        d_first = dot(dq_ref[part], w_in_ref[:, :D], 1, 1) + dot(
            wide_ref[RIM + start : RIM + start + HALF, :], w_in_ref[:, D:], 1, 1
        )
        d_scale = d_scale + jnp.sum(d_first * normed, axis=0, keepdims=True)
        d_shift = d_shift + jnp.sum(d_first, axis=0, keepdims=True)
        done_ref[part] = d_mixed_ref[part] + norm_back(normed, inverse, d_first * scale)
        sends.append(copy_rows(done_ref, grad_ref, part, out_sems.at[len(sends)]))
    row_ref[0:1, :D] = d_scale
    row_ref[0:1, D : 2 * D] = d_shift
    row_ref[0:1, 2 * D : 3 * D] = sums_two_ref[0:1, :]
    row_ref[0:1, 3 * D : 4 * D] = sums_two_ref[1:2, :]
    row_ref[0:1, 4 * D :] = cond_ref[0:1, :].astype(F32) * (1.0 / nodes)
    slab_ref[...] = jnp.zeros_like(slab_ref)
    for copy in range(copies):
        mine = jnp.where(place.n == copy, 1.0, 0.0)
        for group, slab, row, cols in rider_spots(copy, slab_ref.shape[1]):
            values = row_ref[0:1, group * LANES : (group + 1) * LANES]
            slab_ref[slab, row : row + 1, cols] = values * mine
    rider_ref[...] = slab_ref[...].astype(BF16)
    for send in sends:
        send.wait()


def modulate_grads(copies, own, riders, row_ref, slab_ref):
    slab_ref[...] = riders
    row_ref[...] = jnp.zeros_like(row_ref)
    for copy in range(copies):
        for group, slab, row, cols in rider_spots(copy, slab_ref.shape[1]):
            row_ref[copy : copy + 1, group * LANES : (group + 1) * LANES] = slab_ref[
                slab, row : row + 1, cols
            ]
    everyone = row_ref[...].astype(BF16)
    chosen = lax.broadcasted_iota(jnp.int32, (D, own), 0) == (
        lax.broadcasted_iota(jnp.int32, (D, own), 1) + Place().device * own
    )
    conds = dot(everyone[:, 4 * D :], jnp.where(chosen, 1.0, 0.0).astype(BF16), 1, 0)
    return dot(conds.astype(BF16), everyone[:, : 4 * D], 0, 0)


def update_quarters(spots, pair_ref, got_ref, ins, outs, sems):
    role = Place().role
    sends = []
    for k, (cols, by_rows) in enumerate(spots):
        for slot in range(4):
            quarter = role ^ ((slot // 2) + 2 * (slot % 2))
            source = pair_ref if slot < 2 else got_ref
            grads = source[slot % 2, :, cols].astype(F32)
            size = grads.shape[0] if by_rows else grads.shape[1]
            span = pl.ds(pl.multiple_of(quarter * size, size), size)
            at = (span, slice(None)) if by_rows else (slice(None), span)
            values = adamw(*(ref[at] for ref in ins[3 * k : 3 * k + 3]), grads)
            for (scratch, _), value in zip(outs[3 * k : 3 * k + 3], values):
                scratch[at] = value
        for j in range(3 * k, 3 * k + 3):
            sends.append(pltpu.make_async_copy(*outs[j], sems.at[j]))
            sends[-1].start()
    return sends


class Net:
    def __init__(self):
        self.noise = lax.axis_size(NOISE)
        self.nodes = lax.axis_size(NODES)
        self.chips = self.nodes // 2
        self.quick = self.chips == 4

    def permute(self, value, move):
        pairs = []
        for n in range(self.noise):
            for z in range(self.chips):
                for c in range(2):
                    n2, z2, c2 = move(n, z, c)
                    source = (n * self.chips + z) * 2 + c
                    target = (n2 * self.chips + z2 % self.chips) * 2 + c2
                    pairs.append((source, target))
        return lax.ppermute(value, AXES, pairs)

    def role_of(self, n, c):
        return n if c == 0 else (n % 2) * 2 + n // 2

    def swap(self, value, bit):
        return self.permute(value, lambda n, z, c: (n ^ (bit if c == 0 else 3 - bit), z, c))

    def cores(self, value):
        return self.permute(value, lambda n, z, c: (n, z, 1 - c))

    def beside(self, value):
        return self.permute(value, lambda n, z, c: (n, z + 2 * c - 1, 1 - c))

    def across(self, value, step):
        return self.permute(value, lambda n, z, c: (n, z ^ step, c))

    def fetch(self, halves):
        back = (2, 3, 0, 1)
        return self.permute(halves, lambda n, z, c: (n, z + back[n ^ (2 * c)], c))


class Gathering:
    def __init__(self, net, order, kernel, arrays, half, stacked=False):
        self.net, self.order, self.kernel, self.arrays = net, order, kernel, arrays
        self.half, self.stacked = half, stacked

    def shape(self, count):
        return pinned((count, *self.half), BF16)

    def take(self, value):
        return self.order(take_kernel, [value], [pinned(value.shape, value.dtype)])[0]

    def pack(self):
        arrays, free = self.arrays()
        self.halves, = self.order(self.kernel, arrays, [self.shape(2)], free=free)
        if self.net.quick:
            self.got = self.net.fetch(self.halves)
            return
        every = lax.all_gather(self.halves, NODES, axis=1, tiled=True)
        if self.stacked:
            own = self.half[0]
            every = every.reshape(2, -1, own, 2, D).swapaxes(2, 3).swapaxes(0, 1)
            every = every.reshape(2, 2, -1, D).swapaxes(1, 2).reshape(2, -1, 2 * D)
        self.parts = [every]

    def swap(self):
        if not self.net.quick:
            return
        self.fetched = self.take(self.got)
        self.got = self.net.swap(self.fetched, 1)

    def near(self):
        if not self.net.quick:
            return
        near, every = self.order(
            near_kernel, [self.halves, self.fetched, self.got], [self.shape(4), self.shape(6)]
        )
        self.parts = [every, self.net.swap(near, 2), self.net.cores(every), None]

    def core(self):
        if not self.net.quick:
            return
        self.parts[2] = self.take(self.parts[2])

    def far(self):
        if not self.net.quick:
            return
        self.parts[1] = self.take(self.parts[1])
        self.parts[3] = self.net.cores(self.parts[1])


class Reduction:
    def __init__(self, net, order):
        self.net, self.order = net, order
        self.riders = 0

    def begin(self, keep, send):
        self.unit = keep.shape[2:]
        self.held, self.got = keep, self.net.cores(send)

    def shape(self, *lead):
        return pinned((*lead, *self.unit), BF16)

    def one(self):
        def sum_one(held_ref, got_ref, away_ref, out_ref):
            away_ref[...] = held_ref[2:] + got_ref[2:]
            out_ref[...] = held_ref[:2] + got_ref[:2]

        outs = [self.shape(2, self.net.chips)] * 2
        away, self.held = self.order(sum_one, [self.held, self.got], outs)
        self.got = self.net.swap(away, 1)

    def two(self):
        def sum_two(held_ref, got_ref, away_ref, out_ref):
            away_ref[...] = held_ref[1] + got_ref[1]
            out_ref[...] = held_ref[0] + got_ref[0]

        outs = [self.shape(self.net.chips)] * 2
        away, self.held = self.order(sum_two, [self.held, self.got], outs)
        self.got = self.net.swap(away, 2)

    def chip(self, step=1, rider=()):
        if rider:
            self.riders = rider[0].shape[0]
        count = self.net.chips // step
        riders = self.riders

        def sum_chips(held_ref, got_ref, *refs):
            away_ref, out_ref = refs[-2:]
            for k in range(count):
                target = away_ref if k % 2 else out_ref
                target[k // 2] = held_ref[k] + got_ref[k]
            for k in range(riders):
                if rider:
                    total = refs[0][k] + refs[1][k]
                else:
                    total = held_ref[count + k] + got_ref[count + k]
                away_ref[count // 2 + k] = total
                out_ref[count // 2 + k] = total

        outs = [self.shape(count // 2 + riders)] * 2
        away, self.held = self.order(sum_chips, [self.held, self.got, *rider], outs)
        self.got = self.net.across(away, step)

    def chips(self):
        step = 2
        while step < self.net.chips:
            self.chip(step)
            step *= 2

    def three(self):
        outs = [self.shape(1 + self.riders)]
        self.held, = self.order(sum_kernel, [self.held, self.got], outs)
        self.got = self.net.swap(self.held, 2)

    def four(self):
        riders = self.riders

        def join_quarters(held_ref, got_ref, out_ref):
            out_ref[0] = held_ref[0]
            out_ref[1] = got_ref[0]
            for k in range(riders):
                out_ref[2 + k] = held_ref[1 + k] + got_ref[1 + k]

        outs = [self.shape(2 + riders)]
        self.held, = self.order(join_quarters, [self.held, self.got], outs)
        self.got = self.net.swap(self.held, 1)

    def update(self, spots, arrays, more=(), more_grads=None):
        count = len(arrays) + len(more)
        outs = [jax.ShapeDtypeStruct(a.shape, F32) for a in (*arrays, *more)]

        def update_weights(pair_ref, got_ref, *refs):
            ins, targets, scratch = refs[:count], refs[count : 2 * count], refs[2 * count :]
            pairs = list(zip(scratch[:count], targets))
            sems = scratch[count]
            sends = update_quarters(spots, pair_ref, got_ref, ins, pairs, sems)
            if more:
                riders = pair_ref[2:].astype(F32) + got_ref[2:].astype(F32)
                grads = more_grads(riders, *scratch[count + 1 :])
                values = adamw(*(ref[...] for ref in ins[len(arrays) :]), grads)
                for j, value in enumerate(values, len(arrays)):
                    scratch[j][...] = value
                    sends.append(pltpu.make_async_copy(*pairs[j], sems.at[j]))
                    sends[-1].start()
            for send in sends:
                send.wait()

        scratch = [pltpu.VMEM(a.shape, F32) for a in (*arrays, *more)]
        scratch.append(pltpu.SemaphoreType.DMA((count,)))
        if more:
            scratch.extend([pltpu.VMEM((8, 5 * D), F32), pltpu.VMEM((self.riders, *self.unit), F32)])
        return self.order(
            update_weights, [self.held, self.got, *arrays, *more], outs, scratch,
            mib=16, free=range(2, 2 + count), whole=range(count),
        )


class Held:
    pass


def per_device(
    inputs, sigma, neighbours, cotangent,
    inward_weight, inward_first, inward_second,
    outward_weight, outward_first, outward_second,
    expand_weight, expand_first, expand_second,
    contract_weight, contract_first, contract_second,
    modulate_weight, modulate_first, modulate_second,
):
    net = Net()
    order = Order()
    h = Held()
    states = inputs[0]
    cot = cotangent[0]
    rows = states.shape[0]
    own, hidden = expand_weight.shape
    chips = net.chips
    low = lambda *shape: pinned(shape, BF16)
    full = lambda *shape: pinned(shape, F32)
    split = rows // 2
    slab = (own, 3 * D // 4)
    riders = -(-net.noise * RIDER_ROWS // own)
    cond = fourier(sigma).astype(BF16)

    w_in = Gathering(
        net, order, pack_inward_kernel, lambda: ([inward_weight], (0,)), (own, 3 * D // 2)
    )
    w_exp = Gathering(
        net, order, pack_expand_kernel, lambda: ([h.expand, h.outward], ()),
        (own, hidden // 2 + D // 2),
    )
    w_con = Gathering(
        net, order, pack_contract_kernel, lambda: ([h.contract], ()), (own, 2 * D), stacked=True
    )
    g_in, g_exp, g_con = (Reduction(net, order) for _ in range(3))

    def load():
        arrays = [
            expand_weight, outward_weight, contract_weight, modulate_weight, neighbours[0].T, states
        ]
        h.expand, h.outward, h.contract, h.modulate, h.neighbours, h.states = order(
            load_kernel, arrays, [pinned(a.shape, a.dtype) for a in arrays],
            [pltpu.SemaphoreType.DMA((len(arrays),))], loose=range(len(arrays)),
        )

    def mod():
        h.mod, = order(modulation_kernel, [cond, h.modulate], [full(1, 4 * D)], free=(0,))
        h.mod_got = net.cores(h.mod)

    def mod_sum():
        h.mod, = order(sum_kernel, [h.mod, h.mod_got], [full(1, 4 * D)])

    def mod_core():
        mod_sum()
        h.mod_got = net.across(h.mod, 1)

    def mod_near():
        step = 2
        while step < chips:
            mod_sum()
            h.mod_got = net.across(h.mod, step)
            step *= 2

    def counts():
        kernel = functools.partial(count_kernel, rows * net.nodes)
        h.bias, = order(kernel, [h.neighbours], [full(rows, WINDOW)])

    def edges():
        core, chip = order(edges_kernel, [h.states], [low(RIM, D), low(RIM, D)])
        h.edges = [net.cores(core), net.beside(chip)]

    def first():
        h.first, h.mod = order(
            first_kernel, [h.states, *h.edges, h.mod],
            [low(rows + 2 * RIM, D), full(1, 4 * D)],
        )

    def joint():
        h.q, h.kv, h.w_in, h.attended, h.probs = order(
            joint_kernel, [h.first, h.bias, *w_in.parts],
            [low(rows, D), low(rows + 2 * RIM, 2 * D), low(D, 3 * D),
             low(rows, D), low(rows, HEADS * WINDOW)],
            mib=14,
        )

    def mlp():
        slots = low(4, chips, own, D)
        h.mixed, h.second, h.swished, h.slope, h.w_out, h.w_exp, keep, send = order(
            mlp_forward_kernel, [h.attended, h.states, cot, h.mod, *w_exp.parts],
            [full(rows, D), low(rows, D), low(rows, hidden), low(rows, hidden),
             low(D, D), low(D, hidden), slots, slots],
            [pltpu.VMEM((hidden, D), F32)], mib=14, free=(2,),
        )
        g_con.begin(keep, send)

    def back_low():
        h.up_low, h.second_low, h.w_con = order(
            mlp_backward_low_kernel, [h.slope, cot, h.w_exp, *w_con.parts],
            [low(split, hidden), full(split, D), low(hidden, D)], mib=10, free=(1,),
        )

    def back_high():
        h.up_high, h.second_high = order(
            mlp_backward_high_kernel, [h.slope, cot, h.w_exp, h.w_con],
            [low(split, hidden), full(split, D)], mib=10, free=(1,),
        )

    def final():
        h.final, = order(
            final_kernel, [h.mixed, h.swished, h.w_con], [jax.ShapeDtypeStruct((rows, D), BF16)],
            [pltpu.VMEM((rows, D), BF16), pltpu.SemaphoreType.DMA((rows // HALF,))],
            mib=10, whole=(0,),
        )

    def norm():
        h.d_mixed, h.d_low, h.d_attended, h.sums_two = order(
            norm_backward_kernel,
            [h.mixed, h.second_low, h.second_high, cot, h.mod, h.w_out],
            [full(rows, D), low(rows, D), low(rows, D), full(8, D)], mib=8, free=(3,),
        )

    def exp_grad():
        slots = low(4, chips, own, hidden // 4 + D // 4)
        g_exp.begin(*order(
            expand_grads_kernel, [h.second, h.up_low, h.up_high, h.attended, h.d_low],
            [slots, slots], [pltpu.VMEM((D, hidden), F32), pltpu.VMEM((D, D), F32)], mib=12,
        ))

    def attn():
        h.dq, h.dkv, core, chip = order(
            attend_back_kernel, [h.q, h.kv, h.probs, h.d_attended],
            [low(rows, D), low(rows + 2 * RIM, 2 * D), low(RIM, 2 * D), low(RIM, 2 * D)],
            mib=12,
        )
        h.edges = [net.cores(core), net.beside(chip)]

    def edge_take():
        h.edges = [w_in.take(edge) for edge in h.edges]

    def in_grad():
        slots = low(4, chips, *slab)
        g_in.begin(*order(
            in_grads_kernel, [h.first, h.dq, h.dkv], [slots, slots],
            [pltpu.VMEM((D, 3 * D), F32)], mib=8,
        ))

    def input_step():
        kernel = functools.partial(input_grad_kernel, net.noise, net.nodes)
        h.input_grad, rider = order(
            kernel,
            [h.dq, h.dkv, *h.edges, states, h.d_mixed, h.mod, h.w_in, h.sums_two, cond],
            [jax.ShapeDtypeStruct((rows, D), F32), low(riders, *slab)],
            [pltpu.VMEM((rows + 2 * RIM, 2 * D), BF16), pltpu.VMEM((8, 5 * D), F32),
             pltpu.VMEM((riders, *slab), F32), pltpu.VMEM((rows, D), F32),
             pltpu.SemaphoreType.DMA((rows // HALF,))],
            mib=12, free=(4, 9), whole=(0,),
        )
        h.rider = (rider, net.cores(rider))

    def in_chip():
        g_in.chip(1, h.rider)

    def con_up():
        h.contract_new = g_con.update(
            [(slice(None), True)], [contract_weight, contract_first, contract_second]
        )

    def exp_up():
        h.expand_new = g_exp.update(
            [(slice(None, hidden // 4), False), (slice(hidden // 4, None), False)],
            [expand_weight, expand_first, expand_second,
             outward_weight, outward_first, outward_second],
        )

    def in_up():
        h.inward_new = g_in.update(
            [(slice(None), False)], [inward_weight, inward_first, inward_second],
            (modulate_weight, modulate_first, modulate_second),
            functools.partial(modulate_grads, net.noise, own),
        )

    plan = (
        (w_in.pack, 3), (load, 3), (w_exp.pack, 0), (mod, 20), (w_in.swap, 0), (mod_core, 100),
        (mod_near, 1), (counts, 30), (mod_sum, 0), (w_in.near, 0), (edges, 3), (w_in.core, 0),
        (w_con.pack, 0), (w_exp.swap, 10), (w_con.swap, 10), (w_in.far, 50), (w_exp.near, 100),
        (first, 0), (w_con.near, 400), (w_exp.core, 0), (joint, 0), (w_exp.far, 20),
        (w_con.core, 10), (mlp, 1), (w_con.far, 0), (back_low, 100), (g_con.one, 0),
        (back_high, 0), (norm, 100), (exp_grad, 1), (g_con.two, 0), (attn, 50), (in_grad, 50),
        (g_con.chip, 400), (g_exp.one, 0), (g_in.one, 0), (edge_take, 10), (input_step, 0),
        (g_exp.two, 400), (g_con.chips, 100), (g_in.two, 1), (final, 0), (g_con.three, 400),
        (in_chip, 1), (g_exp.chip, 1), (g_con.four, 3), (g_in.chips, 30), (g_exp.chips, 400),
        (g_in.three, 0), (g_exp.three, 100), (con_up, 200), (g_exp.four, 1), (g_in.four, 20),
        (in_up, 50), (exp_up, 3),
    )
    for step, tenths in plan:
        order.tenths = tenths
        step()

    return (
        h.final[None], h.input_grad[None], *h.inward_new[:3], *h.expand_new[3:],
        *h.expand_new[:3], *h.contract_new, *h.inward_new[3:],
    )


def solution(mesh):
    grid = P(NOISE, NODES, None)
    shard = P(NODES, None)
    return jax.shard_map(
        per_device,
        mesh=mesh,
        in_specs=(grid, P(NOISE), grid, grid) + (shard,) * 15,
        out_specs=(grid, grid) + (shard,) * 15,
        check_vma=False,
    )
```

```python
import functools
import math

import jax
import jax.numpy as jnp
from jax import lax
from jax.experimental import pallas as pl
from jax.experimental.pallas import tpu as pltpu
from jax.sharding import PartitionSpec as P

D = 512
HEADS = 4
NEIGH = 16
RIM = 64
STEP = 10
HEAD_DIM = 128
BLOCK = 128
WINDOW = BLOCK + 2 * RIM
GROUP = 4
HALF = 512
CHUNK = 1024
PIECE = 256
LANES = 128
RIDER_ROWS = 8
NOISE, NODES = AXES = ("noise", "nodes")
BF16 = jnp.bfloat16
F32 = jnp.float32
NONE = -1e30
SMALL = 1.0 / math.sqrt(HEAD_DIM)

VMEM = pl.BlockSpec(memory_space=pltpu.VMEM)
HBM = pl.BlockSpec(memory_space=pltpu.HBM)


def dot(left, right, left_dim, right_dim):
    return lax.dot_general(
        left, right, (((left_dim,), (right_dim,)), ((), ())), preferred_element_type=F32
    )


def fourier(sigma):
    half = D // 2
    counter = jnp.arange(half).astype(F32)
    freqs = jnp.exp(counter * (math.log(64.0) / (half - 1)))
    phase = jnp.log(sigma)[:, None] * freqs[None, :]
    return jnp.concatenate([jnp.sin(phase), jnp.cos(phase)], axis=-1)


def normalize_parts(values):
    center = values - jnp.mean(values, axis=-1, keepdims=True)
    inverse = lax.rsqrt(jnp.mean(center * center, axis=-1, keepdims=True) + 1e-06)
    return (center * inverse, inverse)


def norm_back(normed, inverse, grads):
    average = jnp.mean(grads, axis=-1, keepdims=True)
    along = jnp.mean(grads * normed, axis=-1, keepdims=True)
    return inverse * (grads - average - normed * along)


def adamw(weight, first, second, grads):
    moment = 0.5 * first + 0.5 * grads
    square = 0.75 * second + 0.25 * grads * grads
    level = square * (1.0 / (1.0 - 0.75**STEP))
    root = level * lax.rsqrt(level)
    ratio = moment * (1.0 / (1.0 - 0.5**STEP)) / (root + 1e-08)
    return (moment, square, weight - 0.02 * (ratio + 0.1 * weight))


def pinned(shape, dtype):
    return pltpu.VMEM(tuple(shape), dtype)


class Order:
    def __init__(self):
        self.tick = None
        self.tenths = 0

    def __call__(self, kernel, ins, outs, scratch=(), mib=8, free=(), loose=(), whole=()):
        before = [] if self.tick is None else [self.tick]

        def body(*refs):
            first = len(ins) + len(before)
            last = first + len(outs)
            kernel(*refs[: len(ins)], *refs[first:last], *refs[last + 1 :])
            refs[last][...] = jnp.zeros((8, LANES), F32)

        keep = lambda array: pltpu.with_memory_space_constraint(array, pltpu.VMEM)
        stay = lambda array: pltpu.with_memory_space_constraint(array, pltpu.HBM)
        arrays = [
            a if k in free else stay(a) if k in loose else keep(a) for k, a in enumerate(ins)
        ]
        specs = [HBM if k in loose else VMEM for k in range(len(ins))]
        named = kernel.func if isinstance(kernel, functools.partial) else kernel
        *results, self.tick = pl.pallas_call(
            body,
            in_specs=specs + [VMEM] * len(before),
            out_specs=[HBM if k in whole else VMEM for k in range(len(outs))] + [VMEM],
            out_shape=list(outs) + [pinned((8, LANES), F32)],
            scratch_shapes=list(scratch),
            compiler_params=pltpu.CompilerParams(vmem_limit_bytes=mib * 2**20),
            cost_estimate=pl.CostEstimate(
                flops=self.tenths * 10**8, bytes_accessed=1, transcendentals=0
            ),
            name=named.__name__,
        )(*arrays, *map(keep, before))
        return results


class Place:
    def __init__(self):
        self.device = lax.axis_index(NODES)
        self.n = lax.axis_index(NOISE)
        self.core = lax.rem(self.device, 2)
        self.chip = lax.div(self.device, 2)
        swapped = lax.rem(self.n, 2) * 2 + lax.div(self.n, 2)
        self.role = jnp.where(self.core == 0, self.n, swapped)
        self.other = jnp.where(self.core == 0, swapped, self.n)


def load_kernel(*refs):
    count, sems = len(refs) // 2, refs[-1]
    copies = [
        pltpu.make_async_copy(refs[k], refs[count + k], sems.at[k]) for k in range(count)
    ]
    for copy in copies:
        copy.start()
    for copy in copies:
        copy.wait()


def load_cot_kernel(*refs):
    load_kernel(*refs)


def count_kernel(total, near_ref, bias_ref):
    rows = bias_ref.shape[0]
    base = Place().device * rows - RIM
    shape = (WINDOW, BLOCK)
    window = lax.broadcasted_iota(jnp.int32, shape, 0).astype(jnp.int16)
    one, zero = jnp.ones(shape, BF16), jnp.zeros(shape, BF16)
    for start in range(0, rows, BLOCK):
        place = near_ref[:, start : start + BLOCK] - (base + start)
        place = jnp.where(place < 0, place + total, place)
        place = jnp.where(place >= total, place - total, place).astype(jnp.int16)
        count = zero
        for k in range(NEIGH):
            here = jnp.broadcast_to(place[k : k + 1, :], shape) == window
            count = count + jnp.where(here, one, zero)
        count = count.astype(F32)
        bias = jnp.where(count > 0.0, jnp.log(count), NONE)
        bias_ref[start : start + BLOCK, :] = bias.T


def pack_inward_kernel(inward_ref, halves_ref):
    wide = halves_ref.shape[2]
    for half in range(2):
        halves_ref[half] = inward_ref[:, half * wide : (half + 1) * wide].astype(BF16)


def pack_expand_kernel(expand_ref, outward_ref, halves_ref):
    wide = expand_ref.shape[1] // 2
    for half in range(2):
        left = expand_ref[:, half * wide : (half + 1) * wide].astype(BF16)
        right = outward_ref[:, half * D // 2 : (half + 1) * D // 2].astype(BF16)
        halves_ref[half, :, :wide] = left
        halves_ref[half, :, wide:] = right


def pack_contract_kernel(contract_ref, halves_ref):
    own = halves_ref.shape[1]
    for k in range(4):
        rows = contract_ref[k * own : (k + 1) * own, :].astype(BF16)
        halves_ref[k // 2, :, k % 2 * D : (k % 2 + 1) * D] = rows


def near_kernel(halves_ref, fetched_ref, got_ref, near_ref, every_ref):
    place = Place()
    mine = jnp.where(place.core == 0, lax.rem(place.n, 2), 1 - lax.div(place.n, 2))
    for half in range(2):
        near_ref[2 * mine + half] = fetched_ref[half]
        near_ref[2 * (1 - mine) + half] = got_ref[half]
        every_ref[4 + half] = halves_ref[half]
    for k in range(4):
        every_ref[k] = near_ref[k]


def take_kernel(value_ref, out_ref):
    out_ref[...] = value_ref[...]


def edges_kernel(states_ref, core_ref, chip_ref):
    core = Place().core
    rows = states_ref.shape[0]
    head, tail = states_ref[:RIM, :], states_ref[rows - RIM :, :]

    @pl.when(core == 0)
    def _():
        core_ref[...] = tail
        chip_ref[...] = head

    @pl.when(core == 1)
    def _():
        core_ref[...] = head
        chip_ref[...] = tail


def modulation_kernel(cond_ref, weight_ref, out_ref):
    own = weight_ref.shape[0]
    first = Place().device * own
    rows = lax.broadcasted_iota(jnp.int32, (D, own), 0)
    cols = lax.broadcasted_iota(jnp.int32, (D, own), 1)
    chosen = jnp.where(rows == cols + first, 1.0, 0.0).astype(BF16)
    mine = dot(cond_ref[...], chosen, 1, 0).astype(BF16)
    out_ref[...] = dot(mine, weight_ref[...].astype(BF16), 1, 0)


def sum_kernel(left_ref, right_ref, out_ref):
    out_ref[...] = left_ref[...] + right_ref[...]


def first_kernel(states_ref, core_ref, chip_ref, sum_ref, first_ref, mod_ref):
    core = Place().core
    mod_ref[...] = sum_ref[...]
    scale = 1.0 + mod_ref[0:1, :D]
    shift = mod_ref[0:1, D : 2 * D]
    rows = states_ref.shape[0]

    def put(at, values):
        normed, _ = normalize_parts(values.astype(F32))
        first_ref[at : at + values.shape[0], :] = (normed * scale + shift).astype(BF16)

    put(RIM, states_ref[...])

    @pl.when(core == 0)
    def _():
        put(0, chip_ref[...])
        put(RIM + rows, core_ref[...])

    @pl.when(core == 1)
    def _():
        put(0, core_ref[...])
        put(RIM + rows, chip_ref[...])


def heads(array_ref, start, rows, base):
    return [
        array_ref[start : start + rows, base + h * HEAD_DIM : base + (h + 1) * HEAD_DIM]
        for h in range(HEADS)
    ]


def joint_kernel(first_ref, bias_ref, *refs):
    parts = refs[:-5]
    q_ref, kv_ref, w_ref, out_ref, probs_ref = refs[-5:]
    rows = q_ref.shape[0]
    deep, width = parts[0].shape[1:]

    def put(ref, block, half):
        span = pl.ds(pl.multiple_of(block * deep, deep), deep)
        w_ref[span, half * width : (half + 1) * width] = ref[...]

    assemble(parts, put)
    q_ref[...] = dot(first_ref[RIM : RIM + rows, :], w_ref[:, :D], 1, 0).astype(BF16)
    kv_ref[...] = dot(first_ref[...], w_ref[:, D:], 1, 0).astype(BF16)
    for group in range(0, rows, GROUP * BLOCK):
        starts = range(group, min(group + GROUP * BLOCK, rows), BLOCK)
        jobs = [(s, h) for s in starts for h in range(HEADS)]
        queries = [x for s in starts for x in heads(q_ref, s, BLOCK, 0)]
        keys = [x for s in starts for x in heads(kv_ref, s, WINDOW, 0)]
        values = [x for s in starts for x in heads(kv_ref, s, WINDOW, D)]
        scores = [dot(q, k, 1, 1) for q, k in zip(queries, keys)]
        scores = [x * SMALL + bias_ref[s : s + BLOCK, :] for x, (s, _) in zip(scores, jobs)]
        tops = [jnp.max(x, axis=1, keepdims=True) for x in scores]
        expos = [jnp.exp(x - t) for x, t in zip(scores, tops)]
        sums = [jnp.sum(x, axis=1, keepdims=True) for x in expos]
        probs = [(x * (1.0 / t)).astype(BF16) for x, t in zip(expos, sums)]
        outs = [dot(p, v, 1, 0).astype(BF16) for p, v in zip(probs, values)]
        for p, o, (s, h) in zip(probs, outs, jobs):
            probs_ref[s : s + BLOCK, h * WINDOW : (h + 1) * WINDOW] = p
            out_ref[s : s + BLOCK, h * HEAD_DIM : (h + 1) * HEAD_DIM] = o


def attend_back_kernel(
    q_ref, kv_ref, probs_ref, grad_ref, dq_ref, dkv_ref, core_ref, chip_ref
):
    rows = q_ref.shape[0]
    carry = [jnp.zeros((BLOCK, HEAD_DIM), F32)] * (2 * HEADS)
    for group in range(0, rows, GROUP * BLOCK):
        starts = range(group, min(group + GROUP * BLOCK, rows), BLOCK)
        jobs = [(s, h) for s in starts for h in range(HEADS)]
        queries = [x for s in starts for x in heads(q_ref, s, BLOCK, 0)]
        grads = [x for s in starts for x in heads(grad_ref, s, BLOCK, 0)]
        keys = [x for s in starts for x in heads(kv_ref, s, WINDOW, 0)]
        values = [x for s in starts for x in heads(kv_ref, s, WINDOW, D)]
        probs = [probs_ref[s : s + BLOCK, h * WINDOW : (h + 1) * WINDOW] for s, h in jobs]
        d_probs = [dot(g, v, 1, 1) for g, v in zip(grads, values)]
        weighted = [p.astype(F32) * d for p, d in zip(probs, d_probs)]
        totals = [jnp.sum(w, axis=1, keepdims=True) for w in weighted]
        d_scores = [
            ((w - p.astype(F32) * t) * SMALL).astype(BF16)
            for w, p, t in zip(weighted, probs, totals)
        ]
        d_queries = [dot(d, k, 1, 0).astype(BF16) for d, k in zip(d_scores, keys)]
        d_keys = [dot(d, q, 0, 0) for d, q in zip(d_scores, queries)]
        d_values = [dot(p, g, 0, 0) for p, g in zip(probs, grads)]
        for x, (s, h) in zip(d_queries, jobs):
            dq_ref[s : s + BLOCK, h * HEAD_DIM : (h + 1) * HEAD_DIM] = x
        for column in range(2 * HEADS):
            parts = (d_keys if column < HEADS else d_values)[column % HEADS :: HEADS]
            cols = slice(column * HEAD_DIM, (column + 1) * HEAD_DIM)
            for s, part in zip(starts, parts):
                dkv_ref[s : s + BLOCK, cols] = (carry[column] + part[:BLOCK]).astype(BF16)
                carry[column] = part[BLOCK:]
    for column, part in enumerate(carry):
        cols = slice(column * HEAD_DIM, (column + 1) * HEAD_DIM)
        dkv_ref[rows : rows + BLOCK, cols] = part.astype(BF16)
    core = Place().core
    low, high = dkv_ref[:RIM, :], dkv_ref[rows + RIM :, :]

    @pl.when(core == 0)
    def _():
        core_ref[...] = high
        chip_ref[...] = low

    @pl.when(core == 1)
    def _():
        core_ref[...] = low
        chip_ref[...] = high


def assemble(parts, put):
    if len(parts) == 1:
        for half in range(2):
            put(parts[0].at[half], 0, half)
        return
    place = Place()
    for p in range(2):
        near, far = parts[2 * p : 2 * p + 2]
        owner = place.core if p == 0 else 1 - place.core

        def put_all(next_one, second, third):
            for half in range(2):
                for s, ref in enumerate((near.at[4 + half], next_one, second, third)):
                    part = ref if s == 0 else ref[0].at[ref[1] + half]
                    put(part, lax.rem(place.chip + s, 4) * 2 + owner, half)

        for core, bit in ((0, lax.div(place.n, 2)), (1, lax.rem(place.n, 2))):
            for turn in range(2):
                low, high = (near, far) if turn == 0 else (far, near)

                @pl.when(jnp.logical_and(owner == core, bit == turn))
                def _():
                    put_all((low, 2) if core == 0 else (high, 0), (low, 0), (high, 2))


def copy_rows(source, target, rows, sem):
    copy = pltpu.make_async_copy(source.at[rows], target.at[rows], sem)
    copy.start()
    return copy


def write_slots(targets, block_of):
    place = Place()
    owners = (place.core, 1 - place.core)
    for target, owner, role in zip(targets, owners, (place.role, place.other)):
        for slot in range(4):
            quarter = role ^ ((slot // 2) + 2 * (slot % 2))
            for s in range(target.shape[1]):
                target[slot, s] = block_of((place.chip ^ s) * 2 + owner, quarter).astype(BF16)


def mlp_forward_kernel(attended_ref, states_ref, mod_ref, *refs):
    parts = refs[:-6]
    mixed_ref, second_ref, swished_ref, slope_ref, w_out_ref, w_exp_ref = refs[-6:]
    hidden = w_exp_ref.shape[1]
    deep = parts[0].shape[1]

    def put(ref, block, half):
        rows = pl.ds(pl.multiple_of(block * deep, deep), deep)
        wide, thin = hidden // 2, D // 2
        w_exp_ref[rows, half * wide : (half + 1) * wide] = ref[:, :wide]
        w_out_ref[rows, half * thin : (half + 1) * thin] = ref[:, wide:]

    assemble(parts, put)
    scale = 1.0 + mod_ref[0:1, 2 * D : 3 * D]
    shift = mod_ref[0:1, 3 * D :]
    for start in range(0, states_ref.shape[0], HALF):
        rows = slice(start, start + HALF)
        mixed = states_ref[rows].astype(F32) + dot(attended_ref[rows], w_out_ref[...], 1, 0)
        mixed_ref[rows] = mixed
        normed, _ = normalize_parts(mixed)
        second_in = (normed * scale + shift).astype(BF16)
        second_ref[rows] = second_in
        for at in range(0, hidden, CHUNK):
            cols = slice(at, at + CHUNK)
            up = dot(second_in, w_exp_ref[:, cols], 1, 0)
            gate = 0.5 + 0.5 * jnp.tanh(0.5 * up)
            product = up * gate
            swished_ref[rows, cols] = product.astype(BF16)
            slope_ref[rows, cols] = (gate + product * (1.0 - gate)).astype(BF16)

def contract_grads_kernel(swished_ref, cot_ref, keep_ref, send_ref, grad_ref):
    own = keep_ref.shape[2]
    grad_ref[...] = dot(swished_ref[...], cot_ref[...], 0, 0)
    write_slots(
        (keep_ref, send_ref),
        lambda block, quarter: grad_ref[
            pl.ds(pl.multiple_of((block * 4 + quarter) * own, own), own), :
        ],
    )


def mlp_backward(rows, slope_ref, cot_ref, w_exp_ref, w_con_ref, d_up_ref, d_second_ref):
    hidden = w_exp_ref.shape[1]
    cot = cot_ref[rows]
    d_second = jnp.zeros(d_second_ref.shape, F32)
    for at in range(0, hidden, CHUNK):
        cols = slice(at, at + CHUNK)
        d_swished = dot(cot, w_con_ref[cols, :], 1, 1)
        d_up = (d_swished * slope_ref[rows, cols].astype(F32)).astype(BF16)
        d_up_ref[:, cols] = d_up
        d_second = d_second + dot(d_up, w_exp_ref[:, cols], 1, 1)
    d_second_ref[...] = d_second


def mlp_backward_low_kernel(slope_ref, cot_ref, w_exp_ref, *refs):
    parts = refs[:-3]
    d_up_ref, d_second_ref, w_con_ref = refs[-3:]
    deep = parts[0].shape[1]

    def put(ref, block, half):
        for k in range(2):
            start = pl.multiple_of((block * 4 + half * 2 + k) * deep, deep)
            w_con_ref[pl.ds(start, deep), :] = ref[:, k * D : (k + 1) * D]

    assemble(parts, put)
    rows = slice(0, d_up_ref.shape[0])
    mlp_backward(rows, slope_ref, cot_ref, w_exp_ref, w_con_ref, d_up_ref, d_second_ref)


def mlp_backward_high_kernel(slope_ref, cot_ref, w_exp_ref, w_con_ref, d_up_ref, d_second_ref):
    half = d_up_ref.shape[0]
    rows = slice(half, 2 * half)
    mlp_backward(rows, slope_ref, cot_ref, w_exp_ref, w_con_ref, d_up_ref, d_second_ref)


def final_kernel(
    mixed_ref, swished_ref, w_con_ref, grad_ref, final_ref, grad_out_ref, done_ref, sems
):
    sends = [pltpu.make_async_copy(grad_ref, grad_out_ref, sems.at[0])]
    sends[0].start()
    for start in range(0, mixed_ref.shape[0], PIECE):
        rows = slice(start, start + PIECE)
        final = mixed_ref[rows] + dot(swished_ref[rows], w_con_ref[...], 1, 0)
        done_ref[rows] = final.astype(BF16)
        sends.append(copy_rows(done_ref, final_ref, rows, sems.at[len(sends)]))
    for send in sends:
        send.wait()


def norm_backward_kernel(
    mixed_ref, low_ref, high_ref, cot_ref, mod_ref, w_out_ref,
    d_mixed_ref, d_low_ref, d_att_ref, sums_ref,
):
    scale = 1.0 + mod_ref[0:1, 2 * D : 3 * D]
    sums_ref[...] = jnp.zeros_like(sums_ref)
    half = low_ref.shape[0]
    for k, d_second_ref in enumerate((low_ref, high_ref)):
        rows = slice(k * half, (k + 1) * half)
        normed, inverse = normalize_parts(mixed_ref[rows])
        d_second = d_second_ref[...]
        sums_ref[0:1, :] += jnp.sum(d_second * normed, axis=0, keepdims=True)
        sums_ref[1:2, :] += jnp.sum(d_second, axis=0, keepdims=True)
        d_mixed = cot_ref[rows].astype(F32) + norm_back(normed, inverse, d_second * scale)
        d_mixed_ref[rows] = d_mixed
        d_low_ref[rows] = d_mixed.astype(BF16)
        d_att_ref[rows] = dot(d_mixed.astype(BF16), w_out_ref[...], 1, 1).astype(BF16)


def expand_grads_kernel(
    second_ref, low_ref, high_ref, attended_ref, d_low_ref, keep_ref, send_ref, exp_ref, out_ref
):
    own, unit = keep_ref.shape[2:]
    wide = unit - D // 4
    half = low_ref.shape[0]
    exp_ref[...] = dot(second_ref[:half, :], low_ref[...], 0, 0)
    exp_ref[...] += dot(second_ref[half:, :], high_ref[...], 0, 0)
    out_ref[...] = dot(attended_ref[...], d_low_ref[...], 0, 0)

    def block_of(block, quarter):
        rows = pl.ds(pl.multiple_of(block * own, own), own)
        first = exp_ref[rows, pl.ds(pl.multiple_of(quarter * wide, wide), wide)]
        second = out_ref[rows, pl.ds(pl.multiple_of(quarter * (D // 4), D // 4), D // 4)]
        return jnp.concatenate([first, second], axis=1)

    write_slots((keep_ref, send_ref), block_of)


def in_grads_kernel(first_ref, dq_ref, dkv_ref, keep_ref, send_ref, in_ref):
    own, unit = keep_ref.shape[2:]
    rows = dq_ref.shape[0]
    in_ref[:, :D] = dot(first_ref[RIM : RIM + rows, :], dq_ref[...], 0, 0)
    in_ref[:, D:] = dot(first_ref[...], dkv_ref[...], 0, 0)
    write_slots(
        (keep_ref, send_ref),
        lambda block, quarter: in_ref[
            pl.ds(pl.multiple_of(block * own, own), own),
            pl.ds(pl.multiple_of(quarter * unit, unit), unit),
        ],
    )


def rider_spots(copy, own):
    for group in range(5 * D // LANES):
        row = copy * RIDER_ROWS + group // 3
        at = (group % 3) * LANES
        yield group, row // own, row % own, slice(at, at + LANES)


def input_grad_kernel(
    copies, nodes, dq_ref, dkv_ref, core_ref, chip_ref, states_ref, d_mixed_ref, mod_ref, w_in_ref,
    sums_two_ref, cond_ref, grad_ref, rider_ref, wide_ref, row_ref, slab_ref,
):
    place = Place()
    rows = states_ref.shape[0]
    wide_ref[...] = dkv_ref[...]

    def join(at, ref):
        part = slice(at, at + RIM)
        wide_ref[part, :] = (wide_ref[part, :].astype(F32) + ref[...].astype(F32)).astype(BF16)

    @pl.when(place.core == 0)
    def _():
        join(RIM, chip_ref)
        join(rows, core_ref)

    @pl.when(place.core == 1)
    def _():
        join(RIM, core_ref)
        join(rows, chip_ref)

    scale = 1.0 + mod_ref[0:1, :D]
    d_scale = jnp.zeros((1, D), F32)
    d_shift = jnp.zeros((1, D), F32)
    for start in range(0, rows, HALF):
        part = slice(start, start + HALF)
        normed, inverse = normalize_parts(states_ref[part].astype(F32))
        d_first = dot(dq_ref[part], w_in_ref[:, :D], 1, 1) + dot(
            wide_ref[RIM + start : RIM + start + HALF, :], w_in_ref[:, D:], 1, 1
        )
        d_scale = d_scale + jnp.sum(d_first * normed, axis=0, keepdims=True)
        d_shift = d_shift + jnp.sum(d_first, axis=0, keepdims=True)
        grad_ref[part] = d_mixed_ref[part] + norm_back(normed, inverse, d_first * scale)
    row_ref[0:1, :D] = d_scale
    row_ref[0:1, D : 2 * D] = d_shift
    row_ref[0:1, 2 * D : 3 * D] = sums_two_ref[0:1, :]
    row_ref[0:1, 3 * D : 4 * D] = sums_two_ref[1:2, :]
    row_ref[0:1, 4 * D :] = cond_ref[0:1, :].astype(F32) * (1.0 / nodes)
    slab_ref[...] = jnp.zeros_like(slab_ref)
    for copy in range(copies):
        mine = jnp.where(place.n == copy, 1.0, 0.0)
        for group, slab, row, cols in rider_spots(copy, slab_ref.shape[1]):
            values = row_ref[0:1, group * LANES : (group + 1) * LANES]
            slab_ref[slab, row : row + 1, cols] = values * mine
    rider_ref[...] = slab_ref[...].astype(BF16)


def modulate_grads(copies, own, riders, row_ref, slab_ref):
    slab_ref[...] = riders
    row_ref[...] = jnp.zeros_like(row_ref)
    for copy in range(copies):
        for group, slab, row, cols in rider_spots(copy, slab_ref.shape[1]):
            row_ref[copy : copy + 1, group * LANES : (group + 1) * LANES] = slab_ref[
                slab, row : row + 1, cols
            ]
    everyone = row_ref[...].astype(BF16)
    chosen = lax.broadcasted_iota(jnp.int32, (D, own), 0) == (
        lax.broadcasted_iota(jnp.int32, (D, own), 1) + Place().device * own
    )
    conds = dot(everyone[:, 4 * D :], jnp.where(chosen, 1.0, 0.0).astype(BF16), 1, 0)
    return dot(conds.astype(BF16), everyone[:, : 4 * D], 0, 0)


def update_quarters(spots, pair_ref, got_ref, ins, outs, sems, first):
    role = Place().role
    sends = []
    for k, (cols, by_rows) in enumerate(spots):
        for slot in range(4):
            quarter = role ^ ((slot // 2) + 2 * (slot % 2))
            source = pair_ref if slot < 2 else got_ref
            grads = source[slot % 2, :, cols].astype(F32)
            size = grads.shape[0] if by_rows else grads.shape[1]
            span = pl.ds(pl.multiple_of(quarter * size, size), size)
            at = (span, slice(None)) if by_rows else (slice(None), span)
            values = adamw(*(ref[at] for ref in ins[3 * k : 3 * k + 3]), grads)
            for j, value in enumerate(values, 3 * k):
                scratch, target = outs[j]
                scratch[at] = value
                copy = pltpu.make_async_copy(
                    scratch.at[at], target.at[at], sems.at[first + j, slot]
                )
                copy.start()
                sends.append(copy)
    return sends


class Net:
    def __init__(self):
        self.noise = lax.axis_size(NOISE)
        self.nodes = lax.axis_size(NODES)
        self.chips = self.nodes // 2
        self.quick = self.chips == 4

    def permute(self, value, move):
        pairs = []
        for n in range(self.noise):
            for z in range(self.chips):
                for c in range(2):
                    n2, z2, c2 = move(n, z, c)
                    source = (n * self.chips + z) * 2 + c
                    target = (n2 * self.chips + z2 % self.chips) * 2 + c2
                    pairs.append((source, target))
        return lax.ppermute(value, AXES, pairs)

    def role_of(self, n, c):
        return n if c == 0 else (n % 2) * 2 + n // 2

    def swap(self, value, bit):
        return self.permute(value, lambda n, z, c: (n ^ (bit if c == 0 else 3 - bit), z, c))

    def cores(self, value):
        return self.permute(value, lambda n, z, c: (n, z, 1 - c))

    def beside(self, value):
        return self.permute(value, lambda n, z, c: (n, z + 2 * c - 1, 1 - c))

    def across(self, value, step):
        return self.permute(value, lambda n, z, c: (n, z ^ step, c))

    def fetch(self, halves):
        back = (2, 3, 0, 1)
        return self.permute(halves, lambda n, z, c: (n, z + back[n ^ (2 * c)], c))


class Gathering:
    def __init__(self, net, order, kernel, arrays, half, stacked=False):
        self.net, self.order, self.kernel, self.arrays = net, order, kernel, arrays
        self.half, self.stacked = half, stacked

    def shape(self, count):
        return pinned((count, *self.half), BF16)

    def take(self, value):
        return self.order(take_kernel, [value], [pinned(value.shape, value.dtype)])[0]

    def pack(self):
        arrays, free = self.arrays()
        self.halves, = self.order(self.kernel, arrays, [self.shape(2)], free=free)
        if self.net.quick:
            self.got = self.net.fetch(self.halves)
            return
        every = lax.all_gather(self.halves, NODES, axis=1, tiled=True)
        if self.stacked:
            own = self.half[0]
            every = every.reshape(2, -1, own, 2, D).swapaxes(2, 3).swapaxes(0, 1)
            every = every.reshape(2, 2, -1, D).swapaxes(1, 2).reshape(2, -1, 2 * D)
        self.parts = [every]

    def swap(self):
        if not self.net.quick:
            return
        self.fetched = self.take(self.got)
        self.got = self.net.swap(self.fetched, 1)

    def near(self):
        if not self.net.quick:
            return
        near, every = self.order(
            near_kernel, [self.halves, self.fetched, self.got], [self.shape(4), self.shape(6)]
        )
        self.parts = [every, self.net.swap(near, 2), self.net.cores(every), None]

    def core(self):
        if not self.net.quick:
            return
        self.parts[2] = self.take(self.parts[2])

    def far(self):
        if not self.net.quick:
            return
        self.parts[1] = self.take(self.parts[1])
        self.parts[3] = self.net.cores(self.parts[1])


class Reduction:
    def __init__(self, net, order):
        self.net, self.order = net, order
        self.riders = 0

    def begin(self, keep, send):
        self.unit = keep.shape[2:]
        self.held, self.got = keep, self.net.cores(send)

    def shape(self, *lead):
        return pinned((*lead, *self.unit), BF16)

    def one(self):
        def sum_one(held_ref, got_ref, away_ref, out_ref):
            away_ref[...] = held_ref[2:] + got_ref[2:]
            out_ref[...] = held_ref[:2] + got_ref[:2]

        outs = [self.shape(2, self.net.chips)] * 2
        away, self.held = self.order(sum_one, [self.held, self.got], outs)
        self.got = self.net.swap(away, 1)

    def two(self):
        def sum_two(held_ref, got_ref, away_ref, out_ref):
            away_ref[...] = held_ref[1] + got_ref[1]
            out_ref[...] = held_ref[0] + got_ref[0]

        outs = [self.shape(self.net.chips)] * 2
        away, self.held = self.order(sum_two, [self.held, self.got], outs)
        self.got = self.net.swap(away, 2)

    def chip(self, step=1, rider=()):
        if rider:
            self.riders = rider[0].shape[0]
        count = self.net.chips // step
        riders = self.riders

        def sum_chips(held_ref, got_ref, *refs):
            away_ref, out_ref = refs[-2:]
            for k in range(count):
                target = away_ref if k % 2 else out_ref
                target[k // 2] = held_ref[k] + got_ref[k]
            for k in range(riders):
                if rider:
                    total = refs[0][k] + refs[1][k]
                else:
                    total = held_ref[count + k] + got_ref[count + k]
                away_ref[count // 2 + k] = total
                out_ref[count // 2 + k] = total

        outs = [self.shape(count // 2 + riders)] * 2
        away, self.held = self.order(sum_chips, [self.held, self.got, *rider], outs)
        self.got = self.net.across(away, step)

    def chips(self):
        step = 2
        while step < self.net.chips:
            self.chip(step)
            step *= 2

    def three(self):
        outs = [self.shape(1 + self.riders)]
        self.held, = self.order(sum_kernel, [self.held, self.got], outs)
        self.got = self.net.swap(self.held, 2)

    def four(self):
        riders = self.riders

        def join_quarters(held_ref, got_ref, out_ref):
            out_ref[0] = held_ref[0]
            out_ref[1] = got_ref[0]
            for k in range(riders):
                out_ref[2 + k] = held_ref[1 + k] + got_ref[1 + k]

        outs = [self.shape(2 + riders)]
        self.held, = self.order(join_quarters, [self.held, self.got], outs)
        self.got = self.net.swap(self.held, 1)


def update_call(order, jobs, more=(), more_grads=None):
    arrays = [a for _, _, some in jobs for a in some] + list(more)
    count = len(arrays)
    sums = [part for reduction, _, _ in jobs for part in (reduction.held, reduction.got)]

    def update_weights(*refs):
        start = len(sums)
        ins, targets = refs[start : start + count], refs[start + count : start + 2 * count]
        scratch = refs[start + 2 * count :]
        pairs = list(zip(scratch[:count], targets))
        sems = scratch[count]
        sends = []
        at = 0
        for k, (_, spots, some) in enumerate(jobs):
            span = slice(at, at + len(some))
            sends += update_quarters(
                spots, refs[2 * k], refs[2 * k + 1], ins[span], pairs[span], sems, at
            )
            at += len(some)
        if more:
            riders = refs[0][2:].astype(F32) + refs[1][2:].astype(F32)
            grads = more_grads(riders, *scratch[count + 1 :])
            values = adamw(*(ref[...] for ref in ins[at:]), grads)
            for j, value in enumerate(values, at):
                scratch[j][...] = value
                sends.append(pltpu.make_async_copy(*pairs[j], sems.at[j, 0]))
                sends[-1].start()
        for send in sends:
            send.wait()

    scratch = [pltpu.VMEM(a.shape, F32) for a in arrays] + [pltpu.SemaphoreType.DMA((count, 4))]
    if more:
        reduction = jobs[0][0]
        scratch.append(pltpu.VMEM((8, 5 * D), F32))
        scratch.append(pltpu.VMEM((reduction.riders, *reduction.unit), F32))
    return order(
        update_weights, [*sums, *arrays], [jax.ShapeDtypeStruct(a.shape, F32) for a in arrays],
        scratch, mib=16, free=range(len(sums), len(sums) + count), whole=range(count),
    )


class Held:
    pass


def per_device(
    inputs, sigma, neighbours, cotangent,
    inward_weight, inward_first, inward_second,
    outward_weight, outward_first, outward_second,
    expand_weight, expand_first, expand_second,
    contract_weight, contract_first, contract_second,
    modulate_weight, modulate_first, modulate_second,
):
    net = Net()
    order = Order()
    h = Held()
    states = inputs[0]
    cot = cotangent[0]
    rows = states.shape[0]
    own, hidden = expand_weight.shape
    chips = net.chips
    low = lambda *shape: pinned(shape, BF16)
    full = lambda *shape: pinned(shape, F32)
    split = rows // 2
    slab = (own, 3 * D // 4)
    riders = -(-net.noise * RIDER_ROWS // own)
    cond = fourier(sigma).astype(BF16)

    w_in = Gathering(
        net, order, pack_inward_kernel, lambda: ([inward_weight], (0,)), (own, 3 * D // 2)
    )
    w_exp = Gathering(
        net, order, pack_expand_kernel, lambda: ([h.expand, h.outward], ()),
        (own, hidden // 2 + D // 2),
    )
    w_con = Gathering(
        net, order, pack_contract_kernel, lambda: ([h.contract], ()), (own, 2 * D), stacked=True
    )
    g_in, g_exp, g_con = (Reduction(net, order) for _ in range(3))

    def load():
        arrays = [
            expand_weight, outward_weight, contract_weight, modulate_weight, neighbours[0].T, states
        ]
        h.expand, h.outward, h.contract, h.modulate, h.neighbours, h.states = order(
            load_kernel, arrays, [pinned(a.shape, a.dtype) for a in arrays],
            [pltpu.SemaphoreType.DMA((len(arrays),))], loose=range(len(arrays)),
        )

    def load_cot():
        h.cot, = order(
            load_cot_kernel, [cot], [pinned(cot.shape, cot.dtype)], [pltpu.SemaphoreType.DMA((1,))],
            loose=(0,),
        )

    def mod():
        h.mod, = order(modulation_kernel, [cond, h.modulate], [full(1, 4 * D)], free=(0,))
        h.mod_got = net.cores(h.mod)

    def mod_sum():
        h.mod, = order(sum_kernel, [h.mod, h.mod_got], [full(1, 4 * D)])

    def mod_core():
        mod_sum()
        h.mod_got = net.across(h.mod, 1)

    def mod_near():
        step = 2
        while step < chips:
            mod_sum()
            h.mod_got = net.across(h.mod, step)
            step *= 2

    def counts():
        kernel = functools.partial(count_kernel, rows * net.nodes)
        h.bias, = order(kernel, [h.neighbours], [full(rows, WINDOW)])

    def edges():
        core, chip = order(edges_kernel, [h.states], [low(RIM, D), low(RIM, D)])
        h.edges = [net.cores(core), net.beside(chip)]

    def first():
        h.first, h.mod = order(
            first_kernel, [h.states, *h.edges, h.mod],
            [low(rows + 2 * RIM, D), full(1, 4 * D)],
        )

    def joint():
        h.q, h.kv, h.w_in, h.attended, h.probs = order(
            joint_kernel, [h.first, h.bias, *w_in.parts],
            [low(rows, D), low(rows + 2 * RIM, 2 * D), low(D, 3 * D),
             low(rows, D), low(rows, HEADS * WINDOW)],
            mib=14,
        )

    def mlp():
        h.mixed, h.second, h.swished, h.slope, h.w_out, h.w_exp = order(
            mlp_forward_kernel, [h.attended, h.states, h.mod, *w_exp.parts],
            [full(rows, D), low(rows, D), low(rows, hidden), low(rows, hidden),
             low(D, D), low(D, hidden)],
            mib=12,
        )

    def con_grad():
        slots = low(4, chips, own, D)
        g_con.begin(*order(
            contract_grads_kernel, [h.swished, h.cot], [slots, slots],
            [pltpu.VMEM((hidden, D), F32)], mib=12,
        ))

    def back_low():
        h.up_low, h.second_low, h.w_con = order(
            mlp_backward_low_kernel, [h.slope, h.cot, h.w_exp, *w_con.parts],
            [low(split, hidden), full(split, D), low(hidden, D)], mib=10,
        )

    def back_high():
        h.up_high, h.second_high = order(
            mlp_backward_high_kernel, [h.slope, h.cot, h.w_exp, h.w_con],
            [low(split, hidden), full(split, D)], mib=10,
        )

    def final():
        h.final, h.input_grad = order(
            final_kernel, [h.mixed, h.swished, h.w_con, h.input_grad],
            [jax.ShapeDtypeStruct((rows, D), BF16), jax.ShapeDtypeStruct((rows, D), F32)],
            [pltpu.VMEM((rows, D), BF16), pltpu.SemaphoreType.DMA((1 + rows // PIECE,))],
            mib=8, whole=(0, 1),
        )

    def norm():
        h.d_mixed, h.d_low, h.d_attended, h.sums_two = order(
            norm_backward_kernel,
            [h.mixed, h.second_low, h.second_high, h.cot, h.mod, h.w_out],
            [full(rows, D), low(rows, D), low(rows, D), full(8, D)], mib=8,
        )

    def exp_grad():
        slots = low(4, chips, own, hidden // 4 + D // 4)
        g_exp.begin(*order(
            expand_grads_kernel, [h.second, h.up_low, h.up_high, h.attended, h.d_low],
            [slots, slots], [pltpu.VMEM((D, hidden), F32), pltpu.VMEM((D, D), F32)], mib=12,
        ))

    def attn():
        h.dq, h.dkv, core, chip = order(
            attend_back_kernel, [h.q, h.kv, h.probs, h.d_attended],
            [low(rows, D), low(rows + 2 * RIM, 2 * D), low(RIM, 2 * D), low(RIM, 2 * D)],
            mib=12,
        )
        h.edges = [net.cores(core), net.beside(chip)]

    def edge_take():
        h.edges = [w_in.take(edge) for edge in h.edges]

    def in_grad():
        slots = low(4, chips, *slab)
        g_in.begin(*order(
            in_grads_kernel, [h.first, h.dq, h.dkv], [slots, slots],
            [pltpu.VMEM((D, 3 * D), F32)], mib=8,
        ))

    def input_step():
        kernel = functools.partial(input_grad_kernel, net.noise, net.nodes)
        h.input_grad, rider = order(
            kernel,
            [h.dq, h.dkv, *h.edges, h.states, h.d_mixed, h.mod, h.w_in, h.sums_two, cond],
            [full(rows, D), low(riders, *slab)],
            [pltpu.VMEM((rows + 2 * RIM, 2 * D), BF16), pltpu.VMEM((8, 5 * D), F32),
             pltpu.VMEM((riders, *slab), F32)],
            mib=10, free=(9,),
        )
        h.rider = (rider, net.cores(rider))

    def in_chip():
        g_in.chip(1, h.rider)

    def con_up():
        job = (g_con, [(slice(None), True)], [contract_weight, contract_first, contract_second])
        h.contract_new = update_call(order, [job])

    def last_up():
        inward = [inward_weight, inward_first, inward_second]
        others = [
            expand_weight, expand_first, expand_second,
            outward_weight, outward_first, outward_second,
        ]
        cut = hidden // 4
        jobs = [
            (g_in, [(slice(None), False)], inward),
            (g_exp, [(slice(None, cut), False), (slice(cut, None), False)], others),
        ]
        h.last_new = update_call(
            order, jobs, (modulate_weight, modulate_first, modulate_second),
            functools.partial(modulate_grads, net.noise, own),
        )

    plan = (
        (w_in.pack, 0), (load, 20), (w_exp.pack, 50), (mod, 50), (w_in.swap, 3), (mod_core, 20),
        (w_con.pack, 5), (mod_near, 0), (w_in.near, 0), (edges, 0), (w_exp.swap, 80),
        (w_in.core, 0), (w_con.swap, 20), (mod_sum, 3), (w_in.far, 0), (w_exp.near, 200),
        (load_cot, 200), (first, 0), (counts, 5), (joint, 0), (w_con.near, 120), (w_exp.core, 0),
        (w_exp.far, 10), (w_con.core, 10), (mlp, 30), (w_con.far, 80), (con_grad, 120),
        (back_low, 200), (g_con.one, 200), (back_high, 30), (norm, 100), (exp_grad, 1),
        (g_con.two, 50), (attn, 50), (g_exp.one, 120), (g_con.chip, 0), (in_grad, 30),
        (g_exp.two, 50), (g_in.one, 120), (edge_take, 200), (g_con.chips, 20), (input_step, 10),
        (g_con.three, 5), (g_in.two, 0), (g_exp.chip, 3), (in_chip, 10), (g_exp.chips, 80),
        (g_con.four, 10), (g_in.chips, 400), (final, 50), (g_exp.three, 0), (g_in.three, 5),
        (g_exp.four, 30), (g_in.four, 0), (con_up, 80), (last_up, 50),
    )
    for step, tenths in plan:
        order.tenths = tenths
        step()

    inward_new, expand_new, outward_new, modulate_new = (
        h.last_new[k : k + 3] for k in (0, 3, 6, 9)
    )
    return (
        h.final[None], h.input_grad[None],
        *inward_new, *outward_new, *expand_new, *h.contract_new, *modulate_new,
    )


def solution(mesh):
    grid = P(NOISE, NODES, None)
    shard = P(NODES, None)
    return jax.shard_map(
        per_device,
        mesh=mesh,
        in_specs=(grid, P(NOISE), grid, grid) + (shard,) * 15,
        out_specs=(grid, grid) + (shard,) * 15,
        check_vma=False,
    )
```

```python
import functools
import math

import jax
import jax.numpy as jnp
from jax import lax
from jax.experimental import pallas as pl
from jax.experimental.pallas import tpu as pltpu
from jax.sharding import PartitionSpec as P

D = 512
HEADS = 4
NEIGH = 16
RIM = 64
STEP = 10
HEAD_DIM = 128
BLOCK = 128
WINDOW = BLOCK + 2 * RIM
GROUP = 4
HALF = 512
CHUNK = 1024
PIECE = 256
LANES = 128
RIDER_ROWS = 8
NOISE, NODES = AXES = ("noise", "nodes")
BF16 = jnp.bfloat16
F32 = jnp.float32
NONE = -1e30
SMALL = 1.0 / math.sqrt(HEAD_DIM)

VMEM = pl.BlockSpec(memory_space=pltpu.VMEM)
HBM = pl.BlockSpec(memory_space=pltpu.HBM)


def dot(left, right, left_dim, right_dim):
    return lax.dot_general(
        left, right, (((left_dim,), (right_dim,)), ((), ())), preferred_element_type=F32
    )


def fourier(sigma):
    half = D // 2
    counter = jnp.arange(half).astype(F32)
    freqs = jnp.exp(counter * (math.log(64.0) / (half - 1)))
    phase = jnp.log(sigma)[:, None] * freqs[None, :]
    return jnp.concatenate([jnp.sin(phase), jnp.cos(phase)], axis=-1)


def normalize_parts(values):
    center = values - jnp.mean(values, axis=-1, keepdims=True)
    inverse = lax.rsqrt(jnp.mean(center * center, axis=-1, keepdims=True) + 1e-06)
    return (center * inverse, inverse)


def norm_back(normed, inverse, grads):
    average = jnp.mean(grads, axis=-1, keepdims=True)
    along = jnp.mean(grads * normed, axis=-1, keepdims=True)
    return inverse * (grads - average - normed * along)


def adamw(weight, first, second, grads):
    moment = 0.5 * first + 0.5 * grads
    square = 0.75 * second + 0.25 * grads * grads
    level = square * (1.0 / (1.0 - 0.75**STEP))
    root = level * lax.rsqrt(level)
    ratio = moment * (1.0 / (1.0 - 0.5**STEP)) / (root + 1e-08)
    return (moment, square, weight - 0.02 * (ratio + 0.1 * weight))


def pinned(shape, dtype):
    return pltpu.VMEM(tuple(shape), dtype)


class Order:
    def __init__(self):
        self.tick = None
        self.tenths = 0

    def __call__(self, kernel, ins, outs, scratch=(), mib=8, free=(), loose=(), whole=()):
        before = [] if self.tick is None else [self.tick]

        def body(*refs):
            first = len(ins) + len(before)
            last = first + len(outs)
            kernel(*refs[: len(ins)], *refs[first:last], *refs[last + 1 :])
            refs[last][...] = jnp.zeros((8, LANES), F32)

        keep = lambda array: pltpu.with_memory_space_constraint(array, pltpu.VMEM)
        stay = lambda array: pltpu.with_memory_space_constraint(array, pltpu.HBM)
        arrays = [
            a if k in free else stay(a) if k in loose else keep(a) for k, a in enumerate(ins)
        ]
        specs = [HBM if k in loose else VMEM for k in range(len(ins))]
        named = kernel.func if isinstance(kernel, functools.partial) else kernel
        *results, self.tick = pl.pallas_call(
            body,
            in_specs=specs + [VMEM] * len(before),
            out_specs=[HBM if k in whole else VMEM for k in range(len(outs))] + [VMEM],
            out_shape=list(outs) + [pinned((8, LANES), F32)],
            scratch_shapes=list(scratch),
            compiler_params=pltpu.CompilerParams(vmem_limit_bytes=mib * 2**20),
            cost_estimate=pl.CostEstimate(
                flops=self.tenths * 10**8, bytes_accessed=1, transcendentals=0
            ),
            name=named.__name__,
        )(*arrays, *map(keep, before))
        return results


class Place:
    def __init__(self):
        self.device = lax.axis_index(NODES)
        self.n = lax.axis_index(NOISE)
        self.core = lax.rem(self.device, 2)
        self.chip = lax.div(self.device, 2)
        swapped = lax.rem(self.n, 2) * 2 + lax.div(self.n, 2)
        self.role = jnp.where(self.core == 0, self.n, swapped)
        self.other = jnp.where(self.core == 0, swapped, self.n)


def load_kernel(*refs):
    count, sems = len(refs) // 2, refs[-1]
    copies = [
        pltpu.make_async_copy(refs[k], refs[count + k], sems.at[k]) for k in range(count)
    ]
    for copy in copies:
        copy.start()
    for copy in copies:
        copy.wait()


def load_more_kernel(*refs):
    load_kernel(*refs)


def count_kernel(total, near_ref, bias_ref):
    rows = bias_ref.shape[0]
    base = Place().device * rows - RIM
    shape = (WINDOW, BLOCK)
    window = lax.broadcasted_iota(jnp.int32, shape, 0).astype(jnp.int16)
    one, zero = jnp.ones(shape, BF16), jnp.zeros(shape, BF16)
    for start in range(0, rows, BLOCK):
        place = near_ref[:, start : start + BLOCK] - (base + start)
        place = jnp.where(place < 0, place + total, place)
        place = jnp.where(place >= total, place - total, place).astype(jnp.int16)
        count = zero
        for k in range(NEIGH):
            here = jnp.broadcast_to(place[k : k + 1, :], shape) == window
            count = count + jnp.where(here, one, zero)
        count = count.astype(F32)
        bias = jnp.where(count > 0.0, jnp.log(count), NONE)
        bias_ref[start : start + BLOCK, :] = bias.T


def pack_inward_kernel(inward_ref, halves_ref):
    wide = halves_ref.shape[2]
    for half in range(2):
        halves_ref[half] = inward_ref[:, half * wide : (half + 1) * wide].astype(BF16)


def pack_expand_kernel(expand_ref, outward_ref, halves_ref):
    wide = expand_ref.shape[1] // 2
    for half in range(2):
        left = expand_ref[:, half * wide : (half + 1) * wide].astype(BF16)
        right = outward_ref[:, half * D // 2 : (half + 1) * D // 2].astype(BF16)
        halves_ref[half, :, :wide] = left
        halves_ref[half, :, wide:] = right


def pack_contract_kernel(contract_ref, halves_ref):
    own = halves_ref.shape[1]
    for k in range(4):
        rows = contract_ref[k * own : (k + 1) * own, :].astype(BF16)
        halves_ref[k // 2, :, k % 2 * D : (k % 2 + 1) * D] = rows


def near_kernel(halves_ref, fetched_ref, got_ref, near_ref, every_ref):
    place = Place()
    mine = jnp.where(place.core == 0, lax.rem(place.n, 2), 1 - lax.div(place.n, 2))
    for half in range(2):
        near_ref[2 * mine + half] = fetched_ref[half]
        near_ref[2 * (1 - mine) + half] = got_ref[half]
        every_ref[4 + half] = halves_ref[half]
    for k in range(4):
        every_ref[k] = near_ref[k]


def take_kernel(value_ref, out_ref):
    out_ref[...] = value_ref[...]


def edges_kernel(states_ref, core_ref, chip_ref):
    core = Place().core
    rows = states_ref.shape[0]
    head, tail = states_ref[:RIM, :], states_ref[rows - RIM :, :]

    @pl.when(core == 0)
    def _():
        core_ref[...] = tail
        chip_ref[...] = head

    @pl.when(core == 1)
    def _():
        core_ref[...] = head
        chip_ref[...] = tail


def modulation_kernel(cond_ref, weight_ref, out_ref):
    own = weight_ref.shape[0]
    first = Place().device * own
    rows = lax.broadcasted_iota(jnp.int32, (D, own), 0)
    cols = lax.broadcasted_iota(jnp.int32, (D, own), 1)
    chosen = jnp.where(rows == cols + first, 1.0, 0.0).astype(BF16)
    mine = dot(cond_ref[...], chosen, 1, 0).astype(BF16)
    out_ref[...] = dot(mine, weight_ref[...].astype(BF16), 1, 0)


def encode(row_ref, target_ref):
    for k in range(4):
        value = row_ref[0:1, k * D : (k + 1) * D]
        high = value.astype(BF16)
        target_ref[RIM + k : RIM + k + 1, :] = high.astype(F32)
        target_ref[RIM + 4 + k : RIM + 5 + k, :] = value - high.astype(F32)


def decode(source_ref):
    rows = source_ref[RIM : RIM + 16, :].astype(F32)
    return jnp.concatenate([rows[k : k + 1] + rows[4 + k : 5 + k] for k in range(4)], axis=1)


def open_kernel(cond_ref, weight_ref, states_ref, part_ref, core_ref, chip_ref, wide_ref):
    modulation_kernel(cond_ref, weight_ref, part_ref)
    wide_ref[RIM:, :] = jnp.zeros((16, D), F32)
    encode(part_ref, wide_ref)
    core_ref[RIM:, :] = wide_ref[RIM:, :].astype(BF16)
    edges_kernel(states_ref, core_ref.at[:RIM], chip_ref)


def open_core_kernel(part_ref, got_ref, chip_ref, sum_ref, edge_ref, send_ref, wide_ref):
    sum_ref[...] = part_ref[...] + decode(got_ref)
    edge_ref[...] = got_ref[:RIM, :]
    send_ref[:RIM, :] = chip_ref[...]
    wide_ref[RIM:, :] = jnp.zeros((16, D), F32)
    encode(sum_ref, wide_ref)
    send_ref[RIM:, :] = wide_ref[RIM:, :].astype(BF16)


def open_chip_kernel(sum_ref, got_ref, near_ref, edge_ref, out_ref):
    near = decode(got_ref)
    near_ref[...] = near
    edge_ref[...] = got_ref[:RIM, :]
    out_ref[...] = sum_ref[...] + near


def open_far_kernel(sum_ref, got_ref, out_ref, send_ref):
    out_ref[...] = sum_ref[...] + got_ref[...]
    send_ref[...] = got_ref[...]


def sum_kernel(left_ref, right_ref, out_ref):
    out_ref[...] = left_ref[...] + right_ref[...]


def first_kernel(states_ref, core_ref, chip_ref, left_ref, right_ref, first_ref, mod_ref):
    core = Place().core
    mod_ref[...] = left_ref[...] + right_ref[...]
    scale = 1.0 + mod_ref[0:1, :D]
    shift = mod_ref[0:1, D : 2 * D]
    rows = states_ref.shape[0]

    def put(at, values):
        normed, _ = normalize_parts(values.astype(F32))
        first_ref[at : at + values.shape[0], :] = (normed * scale + shift).astype(BF16)

    put(RIM, states_ref[...])

    @pl.when(core == 0)
    def _():
        put(0, chip_ref[...])
        put(RIM + rows, core_ref[...])

    @pl.when(core == 1)
    def _():
        put(0, core_ref[...])
        put(RIM + rows, chip_ref[...])


def heads(array_ref, start, rows, base):
    return [
        array_ref[start : start + rows, base + h * HEAD_DIM : base + (h + 1) * HEAD_DIM]
        for h in range(HEADS)
    ]


def joint_kernel(first_ref, bias_ref, *refs):
    parts = refs[:-5]
    q_ref, kv_ref, w_ref, out_ref, probs_ref = refs[-5:]
    rows = q_ref.shape[0]
    deep, width = parts[0].shape[1:]

    def put(ref, block, half):
        span = pl.ds(pl.multiple_of(block * deep, deep), deep)
        w_ref[span, half * width : (half + 1) * width] = ref[...]

    assemble(parts, put)
    q_ref[...] = dot(first_ref[RIM : RIM + rows, :], w_ref[:, :D], 1, 0).astype(BF16)
    kv_ref[...] = dot(first_ref[...], w_ref[:, D:], 1, 0).astype(BF16)
    for group in range(0, rows, GROUP * BLOCK):
        starts = range(group, min(group + GROUP * BLOCK, rows), BLOCK)
        jobs = [(s, h) for s in starts for h in range(HEADS)]
        queries = [x for s in starts for x in heads(q_ref, s, BLOCK, 0)]
        keys = [x for s in starts for x in heads(kv_ref, s, WINDOW, 0)]
        values = [x for s in starts for x in heads(kv_ref, s, WINDOW, D)]
        scores = [dot(q, k, 1, 1) for q, k in zip(queries, keys)]
        scores = [x * SMALL + bias_ref[s : s + BLOCK, :] for x, (s, _) in zip(scores, jobs)]
        tops = [jnp.max(x, axis=1, keepdims=True) for x in scores]
        expos = [jnp.exp(x - t) for x, t in zip(scores, tops)]
        sums = [jnp.sum(x, axis=1, keepdims=True) for x in expos]
        probs = [(x * (1.0 / t)).astype(BF16) for x, t in zip(expos, sums)]
        outs = [dot(p, v, 1, 0).astype(BF16) for p, v in zip(probs, values)]
        for p, o, (s, h) in zip(probs, outs, jobs):
            probs_ref[s : s + BLOCK, h * WINDOW : (h + 1) * WINDOW] = p
            out_ref[s : s + BLOCK, h * HEAD_DIM : (h + 1) * HEAD_DIM] = o


def attend_back_kernel(
    q_ref, kv_ref, probs_ref, grad_ref, dq_ref, dkv_ref, core_ref, chip_ref
):
    rows = q_ref.shape[0]
    carry = [jnp.zeros((BLOCK, HEAD_DIM), F32)] * (2 * HEADS)
    for group in range(0, rows, GROUP * BLOCK):
        starts = range(group, min(group + GROUP * BLOCK, rows), BLOCK)
        jobs = [(s, h) for s in starts for h in range(HEADS)]
        queries = [x for s in starts for x in heads(q_ref, s, BLOCK, 0)]
        grads = [x for s in starts for x in heads(grad_ref, s, BLOCK, 0)]
        keys = [x for s in starts for x in heads(kv_ref, s, WINDOW, 0)]
        values = [x for s in starts for x in heads(kv_ref, s, WINDOW, D)]
        probs = [probs_ref[s : s + BLOCK, h * WINDOW : (h + 1) * WINDOW] for s, h in jobs]
        d_probs = [dot(g, v, 1, 1) for g, v in zip(grads, values)]
        weighted = [p.astype(F32) * d for p, d in zip(probs, d_probs)]
        totals = [jnp.sum(w, axis=1, keepdims=True) for w in weighted]
        d_scores = [
            ((w - p.astype(F32) * t) * SMALL).astype(BF16)
            for w, p, t in zip(weighted, probs, totals)
        ]
        d_queries = [dot(d, k, 1, 0).astype(BF16) for d, k in zip(d_scores, keys)]
        d_keys = [dot(d, q, 0, 0) for d, q in zip(d_scores, queries)]
        d_values = [dot(p, g, 0, 0) for p, g in zip(probs, grads)]
        for x, (s, h) in zip(d_queries, jobs):
            dq_ref[s : s + BLOCK, h * HEAD_DIM : (h + 1) * HEAD_DIM] = x
        for column in range(2 * HEADS):
            parts = (d_keys if column < HEADS else d_values)[column % HEADS :: HEADS]
            cols = slice(column * HEAD_DIM, (column + 1) * HEAD_DIM)
            for s, part in zip(starts, parts):
                dkv_ref[s : s + BLOCK, cols] = (carry[column] + part[:BLOCK]).astype(BF16)
                carry[column] = part[BLOCK:]
    for column, part in enumerate(carry):
        cols = slice(column * HEAD_DIM, (column + 1) * HEAD_DIM)
        dkv_ref[rows : rows + BLOCK, cols] = part.astype(BF16)
    core = Place().core
    low, high = dkv_ref[:RIM, :], dkv_ref[rows + RIM :, :]

    @pl.when(core == 0)
    def _():
        core_ref[...] = high
        chip_ref[...] = low

    @pl.when(core == 1)
    def _():
        core_ref[...] = low
        chip_ref[...] = high


def assemble(parts, put):
    if len(parts) == 1:
        for half in range(2):
            put(parts[0].at[half], 0, half)
        return
    place = Place()
    for p in range(2):
        near, far = parts[2 * p : 2 * p + 2]
        owner = place.core if p == 0 else 1 - place.core

        def put_all(next_one, second, third):
            for half in range(2):
                for s, ref in enumerate((near.at[4 + half], next_one, second, third)):
                    part = ref if s == 0 else ref[0].at[ref[1] + half]
                    put(part, lax.rem(place.chip + s, 4) * 2 + owner, half)

        for core, bit in ((0, lax.div(place.n, 2)), (1, lax.rem(place.n, 2))):
            for turn in range(2):
                low, high = (near, far) if turn == 0 else (far, near)

                @pl.when(jnp.logical_and(owner == core, bit == turn))
                def _():
                    put_all((low, 2) if core == 0 else (high, 0), (low, 0), (high, 2))


def copy_rows(source, target, rows, sem):
    copy = pltpu.make_async_copy(source.at[rows], target.at[rows], sem)
    copy.start()
    return copy


def write_slots(targets, block_of):
    place = Place()
    owners = (place.core, 1 - place.core)
    for target, owner, role in zip(targets, owners, (place.role, place.other)):
        for slot in range(4):
            quarter = role ^ ((slot // 2) + 2 * (slot % 2))
            for s in range(target.shape[1]):
                target[slot, s] = block_of((place.chip ^ s) * 2 + owner, quarter).astype(BF16)


def mlp_forward_kernel(attended_ref, states_ref, mod_ref, *refs):
    parts = refs[:-6]
    mixed_ref, second_ref, swished_ref, slope_ref, w_out_ref, w_exp_ref = refs[-6:]
    hidden = w_exp_ref.shape[1]
    deep = parts[0].shape[1]

    def put(ref, block, half):
        rows = pl.ds(pl.multiple_of(block * deep, deep), deep)
        wide, thin = hidden // 2, D // 2
        w_exp_ref[rows, half * wide : (half + 1) * wide] = ref[:, :wide]
        w_out_ref[rows, half * thin : (half + 1) * thin] = ref[:, wide:]

    assemble(parts, put)
    scale = 1.0 + mod_ref[0:1, 2 * D : 3 * D]
    shift = mod_ref[0:1, 3 * D :]
    for start in range(0, states_ref.shape[0], HALF):
        rows = slice(start, start + HALF)
        mixed = states_ref[rows].astype(F32) + dot(attended_ref[rows], w_out_ref[...], 1, 0)
        mixed_ref[rows] = mixed
        normed, _ = normalize_parts(mixed)
        second_in = (normed * scale + shift).astype(BF16)
        second_ref[rows] = second_in
        for at in range(0, hidden, CHUNK):
            cols = slice(at, at + CHUNK)
            up = dot(second_in, w_exp_ref[:, cols], 1, 0)
            gate = 0.5 + 0.5 * jnp.tanh(0.5 * up)
            product = up * gate
            swished_ref[rows, cols] = product.astype(BF16)
            slope_ref[rows, cols] = (gate + product * (1.0 - gate)).astype(BF16)

def contract_grads_kernel(swished_ref, cot_ref, keep_ref, send_ref, grad_ref):
    own = keep_ref.shape[2]
    grad_ref[...] = dot(swished_ref[...], cot_ref[...], 0, 0)
    write_slots(
        (keep_ref, send_ref),
        lambda block, quarter: grad_ref[
            pl.ds(pl.multiple_of((block * 4 + quarter) * own, own), own), :
        ],
    )


def mlp_backward(rows, slope_ref, cot_ref, w_exp_ref, w_con_ref, d_up_ref, d_second_ref):
    hidden = w_exp_ref.shape[1]
    cot = cot_ref[rows]
    d_second = jnp.zeros(d_second_ref.shape, F32)
    for at in range(0, hidden, CHUNK):
        cols = slice(at, at + CHUNK)
        d_swished = dot(cot, w_con_ref[cols, :], 1, 1)
        d_up = (d_swished * slope_ref[rows, cols].astype(F32)).astype(BF16)
        d_up_ref[:, cols] = d_up
        d_second = d_second + dot(d_up, w_exp_ref[:, cols], 1, 1)
    d_second_ref[...] = d_second


def mlp_backward_low_kernel(slope_ref, cot_ref, w_exp_ref, *refs):
    parts = refs[:-3]
    d_up_ref, d_second_ref, w_con_ref = refs[-3:]
    deep = parts[0].shape[1]

    def put(ref, block, half):
        for k in range(2):
            start = pl.multiple_of((block * 4 + half * 2 + k) * deep, deep)
            w_con_ref[pl.ds(start, deep), :] = ref[:, k * D : (k + 1) * D]

    assemble(parts, put)
    rows = slice(0, d_up_ref.shape[0])
    mlp_backward(rows, slope_ref, cot_ref, w_exp_ref, w_con_ref, d_up_ref, d_second_ref)


def mlp_backward_high_kernel(slope_ref, cot_ref, w_exp_ref, w_con_ref, d_up_ref, d_second_ref):
    half = d_up_ref.shape[0]
    rows = slice(half, 2 * half)
    mlp_backward(rows, slope_ref, cot_ref, w_exp_ref, w_con_ref, d_up_ref, d_second_ref)


def final_kernel(
    mixed_ref, swished_ref, w_con_ref, grad_ref, final_ref, grad_out_ref, done_ref, sems
):
    sends = [pltpu.make_async_copy(grad_ref, grad_out_ref, sems.at[0])]
    sends[0].start()
    for start in range(0, mixed_ref.shape[0], PIECE):
        rows = slice(start, start + PIECE)
        final = mixed_ref[rows] + dot(swished_ref[rows], w_con_ref[...], 1, 0)
        done_ref[rows] = final.astype(BF16)
        sends.append(copy_rows(done_ref, final_ref, rows, sems.at[len(sends)]))
    for send in sends:
        send.wait()


def norm_backward_kernel(
    mixed_ref, low_ref, high_ref, cot_ref, mod_ref, w_out_ref,
    d_mixed_ref, d_low_ref, d_att_ref, sums_ref,
):
    scale = 1.0 + mod_ref[0:1, 2 * D : 3 * D]
    sums_ref[...] = jnp.zeros_like(sums_ref)
    half = low_ref.shape[0]
    for k, d_second_ref in enumerate((low_ref, high_ref)):
        rows = slice(k * half, (k + 1) * half)
        normed, inverse = normalize_parts(mixed_ref[rows])
        d_second = d_second_ref[...]
        sums_ref[0:1, :] += jnp.sum(d_second * normed, axis=0, keepdims=True)
        sums_ref[1:2, :] += jnp.sum(d_second, axis=0, keepdims=True)
        d_mixed = cot_ref[rows].astype(F32) + norm_back(normed, inverse, d_second * scale)
        d_mixed_ref[rows] = d_mixed
        d_low_ref[rows] = d_mixed.astype(BF16)
        d_att_ref[rows] = dot(d_mixed.astype(BF16), w_out_ref[...], 1, 1).astype(BF16)


def expand_grads_kernel(
    second_ref, low_ref, high_ref, attended_ref, d_low_ref, keep_ref, send_ref, exp_ref, out_ref
):
    own, unit = keep_ref.shape[2:]
    wide = unit - D // 4
    half = low_ref.shape[0]
    exp_ref[...] = dot(second_ref[:half, :], low_ref[...], 0, 0)
    exp_ref[...] += dot(second_ref[half:, :], high_ref[...], 0, 0)
    out_ref[...] = dot(attended_ref[...], d_low_ref[...], 0, 0)

    def block_of(block, quarter):
        rows = pl.ds(pl.multiple_of(block * own, own), own)
        first = exp_ref[rows, pl.ds(pl.multiple_of(quarter * wide, wide), wide)]
        second = out_ref[rows, pl.ds(pl.multiple_of(quarter * (D // 4), D // 4), D // 4)]
        return jnp.concatenate([first, second], axis=1)

    write_slots((keep_ref, send_ref), block_of)


def in_grads_kernel(first_ref, dq_ref, dkv_ref, keep_ref, send_ref, in_ref):
    own, unit = keep_ref.shape[2:]
    rows = dq_ref.shape[0]
    in_ref[:, :D] = dot(first_ref[RIM : RIM + rows, :], dq_ref[...], 0, 0)
    in_ref[:, D:] = dot(first_ref[...], dkv_ref[...], 0, 0)
    write_slots(
        (keep_ref, send_ref),
        lambda block, quarter: in_ref[
            pl.ds(pl.multiple_of(block * own, own), own),
            pl.ds(pl.multiple_of(quarter * unit, unit), unit),
        ],
    )


def rider_spots(copy, own):
    for group in range(5 * D // LANES):
        row = copy * RIDER_ROWS + group // 3
        at = (group % 3) * LANES
        yield group, row // own, row % own, slice(at, at + LANES)


def input_grad_kernel(
    copies, nodes, dq_ref, dkv_ref, core_ref, chip_ref, states_ref, d_mixed_ref, mod_ref, w_in_ref,
    sums_two_ref, cond_ref, grad_ref, rider_ref, wide_ref, row_ref, slab_ref,
):
    place = Place()
    rows = states_ref.shape[0]
    wide_ref[...] = dkv_ref[...]

    def join(at, ref):
        part = slice(at, at + RIM)
        wide_ref[part, :] = (wide_ref[part, :].astype(F32) + ref[...].astype(F32)).astype(BF16)

    @pl.when(place.core == 0)
    def _():
        join(RIM, chip_ref)
        join(rows, core_ref)

    @pl.when(place.core == 1)
    def _():
        join(RIM, core_ref)
        join(rows, chip_ref)

    scale = 1.0 + mod_ref[0:1, :D]
    d_scale = jnp.zeros((1, D), F32)
    d_shift = jnp.zeros((1, D), F32)
    for start in range(0, rows, HALF):
        part = slice(start, start + HALF)
        normed, inverse = normalize_parts(states_ref[part].astype(F32))
        d_first = dot(dq_ref[part], w_in_ref[:, :D], 1, 1) + dot(
            wide_ref[RIM + start : RIM + start + HALF, :], w_in_ref[:, D:], 1, 1
        )
        d_scale = d_scale + jnp.sum(d_first * normed, axis=0, keepdims=True)
        d_shift = d_shift + jnp.sum(d_first, axis=0, keepdims=True)
        grad_ref[part] = d_mixed_ref[part] + norm_back(normed, inverse, d_first * scale)
    row_ref[0:1, :D] = d_scale
    row_ref[0:1, D : 2 * D] = d_shift
    row_ref[0:1, 2 * D : 3 * D] = sums_two_ref[0:1, :]
    row_ref[0:1, 3 * D : 4 * D] = sums_two_ref[1:2, :]
    row_ref[0:1, 4 * D :] = cond_ref[0:1, :].astype(F32) * (1.0 / nodes)
    slab_ref[...] = jnp.zeros_like(slab_ref)
    for copy in range(copies):
        mine = jnp.where(place.n == copy, 1.0, 0.0)
        for group, slab, row, cols in rider_spots(copy, slab_ref.shape[1]):
            values = row_ref[0:1, group * LANES : (group + 1) * LANES]
            slab_ref[slab, row : row + 1, cols] = values * mine
    rider_ref[...] = slab_ref[...].astype(BF16)


def modulate_grads(copies, own, riders, row_ref, slab_ref):
    slab_ref[...] = riders
    row_ref[...] = jnp.zeros_like(row_ref)
    for copy in range(copies):
        for group, slab, row, cols in rider_spots(copy, slab_ref.shape[1]):
            row_ref[copy : copy + 1, group * LANES : (group + 1) * LANES] = slab_ref[
                slab, row : row + 1, cols
            ]
    everyone = row_ref[...].astype(BF16)
    chosen = lax.broadcasted_iota(jnp.int32, (D, own), 0) == (
        lax.broadcasted_iota(jnp.int32, (D, own), 1) + Place().device * own
    )
    conds = dot(everyone[:, 4 * D :], jnp.where(chosen, 1.0, 0.0).astype(BF16), 1, 0)
    return dot(conds.astype(BF16), everyone[:, : 4 * D], 0, 0)


def update_quarters(spots, cut, pair_ref, got_ref, ins, outs, sems):
    role = Place().role
    sends = []
    for k, (cols, by_rows) in enumerate(spots):
        for slot in range(4):
            quarter = role ^ ((slot // 2) + 2 * (slot % 2))
            source = pair_ref if slot < 2 else got_ref
            for part in range(cut):
                grads = source[slot % 2 * cut + part, :, cols].astype(F32)
                height, width = grads.shape
                if by_rows:
                    at = (pl.ds(pl.multiple_of(quarter * height, height), height), slice(None))
                else:
                    at = (
                        slice(part * height, (part + 1) * height),
                        pl.ds(pl.multiple_of(quarter * width, width), width),
                    )
                values = adamw(*(ref[at] for ref in ins[3 * k : 3 * k + 3]), grads)
                for j, value in enumerate(values, 3 * k):
                    scratch, target = outs[j]
                    scratch[at] = value
                    sends.append(pltpu.make_async_copy(
                        scratch.at[at], target.at[at], sems.at[j, slot * cut + part]
                    ))
                    sends[-1].start()
    return sends


class Net:
    def __init__(self):
        self.noise = lax.axis_size(NOISE)
        self.nodes = lax.axis_size(NODES)
        self.chips = self.nodes // 2
        self.quick = self.chips == 4

    def permute(self, value, move):
        pairs = []
        for n in range(self.noise):
            for z in range(self.chips):
                for c in range(2):
                    n2, z2, c2 = move(n, z, c)
                    source = (n * self.chips + z) * 2 + c
                    target = (n2 * self.chips + z2 % self.chips) * 2 + c2
                    pairs.append((source, target))
        return lax.ppermute(value, AXES, pairs)

    def role_of(self, n, c):
        return n if c == 0 else (n % 2) * 2 + n // 2

    def swap(self, value, bit):
        return self.permute(value, lambda n, z, c: (n ^ (bit if c == 0 else 3 - bit), z, c))

    def cores(self, value):
        return self.permute(value, lambda n, z, c: (n, z, 1 - c))

    def beside(self, value):
        return self.permute(value, lambda n, z, c: (n, z + 2 * c - 1, 1 - c))

    def across(self, value, step):
        return self.permute(value, lambda n, z, c: (n, z ^ step, c))

    def fetch(self, halves):
        back = (2, 3, 0, 1)
        return self.permute(halves, lambda n, z, c: (n, z + back[n ^ (2 * c)], c))


class Gathering:
    def __init__(self, net, order, kernel, arrays, half, stacked=False):
        self.net, self.order, self.kernel, self.arrays = net, order, kernel, arrays
        self.half, self.stacked = half, stacked

    def shape(self, count):
        return pinned((count, *self.half), BF16)

    def take(self, value):
        return self.order(take_kernel, [value], [pinned(value.shape, value.dtype)])[0]

    def pack(self):
        arrays, free = self.arrays()
        self.halves, = self.order(self.kernel, arrays, [self.shape(2)], free=free)
        if self.net.quick:
            self.got = self.net.fetch(self.halves)
            return
        every = lax.all_gather(self.halves, NODES, axis=1, tiled=True)
        if self.stacked:
            own = self.half[0]
            every = every.reshape(2, -1, own, 2, D).swapaxes(2, 3).swapaxes(0, 1)
            every = every.reshape(2, 2, -1, D).swapaxes(1, 2).reshape(2, -1, 2 * D)
        self.parts = [every]

    def swap(self):
        if not self.net.quick:
            return
        self.fetched = self.take(self.got)
        self.got = self.net.swap(self.fetched, 1)

    def near(self):
        if not self.net.quick:
            return
        near, every = self.order(
            near_kernel, [self.halves, self.fetched, self.got], [self.shape(4), self.shape(6)]
        )
        self.parts = [every, self.net.swap(near, 2), self.net.cores(every), None]

    def core(self):
        if not self.net.quick:
            return
        self.parts[2] = self.take(self.parts[2])

    def far(self):
        if not self.net.quick:
            return
        self.parts[1] = self.take(self.parts[1])
        self.parts[3] = self.net.cores(self.parts[1])


class Reduction:
    def __init__(self, net, order):
        self.net, self.order = net, order
        self.riders = 0
        self.cut = 1

    def begin(self, keep, send):
        self.unit = keep.shape[2:]
        self.held, self.got = keep, self.net.cores(send)

    def shape(self, *lead):
        return pinned((*lead, *self.unit), BF16)

    def one(self):
        def sum_one(held_ref, got_ref, away_ref, out_ref):
            away_ref[...] = held_ref[2:] + got_ref[2:]
            out_ref[...] = held_ref[:2] + got_ref[:2]

        outs = [self.shape(2, self.net.chips)] * 2
        away, self.held = self.order(sum_one, [self.held, self.got], outs)
        self.got = self.net.swap(away, 1)

    def two(self):
        def sum_two(held_ref, got_ref, away_ref, out_ref):
            away_ref[...] = held_ref[1] + got_ref[1]
            out_ref[...] = held_ref[0] + got_ref[0]

        outs = [self.shape(self.net.chips)] * 2
        away, self.held = self.order(sum_two, [self.held, self.got], outs)
        self.got = self.net.swap(away, 2)

    def chip(self, step=1, rider=()):
        own = self.unit[0]
        if rider:
            self.riders = rider[0].shape[0]
            self.cut = own // rider[0].shape[1]
            self.unit = rider[0].shape[1:]
        count = self.net.chips // step
        riders, cut = self.riders, self.cut

        def sum_chips(held_ref, got_ref, *refs):
            away_ref, out_ref = refs[-2:]
            for k in range(count):
                target = away_ref if k % 2 else out_ref
                for part in range(cut):
                    if rider:
                        rows = slice(part * own // cut, (part + 1) * own // cut)
                        total = held_ref[k, rows] + got_ref[k, rows]
                    else:
                        total = held_ref[k * cut + part] + got_ref[k * cut + part]
                    target[k // 2 * cut + part] = total
            for k in range(riders):
                if rider:
                    total = refs[0][k] + refs[1][k]
                else:
                    total = held_ref[count * cut + k] + got_ref[count * cut + k]
                away_ref[count // 2 * cut + k] = total
                out_ref[count // 2 * cut + k] = total

        outs = [self.shape(count // 2 * cut + riders)] * 2
        away, self.held = self.order(sum_chips, [self.held, self.got, *rider], outs)
        self.got = self.net.across(away, step)

    def chips(self):
        step = 2
        while step < self.net.chips:
            self.chip(step)
            step *= 2

    def three(self):
        outs = [self.shape(self.cut + self.riders)]
        self.held, = self.order(sum_kernel, [self.held, self.got], outs)
        self.got = self.net.swap(self.held, 2)

    def four(self):
        riders, cut = self.riders, self.cut

        def join_quarters(held_ref, got_ref, out_ref):
            for k in range(cut):
                out_ref[k] = held_ref[k]
                out_ref[cut + k] = got_ref[k]
            for k in range(riders):
                out_ref[2 * cut + k] = held_ref[cut + k] + got_ref[cut + k]

        outs = [self.shape(2 * cut + riders)]
        self.held, = self.order(join_quarters, [self.held, self.got], outs)
        self.got = self.net.swap(self.held, 1)


def update_call(order, reduction, spots, arrays, more=(), more_grads=None):
    count = len(arrays) + len(more)
    cut = reduction.cut

    def update_weights(pair_ref, got_ref, *refs):
        ins, targets, scratch = refs[:count], refs[count : 2 * count], refs[2 * count :]
        pairs = list(zip(scratch[:count], targets))
        sems = scratch[count]
        sends = update_quarters(spots, cut, pair_ref, got_ref, ins, pairs, sems)
        if more:
            first = 2 * cut
            riders = pair_ref[first:].astype(F32) + got_ref[first:].astype(F32)
            grads = more_grads(riders, *scratch[count + 1 :])
            values = adamw(*(ref[...] for ref in ins[len(arrays) :]), grads)
            for j, value in enumerate(values, len(arrays)):
                scratch[j][...] = value
                sends.append(pltpu.make_async_copy(*pairs[j], sems.at[j, 0]))
                sends[-1].start()
        for send in sends:
            send.wait()

    every = [*arrays, *more]
    scratch = [pltpu.VMEM(a.shape, F32) for a in every]
    scratch.append(pltpu.SemaphoreType.DMA((count, 4 * cut)))
    if more:
        scratch.append(pltpu.VMEM((8, 5 * D), F32))
        scratch.append(pltpu.VMEM((reduction.riders, *reduction.unit), F32))
    return order(
        update_weights, [reduction.held, reduction.got, *every],
        [jax.ShapeDtypeStruct(a.shape, F32) for a in every], scratch,
        mib=12, free=range(2, 2 + count), whole=range(count),
    )


class Held:
    pass


def per_device(
    inputs, sigma, neighbours, cotangent,
    inward_weight, inward_first, inward_second,
    outward_weight, outward_first, outward_second,
    expand_weight, expand_first, expand_second,
    contract_weight, contract_first, contract_second,
    modulate_weight, modulate_first, modulate_second,
):
    net = Net()
    order = Order()
    h = Held()
    states = inputs[0]
    cot = cotangent[0]
    rows = states.shape[0]
    own, hidden = expand_weight.shape
    chips = net.chips
    low = lambda *shape: pinned(shape, BF16)
    full = lambda *shape: pinned(shape, F32)
    split = rows // 2
    slab = (own, 3 * D // 4)
    rider_slab = (own // 2 if own % 32 == 0 else own, 3 * D // 4)
    riders = -(-net.noise * RIDER_ROWS // rider_slab[0])
    cond = fourier(sigma).astype(BF16)

    w_in = Gathering(
        net, order, pack_inward_kernel, lambda: ([inward_weight], (0,)), (own, 3 * D // 2)
    )
    w_exp = Gathering(
        net, order, pack_expand_kernel, lambda: ([h.expand, h.outward], ()),
        (own, hidden // 2 + D // 2),
    )
    w_con = Gathering(
        net, order, pack_contract_kernel, lambda: ([h.contract], ()), (own, 2 * D), stacked=True
    )
    g_in, g_exp, g_con = (Reduction(net, order) for _ in range(3))

    def load_arrays(kernel, arrays):
        return order(
            kernel, arrays, [pinned(a.shape, a.dtype) for a in arrays],
            [pltpu.SemaphoreType.DMA((len(arrays),))], loose=range(len(arrays)),
        )

    def load():
        h.expand, h.outward, h.contract = load_arrays(
            load_kernel, [expand_weight, outward_weight, contract_weight]
        )

    def load_more():
        h.modulate, h.neighbours, h.states, h.cot = load_arrays(
            load_more_kernel, [modulate_weight, neighbours[0].T, states, cot]
        )

    def mod():
        if not net.quick:
            h.mod, = order(modulation_kernel, [cond, h.modulate], [full(1, 4 * D)], free=(0,))
            h.mod_got = net.cores(h.mod)
            return
        wide = RIM + 16
        h.mod, core, h.edge = order(
            open_kernel, [cond, h.modulate, h.states],
            [full(1, 4 * D), low(wide, D), low(RIM, D)], [pltpu.VMEM((wide, D), F32)], free=(0,),
        )
        h.mod_got = net.cores(core)

    def mod_sum():
        h.mod, = order(sum_kernel, [h.mod, h.mod_got], [full(1, 4 * D)])

    def mod_core():
        if not net.quick:
            mod_sum()
            h.mod_got = net.across(h.mod, 1)
            return
        wide = RIM + 16
        h.mod, core_edge, send = order(
            open_core_kernel, [h.mod, h.mod_got, h.edge],
            [full(1, 4 * D), low(RIM, D), low(wide, D)], [pltpu.VMEM((wide, D), F32)],
        )
        h.edges = [core_edge]
        h.mod_got = net.beside(send)

    def mod_near():
        if net.quick:
            near, chip_edge, h.mod = order(
                open_chip_kernel, [h.mod, h.mod_got],
                [full(1, 4 * D), low(RIM, D), full(1, 4 * D)],
            )
            h.edges.append(chip_edge)
            h.mod_got = net.cores(near)
            return
        step = 2
        while step < chips:
            mod_sum()
            h.mod_got = net.across(h.mod, step)
            step *= 2

    def mod_far():
        if net.quick:
            h.mod, send = order(
                open_far_kernel, [h.mod, h.mod_got], [full(1, 4 * D), full(1, 4 * D)]
            )
            h.mod_got = net.beside(send)
            return
        core, chip = order(edges_kernel, [h.states], [low(RIM, D), low(RIM, D)])
        h.edges = [net.cores(core), net.beside(chip)]

    def counts():
        kernel = functools.partial(count_kernel, rows * net.nodes)
        h.bias, = order(kernel, [h.neighbours], [full(rows, WINDOW)])

    def first():
        h.first, h.mod = order(
            first_kernel, [h.states, *h.edges, h.mod, h.mod_got],
            [low(rows + 2 * RIM, D), full(1, 4 * D)],
        )

    def joint():
        h.q, h.kv, h.w_in, h.attended, h.probs = order(
            joint_kernel, [h.first, h.bias, *w_in.parts],
            [low(rows, D), low(rows + 2 * RIM, 2 * D), low(D, 3 * D),
             low(rows, D), low(rows, HEADS * WINDOW)],
            mib=14,
        )

    def mlp():
        h.mixed, h.second, h.swished, h.slope, h.w_out, h.w_exp = order(
            mlp_forward_kernel, [h.attended, h.states, h.mod, *w_exp.parts],
            [full(rows, D), low(rows, D), low(rows, hidden), low(rows, hidden),
             low(D, D), low(D, hidden)],
            mib=12,
        )

    def con_grad():
        slots = low(4, chips, own, D)
        g_con.begin(*order(
            contract_grads_kernel, [h.swished, h.cot], [slots, slots],
            [pltpu.VMEM((hidden, D), F32)], mib=12,
        ))

    def back_low():
        h.up_low, h.second_low, h.w_con = order(
            mlp_backward_low_kernel, [h.slope, h.cot, h.w_exp, *w_con.parts],
            [low(split, hidden), full(split, D), low(hidden, D)], mib=10,
        )

    def back_high():
        h.up_high, h.second_high = order(
            mlp_backward_high_kernel, [h.slope, h.cot, h.w_exp, h.w_con],
            [low(split, hidden), full(split, D)], mib=10,
        )

    def final():
        h.final, h.input_grad = order(
            final_kernel, [h.mixed, h.swished, h.w_con, h.input_grad],
            [jax.ShapeDtypeStruct((rows, D), BF16), jax.ShapeDtypeStruct((rows, D), F32)],
            [pltpu.VMEM((rows, D), BF16), pltpu.SemaphoreType.DMA((1 + rows // PIECE,))],
            mib=8, whole=(0, 1),
        )

    def norm():
        h.d_mixed, h.d_low, h.d_attended, h.sums_two = order(
            norm_backward_kernel,
            [h.mixed, h.second_low, h.second_high, h.cot, h.mod, h.w_out],
            [full(rows, D), low(rows, D), low(rows, D), full(8, D)], mib=8,
        )

    def exp_grad():
        slots = low(4, chips, own, hidden // 4 + D // 4)
        g_exp.begin(*order(
            expand_grads_kernel, [h.second, h.up_low, h.up_high, h.attended, h.d_low],
            [slots, slots], [pltpu.VMEM((D, hidden), F32), pltpu.VMEM((D, D), F32)], mib=12,
        ))

    def attn():
        h.dq, h.dkv, core, chip = order(
            attend_back_kernel, [h.q, h.kv, h.probs, h.d_attended],
            [low(rows, D), low(rows + 2 * RIM, 2 * D), low(RIM, 2 * D), low(RIM, 2 * D)],
            mib=12,
        )
        h.edges = [net.cores(core), net.beside(chip)]

    def edge_take():
        h.edges = [w_in.take(edge) for edge in h.edges]

    def in_grad():
        slots = low(4, chips, *slab)
        g_in.begin(*order(
            in_grads_kernel, [h.first, h.dq, h.dkv], [slots, slots],
            [pltpu.VMEM((D, 3 * D), F32)], mib=8,
        ))

    def input_step():
        kernel = functools.partial(input_grad_kernel, net.noise, net.nodes)
        h.input_grad, rider = order(
            kernel,
            [h.dq, h.dkv, *h.edges, h.states, h.d_mixed, h.mod, h.w_in, h.sums_two, cond],
            [full(rows, D), low(riders, *rider_slab)],
            [pltpu.VMEM((rows + 2 * RIM, 2 * D), BF16), pltpu.VMEM((8, 5 * D), F32),
             pltpu.VMEM((riders, *rider_slab), F32)],
            mib=10, free=(9,),
        )
        h.rider = (rider, net.cores(rider))

    def in_chip():
        g_in.chip(1, h.rider)

    def con_up():
        h.contract_new = update_call(
            order, g_con, [(slice(None), True)],
            [contract_weight, contract_first, contract_second],
        )

    def exp_up():
        cut = hidden // 4
        h.expand_new = update_call(
            order, g_exp, [(slice(None, cut), False), (slice(cut, None), False)],
            [expand_weight, expand_first, expand_second,
             outward_weight, outward_first, outward_second],
        )

    def in_up():
        h.inward_new = update_call(
            order, g_in, [(slice(None), False)], [inward_weight, inward_first, inward_second],
            (modulate_weight, modulate_first, modulate_second),
            functools.partial(modulate_grads, net.noise, own),
        )

    plan = (
        (w_in.pack, 0), (load_more, 10), (load, 0), (w_exp.pack, 1), (mod, 200), (w_in.swap, 100),
        (w_con.pack, 20), (mod_core, 0), (w_in.near, 0), (w_exp.swap, 10), (mod_near, 20),
        (counts, 0), (mod_far, 0), (w_con.swap, 30), (w_exp.near, 0), (w_in.core, 0),
        (w_in.far, 20), (w_con.near, 30), (first, 120), (joint, 20), (w_exp.core, 0),
        (w_exp.far, 200), (mlp, 200), (w_con.core, 1), (w_con.far, 0), (con_grad, 0),
        (back_low, 80), (g_con.one, 50), (back_high, 0), (norm, 120), (attn, 10), (exp_grad, 30),
        (g_con.two, 30), (in_grad, 80), (g_exp.one, 1), (g_con.chip, 200), (g_in.one, 0),
        (g_con.chips, 0), (edge_take, 0), (g_exp.two, 10), (input_step, 20), (g_con.three, 30),
        (g_in.two, 80), (g_exp.chip, 0), (final, 0), (in_chip, 120), (g_exp.chips, 5),
        (g_in.chips, 0), (g_con.four, 0), (g_exp.three, 120), (g_in.three, 30), (g_exp.four, 5),
        (g_in.four, 0), (con_up, 10), (exp_up, 0), (in_up, 100),
    )
    for step, tenths in plan:
        order.tenths = tenths
        step()

    return (
        h.final[None], h.input_grad[None], *h.inward_new[:3], *h.expand_new[3:],
        *h.expand_new[:3], *h.contract_new, *h.inward_new[3:],
    )


def solution(mesh):
    grid = P(NOISE, NODES, None)
    shard = P(NODES, None)
    return jax.shard_map(
        per_device,
        mesh=mesh,
        in_specs=(grid, P(NOISE), grid, grid) + (shard,) * 15,
        out_specs=(grid, grid) + (shard,) * 15,
        check_vma=False,
    )
```

```python
import functools
import math

import jax
import jax.numpy as jnp
from jax import lax
from jax.experimental import pallas as pl
from jax.experimental.pallas import tpu as pltpu
from jax.sharding import PartitionSpec as P

D = 512
HEADS = 4
NEIGH = 16
RIM = 64
STEP = 10
HEAD_DIM = 128
BLOCK = 128
WINDOW = BLOCK + 2 * RIM
GROUP = 4
HALF = 512
CHUNK = 1024
PIECE = 256
LANES = 128
RIDER_ROWS = 8
NOISE, NODES = AXES = ("noise", "nodes")
BF16 = jnp.bfloat16
F32 = jnp.float32
NONE = -1e30
SMALL = 1.0 / math.sqrt(HEAD_DIM)

VMEM = pl.BlockSpec(memory_space=pltpu.VMEM)
HBM = pl.BlockSpec(memory_space=pltpu.HBM)


def dot(left, right, left_dim, right_dim):
    return lax.dot_general(
        left, right, (((left_dim,), (right_dim,)), ((), ())), preferred_element_type=F32
    )


def fourier(sigma):
    half = D // 2
    counter = jnp.arange(half).astype(F32)
    freqs = jnp.exp(counter * (math.log(64.0) / (half - 1)))
    phase = jnp.log(sigma)[:, None] * freqs[None, :]
    return jnp.concatenate([jnp.sin(phase), jnp.cos(phase)], axis=-1)


def normalize_parts(values):
    center = values - jnp.mean(values, axis=-1, keepdims=True)
    inverse = lax.rsqrt(jnp.mean(center * center, axis=-1, keepdims=True) + 1e-06)
    return (center * inverse, inverse)


def norm_back(normed, inverse, grads):
    average = jnp.mean(grads, axis=-1, keepdims=True)
    along = jnp.mean(grads * normed, axis=-1, keepdims=True)
    return inverse * (grads - average - normed * along)


def adamw(weight, first, second, grads):
    moment = 0.5 * first + 0.5 * grads
    square = 0.75 * second + 0.25 * grads * grads
    level = square * (1.0 / (1.0 - 0.75**STEP))
    root = level * lax.rsqrt(level)
    ratio = moment * (1.0 / (1.0 - 0.5**STEP)) / (root + 1e-08)
    return (moment, square, weight - 0.02 * (ratio + 0.1 * weight))


def pinned(shape, dtype):
    return pltpu.VMEM(tuple(shape), dtype)


class Order:
    def __init__(self):
        self.tick = None
        self.tenths = 0

    def __call__(self, kernel, ins, outs, scratch=(), mib=8, free=(), loose=(), whole=()):
        before = [] if self.tick is None else [self.tick]

        def body(*refs):
            first = len(ins) + len(before)
            last = first + len(outs)
            kernel(*refs[: len(ins)], *refs[first:last], *refs[last + 1 :])
            refs[last][...] = jnp.zeros((8, LANES), F32)

        keep = lambda array: pltpu.with_memory_space_constraint(array, pltpu.VMEM)
        stay = lambda array: pltpu.with_memory_space_constraint(array, pltpu.HBM)
        arrays = [
            a if k in free else stay(a) if k in loose else keep(a) for k, a in enumerate(ins)
        ]
        specs = [HBM if k in loose else VMEM for k in range(len(ins))]
        named = kernel.func if isinstance(kernel, functools.partial) else kernel
        *results, self.tick = pl.pallas_call(
            body,
            in_specs=specs + [VMEM] * len(before),
            out_specs=[HBM if k in whole else VMEM for k in range(len(outs))] + [VMEM],
            out_shape=list(outs) + [pinned((8, LANES), F32)],
            scratch_shapes=list(scratch),
            compiler_params=pltpu.CompilerParams(vmem_limit_bytes=mib * 2**20),
            cost_estimate=pl.CostEstimate(
                flops=self.tenths * 10**8, bytes_accessed=1, transcendentals=0
            ),
            name=named.__name__,
        )(*arrays, *map(keep, before))
        return results


class Place:
    def __init__(self):
        self.device = lax.axis_index(NODES)
        self.n = lax.axis_index(NOISE)
        self.core = lax.rem(self.device, 2)
        self.chip = lax.div(self.device, 2)
        swapped = lax.rem(self.n, 2) * 2 + lax.div(self.n, 2)
        self.role = jnp.where(self.core == 0, self.n, swapped)
        self.other = jnp.where(self.core == 0, swapped, self.n)


def load_kernel(*refs):
    count, sems = len(refs) // 2, refs[-1]
    copies = [
        pltpu.make_async_copy(refs[k], refs[count + k], sems.at[k]) for k in range(count)
    ]
    for copy in copies:
        copy.start()
    for copy in copies:
        copy.wait()


def load_more_kernel(*refs):
    load_kernel(*refs)


def count_kernel(total, near_ref, bias_ref):
    rows = bias_ref.shape[0]
    base = Place().device * rows - RIM
    shape = (WINDOW, BLOCK)
    window = lax.broadcasted_iota(jnp.int32, shape, 0).astype(jnp.int16)
    one, zero = jnp.ones(shape, BF16), jnp.zeros(shape, BF16)
    for start in range(0, rows, BLOCK):
        place = near_ref[:, start : start + BLOCK] - (base + start)
        place = jnp.where(place < 0, place + total, place)
        place = jnp.where(place >= total, place - total, place).astype(jnp.int16)
        count = zero
        for k in range(NEIGH):
            here = jnp.broadcast_to(place[k : k + 1, :], shape) == window
            count = count + jnp.where(here, one, zero)
        count = count.astype(F32)
        bias = jnp.where(count > 0.0, jnp.log(count), NONE)
        bias_ref[start : start + BLOCK, :] = bias.T


def pack_inward_kernel(inward_ref, halves_ref):
    wide = halves_ref.shape[2]
    for half in range(2):
        halves_ref[half] = inward_ref[:, half * wide : (half + 1) * wide].astype(BF16)


def pack_expand_kernel(expand_ref, outward_ref, halves_ref):
    wide = expand_ref.shape[1] // 2
    for half in range(2):
        left = expand_ref[:, half * wide : (half + 1) * wide].astype(BF16)
        right = outward_ref[:, half * D // 2 : (half + 1) * D // 2].astype(BF16)
        halves_ref[half, :, :wide] = left
        halves_ref[half, :, wide:] = right


def pack_contract_kernel(contract_ref, halves_ref):
    own = halves_ref.shape[1]
    for k in range(4):
        rows = contract_ref[k * own : (k + 1) * own, :].astype(BF16)
        halves_ref[k // 2, :, k % 2 * D : (k % 2 + 1) * D] = rows


def near_kernel(halves_ref, fetched_ref, got_ref, near_ref, every_ref):
    place = Place()
    mine = jnp.where(place.core == 0, lax.rem(place.n, 2), 1 - lax.div(place.n, 2))
    for half in range(2):
        near_ref[2 * mine + half] = fetched_ref[half]
        near_ref[2 * (1 - mine) + half] = got_ref[half]
        every_ref[4 + half] = halves_ref[half]
    for k in range(4):
        every_ref[k] = near_ref[k]


def take_kernel(value_ref, out_ref):
    out_ref[...] = value_ref[...]


def edges_kernel(states_ref, core_ref, chip_ref):
    core = Place().core
    rows = states_ref.shape[0]
    head, tail = states_ref[:RIM, :], states_ref[rows - RIM :, :]

    @pl.when(core == 0)
    def _():
        core_ref[...] = tail
        chip_ref[...] = head

    @pl.when(core == 1)
    def _():
        core_ref[...] = head
        chip_ref[...] = tail


def modulation_kernel(cond_ref, weight_ref, out_ref):
    own = weight_ref.shape[0]
    first = Place().device * own
    rows = lax.broadcasted_iota(jnp.int32, (D, own), 0)
    cols = lax.broadcasted_iota(jnp.int32, (D, own), 1)
    chosen = jnp.where(rows == cols + first, 1.0, 0.0).astype(BF16)
    mine = dot(cond_ref[...], chosen, 1, 0).astype(BF16)
    out_ref[...] = dot(mine, weight_ref[...].astype(BF16), 1, 0)


def encode(row_ref, target_ref):
    for k in range(4):
        value = row_ref[0:1, k * D : (k + 1) * D]
        high = value.astype(BF16)
        target_ref[RIM + k : RIM + k + 1, :] = high.astype(F32)
        target_ref[RIM + 4 + k : RIM + 5 + k, :] = value - high.astype(F32)


def decode(source_ref):
    rows = source_ref[RIM : RIM + 16, :].astype(F32)
    return jnp.concatenate([rows[k : k + 1] + rows[4 + k : 5 + k] for k in range(4)], axis=1)


def open_kernel(cond_ref, weight_ref, states_ref, part_ref, core_ref, chip_ref, wide_ref):
    modulation_kernel(cond_ref, weight_ref, part_ref)
    wide_ref[RIM:, :] = jnp.zeros((16, D), F32)
    encode(part_ref, wide_ref)
    core_ref[RIM:, :] = wide_ref[RIM:, :].astype(BF16)
    edges_kernel(states_ref, core_ref.at[:RIM], chip_ref)


def open_core_kernel(part_ref, got_ref, chip_ref, sum_ref, edge_ref, send_ref, wide_ref):
    sum_ref[...] = part_ref[...] + decode(got_ref)
    edge_ref[...] = got_ref[:RIM, :]
    send_ref[:RIM, :] = chip_ref[...]
    wide_ref[RIM:, :] = jnp.zeros((16, D), F32)
    encode(sum_ref, wide_ref)
    send_ref[RIM:, :] = wide_ref[RIM:, :].astype(BF16)


def open_chip_kernel(sum_ref, got_ref, near_ref, edge_ref, out_ref):
    near = decode(got_ref)
    near_ref[...] = near
    edge_ref[...] = got_ref[:RIM, :]
    out_ref[...] = sum_ref[...] + near


def open_far_kernel(sum_ref, got_ref, out_ref, send_ref):
    out_ref[...] = sum_ref[...] + got_ref[...]
    send_ref[...] = got_ref[...]


def sum_kernel(left_ref, right_ref, out_ref):
    out_ref[...] = left_ref[...] + right_ref[...]


def first_kernel(states_ref, core_ref, chip_ref, left_ref, right_ref, first_ref, mod_ref):
    core = Place().core
    mod_ref[...] = left_ref[...] + right_ref[...]
    scale = 1.0 + mod_ref[0:1, :D]
    shift = mod_ref[0:1, D : 2 * D]
    rows = states_ref.shape[0]

    def put(at, values):
        normed, _ = normalize_parts(values.astype(F32))
        first_ref[at : at + values.shape[0], :] = (normed * scale + shift).astype(BF16)

    put(RIM, states_ref[...])

    @pl.when(core == 0)
    def _():
        put(0, chip_ref[...])
        put(RIM + rows, core_ref[...])

    @pl.when(core == 1)
    def _():
        put(0, core_ref[...])
        put(RIM + rows, chip_ref[...])


def heads(array_ref, start, rows, base):
    return [
        array_ref[start : start + rows, base + h * HEAD_DIM : base + (h + 1) * HEAD_DIM]
        for h in range(HEADS)
    ]


def joint_kernel(first_ref, bias_ref, *refs):
    parts = refs[:-5]
    q_ref, kv_ref, w_ref, out_ref, probs_ref = refs[-5:]
    rows = q_ref.shape[0]
    deep, width = parts[0].shape[1:]

    def put(ref, block, half):
        span = pl.ds(pl.multiple_of(block * deep, deep), deep)
        w_ref[span, half * width : (half + 1) * width] = ref[...]

    assemble(parts, put)
    q_ref[...] = dot(first_ref[RIM : RIM + rows, :], w_ref[:, :D], 1, 0).astype(BF16)
    kv_ref[...] = dot(first_ref[...], w_ref[:, D:], 1, 0).astype(BF16)
    for group in range(0, rows, GROUP * BLOCK):
        starts = range(group, min(group + GROUP * BLOCK, rows), BLOCK)
        jobs = [(s, h) for s in starts for h in range(HEADS)]
        queries = [x for s in starts for x in heads(q_ref, s, BLOCK, 0)]
        keys = [x for s in starts for x in heads(kv_ref, s, WINDOW, 0)]
        values = [x for s in starts for x in heads(kv_ref, s, WINDOW, D)]
        scores = [dot(q, k, 1, 1) for q, k in zip(queries, keys)]
        scores = [x * SMALL + bias_ref[s : s + BLOCK, :] for x, (s, _) in zip(scores, jobs)]
        tops = [jnp.max(x, axis=1, keepdims=True) for x in scores]
        expos = [jnp.exp(x - t) for x, t in zip(scores, tops)]
        sums = [jnp.sum(x, axis=1, keepdims=True) for x in expos]
        probs = [(x * (1.0 / t)).astype(BF16) for x, t in zip(expos, sums)]
        outs = [dot(p, v, 1, 0).astype(BF16) for p, v in zip(probs, values)]
        for p, o, (s, h) in zip(probs, outs, jobs):
            probs_ref[s : s + BLOCK, h * WINDOW : (h + 1) * WINDOW] = p
            out_ref[s : s + BLOCK, h * HEAD_DIM : (h + 1) * HEAD_DIM] = o


def attend_back_kernel(
    q_ref, kv_ref, probs_ref, grad_ref, dq_ref, dkv_ref, core_ref, chip_ref
):
    rows = q_ref.shape[0]
    carry = [jnp.zeros((BLOCK, HEAD_DIM), F32)] * (2 * HEADS)
    for group in range(0, rows, GROUP * BLOCK):
        starts = range(group, min(group + GROUP * BLOCK, rows), BLOCK)
        jobs = [(s, h) for s in starts for h in range(HEADS)]
        queries = [x for s in starts for x in heads(q_ref, s, BLOCK, 0)]
        grads = [x for s in starts for x in heads(grad_ref, s, BLOCK, 0)]
        keys = [x for s in starts for x in heads(kv_ref, s, WINDOW, 0)]
        values = [x for s in starts for x in heads(kv_ref, s, WINDOW, D)]
        probs = [probs_ref[s : s + BLOCK, h * WINDOW : (h + 1) * WINDOW] for s, h in jobs]
        d_probs = [dot(g, v, 1, 1) for g, v in zip(grads, values)]
        weighted = [p.astype(F32) * d for p, d in zip(probs, d_probs)]
        totals = [jnp.sum(w, axis=1, keepdims=True) for w in weighted]
        d_scores = [
            ((w - p.astype(F32) * t) * SMALL).astype(BF16)
            for w, p, t in zip(weighted, probs, totals)
        ]
        d_queries = [dot(d, k, 1, 0).astype(BF16) for d, k in zip(d_scores, keys)]
        d_keys = [dot(d, q, 0, 0) for d, q in zip(d_scores, queries)]
        d_values = [dot(p, g, 0, 0) for p, g in zip(probs, grads)]
        for x, (s, h) in zip(d_queries, jobs):
            dq_ref[s : s + BLOCK, h * HEAD_DIM : (h + 1) * HEAD_DIM] = x
        for column in range(2 * HEADS):
            parts = (d_keys if column < HEADS else d_values)[column % HEADS :: HEADS]
            cols = slice(column * HEAD_DIM, (column + 1) * HEAD_DIM)
            for s, part in zip(starts, parts):
                dkv_ref[s : s + BLOCK, cols] = (carry[column] + part[:BLOCK]).astype(BF16)
                carry[column] = part[BLOCK:]
    for column, part in enumerate(carry):
        cols = slice(column * HEAD_DIM, (column + 1) * HEAD_DIM)
        dkv_ref[rows : rows + BLOCK, cols] = part.astype(BF16)
    core = Place().core
    low, high = dkv_ref[:RIM, :], dkv_ref[rows + RIM :, :]

    @pl.when(core == 0)
    def _():
        core_ref[...] = high
        chip_ref[...] = low

    @pl.when(core == 1)
    def _():
        core_ref[...] = low
        chip_ref[...] = high


def assemble(parts, put):
    if len(parts) == 1:
        for half in range(2):
            put(parts[0].at[half], 0, half)
        return
    place = Place()
    for p in range(2):
        near, far = parts[2 * p : 2 * p + 2]
        owner = place.core if p == 0 else 1 - place.core

        def put_all(next_one, second, third):
            for half in range(2):
                for s, ref in enumerate((near.at[4 + half], next_one, second, third)):
                    part = ref if s == 0 else ref[0].at[ref[1] + half]
                    put(part, lax.rem(place.chip + s, 4) * 2 + owner, half)

        for core, bit in ((0, lax.div(place.n, 2)), (1, lax.rem(place.n, 2))):
            for turn in range(2):
                low, high = (near, far) if turn == 0 else (far, near)

                @pl.when(jnp.logical_and(owner == core, bit == turn))
                def _():
                    put_all((low, 2) if core == 0 else (high, 0), (low, 0), (high, 2))


def copy_rows(source, target, rows, sem):
    copy = pltpu.make_async_copy(source.at[rows], target.at[rows], sem)
    copy.start()
    return copy


def write_slots(targets, block_of):
    place = Place()
    owners = (place.core, 1 - place.core)
    for target, owner, role in zip(targets, owners, (place.role, place.other)):
        for slot in range(4):
            quarter = role ^ ((slot // 2) + 2 * (slot % 2))
            for s in range(target.shape[1]):
                target[slot, s] = block_of((place.chip ^ s) * 2 + owner, quarter).astype(BF16)


def mlp_forward_kernel(attended_ref, states_ref, mod_ref, *refs):
    parts = refs[:-6]
    mixed_ref, second_ref, swished_ref, slope_ref, w_out_ref, w_exp_ref = refs[-6:]
    hidden = w_exp_ref.shape[1]
    deep = parts[0].shape[1]

    def put(ref, block, half):
        rows = pl.ds(pl.multiple_of(block * deep, deep), deep)
        wide, thin = hidden // 2, D // 2
        w_exp_ref[rows, half * wide : (half + 1) * wide] = ref[:, :wide]
        w_out_ref[rows, half * thin : (half + 1) * thin] = ref[:, wide:]

    assemble(parts, put)
    scale = 1.0 + mod_ref[0:1, 2 * D : 3 * D]
    shift = mod_ref[0:1, 3 * D :]
    for start in range(0, states_ref.shape[0], HALF):
        rows = slice(start, start + HALF)
        mixed = states_ref[rows].astype(F32) + dot(attended_ref[rows], w_out_ref[...], 1, 0)
        mixed_ref[rows] = mixed
        normed, _ = normalize_parts(mixed)
        second_in = (normed * scale + shift).astype(BF16)
        second_ref[rows] = second_in
        for at in range(0, hidden, CHUNK):
            cols = slice(at, at + CHUNK)
            up = dot(second_in, w_exp_ref[:, cols], 1, 0)
            gate = 0.5 + 0.5 * jnp.tanh(0.5 * up)
            product = up * gate
            swished_ref[rows, cols] = product.astype(BF16)
            slope_ref[rows, cols] = (gate + product * (1.0 - gate)).astype(BF16)

def contract_grads_kernel(swished_ref, cot_ref, keep_ref, send_ref, grad_ref):
    own = keep_ref.shape[2]
    grad_ref[...] = dot(swished_ref[...], cot_ref[...], 0, 0)
    write_slots(
        (keep_ref, send_ref),
        lambda block, quarter: grad_ref[
            pl.ds(pl.multiple_of((block * 4 + quarter) * own, own), own), :
        ],
    )


def mlp_backward(rows, slope_ref, cot_ref, w_exp_ref, w_con_ref, d_up_ref, d_second_ref):
    hidden = w_exp_ref.shape[1]
    cot = cot_ref[rows]
    d_second = jnp.zeros(d_second_ref.shape, F32)
    for at in range(0, hidden, CHUNK):
        cols = slice(at, at + CHUNK)
        d_swished = dot(cot, w_con_ref[cols, :], 1, 1)
        d_up = (d_swished * slope_ref[rows, cols].astype(F32)).astype(BF16)
        d_up_ref[:, cols] = d_up
        d_second = d_second + dot(d_up, w_exp_ref[:, cols], 1, 1)
    d_second_ref[...] = d_second


def mlp_backward_low_kernel(slope_ref, cot_ref, w_exp_ref, *refs):
    parts = refs[:-3]
    d_up_ref, d_second_ref, w_con_ref = refs[-3:]
    deep = parts[0].shape[1]

    def put(ref, block, half):
        for k in range(2):
            start = pl.multiple_of((block * 4 + half * 2 + k) * deep, deep)
            w_con_ref[pl.ds(start, deep), :] = ref[:, k * D : (k + 1) * D]

    assemble(parts, put)
    rows = slice(0, d_up_ref.shape[0])
    mlp_backward(rows, slope_ref, cot_ref, w_exp_ref, w_con_ref, d_up_ref, d_second_ref)


def mlp_backward_high_kernel(slope_ref, cot_ref, w_exp_ref, w_con_ref, d_up_ref, d_second_ref):
    half = d_up_ref.shape[0]
    rows = slice(half, 2 * half)
    mlp_backward(rows, slope_ref, cot_ref, w_exp_ref, w_con_ref, d_up_ref, d_second_ref)


def final_kernel(
    mixed_ref, swished_ref, w_con_ref, grad_ref, final_ref, grad_out_ref, done_ref, sems
):
    sends = [pltpu.make_async_copy(grad_ref, grad_out_ref, sems.at[0])]
    sends[0].start()
    for start in range(0, mixed_ref.shape[0], PIECE):
        rows = slice(start, start + PIECE)
        final = mixed_ref[rows] + dot(swished_ref[rows], w_con_ref[...], 1, 0)
        done_ref[rows] = final.astype(BF16)
        sends.append(copy_rows(done_ref, final_ref, rows, sems.at[len(sends)]))
    for send in sends:
        send.wait()


def norm_backward_kernel(
    mixed_ref, low_ref, high_ref, cot_ref, mod_ref, w_out_ref,
    d_mixed_ref, d_low_ref, d_att_ref, sums_ref,
):
    scale = 1.0 + mod_ref[0:1, 2 * D : 3 * D]
    sums_ref[...] = jnp.zeros_like(sums_ref)
    half = low_ref.shape[0]
    for k, d_second_ref in enumerate((low_ref, high_ref)):
        rows = slice(k * half, (k + 1) * half)
        normed, inverse = normalize_parts(mixed_ref[rows])
        d_second = d_second_ref[...]
        sums_ref[0:1, :] += jnp.sum(d_second * normed, axis=0, keepdims=True)
        sums_ref[1:2, :] += jnp.sum(d_second, axis=0, keepdims=True)
        d_mixed = cot_ref[rows].astype(F32) + norm_back(normed, inverse, d_second * scale)
        d_mixed_ref[rows] = d_mixed
        d_low_ref[rows] = d_mixed.astype(BF16)
        d_att_ref[rows] = dot(d_mixed.astype(BF16), w_out_ref[...], 1, 1).astype(BF16)


def expand_grads_kernel(
    second_ref, low_ref, high_ref, attended_ref, d_low_ref, keep_ref, send_ref, exp_ref, out_ref
):
    own, unit = keep_ref.shape[2:]
    wide = unit - D // 4
    half = low_ref.shape[0]
    for at in range(0, exp_ref.shape[1], D):
        cols = slice(at, at + D)
        exp_ref[:, cols] = dot(second_ref[:half, :], low_ref[:, cols], 0, 0) + dot(
            second_ref[half:, :], high_ref[:, cols], 0, 0
        )
    out_ref[...] = dot(attended_ref[...], d_low_ref[...], 0, 0)

    def block_of(block, quarter):
        rows = pl.ds(pl.multiple_of(block * own, own), own)
        first = exp_ref[rows, pl.ds(pl.multiple_of(quarter * wide, wide), wide)]
        second = out_ref[rows, pl.ds(pl.multiple_of(quarter * (D // 4), D // 4), D // 4)]
        return jnp.concatenate([first, second], axis=1)

    write_slots((keep_ref, send_ref), block_of)


def in_grads_kernel(first_ref, dq_ref, dkv_ref, keep_ref, send_ref, in_ref):
    own, unit = keep_ref.shape[2:]
    rows = dq_ref.shape[0]
    in_ref[:, :D] = dot(first_ref[RIM : RIM + rows, :], dq_ref[...], 0, 0)
    in_ref[:, D:] = dot(first_ref[...], dkv_ref[...], 0, 0)
    write_slots(
        (keep_ref, send_ref),
        lambda block, quarter: in_ref[
            pl.ds(pl.multiple_of(block * own, own), own),
            pl.ds(pl.multiple_of(quarter * unit, unit), unit),
        ],
    )


def rider_spots(copy, own):
    for group in range(5 * D // LANES):
        row = copy * RIDER_ROWS + group // 3
        at = (group % 3) * LANES
        yield group, row // own, row % own, slice(at, at + LANES)


def input_grad_kernel(
    copies, nodes, dq_ref, dkv_ref, core_ref, chip_ref, states_ref, d_mixed_ref, mod_ref, w_in_ref,
    sums_two_ref, cond_ref, grad_ref, rider_ref, wide_ref, row_ref, slab_ref,
):
    place = Place()
    rows = states_ref.shape[0]
    wide_ref[...] = dkv_ref[...]

    def join(at, ref):
        part = slice(at, at + RIM)
        wide_ref[part, :] = (wide_ref[part, :].astype(F32) + ref[...].astype(F32)).astype(BF16)

    @pl.when(place.core == 0)
    def _():
        join(RIM, chip_ref)
        join(rows, core_ref)

    @pl.when(place.core == 1)
    def _():
        join(RIM, core_ref)
        join(rows, chip_ref)

    scale = 1.0 + mod_ref[0:1, :D]
    d_scale = jnp.zeros((1, D), F32)
    d_shift = jnp.zeros((1, D), F32)
    for start in range(0, rows, HALF):
        part = slice(start, start + HALF)
        normed, inverse = normalize_parts(states_ref[part].astype(F32))
        d_first = dot(dq_ref[part], w_in_ref[:, :D], 1, 1) + dot(
            wide_ref[RIM + start : RIM + start + HALF, :], w_in_ref[:, D:], 1, 1
        )
        d_scale = d_scale + jnp.sum(d_first * normed, axis=0, keepdims=True)
        d_shift = d_shift + jnp.sum(d_first, axis=0, keepdims=True)
        grad_ref[part] = d_mixed_ref[part] + norm_back(normed, inverse, d_first * scale)
    row_ref[0:1, :D] = d_scale
    row_ref[0:1, D : 2 * D] = d_shift
    row_ref[0:1, 2 * D : 3 * D] = sums_two_ref[0:1, :]
    row_ref[0:1, 3 * D : 4 * D] = sums_two_ref[1:2, :]
    row_ref[0:1, 4 * D :] = cond_ref[0:1, :].astype(F32) * (1.0 / nodes)
    slab_ref[...] = jnp.zeros_like(slab_ref)
    for copy in range(copies):
        mine = jnp.where(place.n == copy, 1.0, 0.0)
        for group, slab, row, cols in rider_spots(copy, slab_ref.shape[1]):
            values = row_ref[0:1, group * LANES : (group + 1) * LANES]
            slab_ref[slab, row : row + 1, cols] = values * mine
    rider_ref[...] = slab_ref[...].astype(BF16)


def modulate_grads(copies, own, riders, row_ref, slab_ref):
    slab_ref[...] = riders
    row_ref[...] = jnp.zeros_like(row_ref)
    for copy in range(copies):
        for group, slab, row, cols in rider_spots(copy, slab_ref.shape[1]):
            row_ref[copy : copy + 1, group * LANES : (group + 1) * LANES] = slab_ref[
                slab, row : row + 1, cols
            ]
    everyone = row_ref[...].astype(BF16)
    chosen = lax.broadcasted_iota(jnp.int32, (D, own), 0) == (
        lax.broadcasted_iota(jnp.int32, (D, own), 1) + Place().device * own
    )
    conds = dot(everyone[:, 4 * D :], jnp.where(chosen, 1.0, 0.0).astype(BF16), 1, 0)
    return dot(conds.astype(BF16), everyone[:, : 4 * D], 0, 0)


def update_quarters(spots, cut, pair_ref, got_ref, ins, outs, sems):
    role = Place().role
    sends = []
    for k, (cols, by_rows) in enumerate(spots):
        for slot in range(4):
            quarter = role ^ ((slot // 2) + 2 * (slot % 2))
            source = pair_ref if slot < 2 else got_ref
            for part in range(cut):
                grads = source[slot % 2 * cut + part, :, cols].astype(F32)
                height, width = grads.shape
                if by_rows:
                    at = (pl.ds(pl.multiple_of(quarter * height, height), height), slice(None))
                else:
                    at = (
                        slice(part * height, (part + 1) * height),
                        pl.ds(pl.multiple_of(quarter * width, width), width),
                    )
                values = adamw(*(ref[at] for ref in ins[3 * k : 3 * k + 3]), grads)
                for j, value in enumerate(values, 3 * k):
                    scratch, target = outs[j]
                    scratch[at] = value
                    sends.append(pltpu.make_async_copy(
                        scratch.at[at], target.at[at], sems.at[j, slot * cut + part]
                    ))
                    sends[-1].start()
    return sends


class Net:
    def __init__(self):
        self.noise = lax.axis_size(NOISE)
        self.nodes = lax.axis_size(NODES)
        self.chips = self.nodes // 2
        self.quick = self.chips == 4

    def permute(self, value, move):
        pairs = []
        for n in range(self.noise):
            for z in range(self.chips):
                for c in range(2):
                    n2, z2, c2 = move(n, z, c)
                    source = (n * self.chips + z) * 2 + c
                    target = (n2 * self.chips + z2 % self.chips) * 2 + c2
                    pairs.append((source, target))
        return lax.ppermute(value, AXES, pairs)

    def role_of(self, n, c):
        return n if c == 0 else (n % 2) * 2 + n // 2

    def swap(self, value, bit):
        return self.permute(value, lambda n, z, c: (n ^ (bit if c == 0 else 3 - bit), z, c))

    def cores(self, value):
        return self.permute(value, lambda n, z, c: (n, z, 1 - c))

    def beside(self, value):
        return self.permute(value, lambda n, z, c: (n, z + 2 * c - 1, 1 - c))

    def across(self, value, step):
        return self.permute(value, lambda n, z, c: (n, z ^ step, c))

    def fetch(self, halves):
        back = (2, 3, 0, 1)
        return self.permute(halves, lambda n, z, c: (n, z + back[n ^ (2 * c)], c))


class Gathering:
    def __init__(self, net, order, kernel, arrays, half, stacked=False):
        self.net, self.order, self.kernel, self.arrays = net, order, kernel, arrays
        self.half, self.stacked = half, stacked

    def shape(self, count):
        return pinned((count, *self.half), BF16)

    def take(self, value):
        return self.order(take_kernel, [value], [pinned(value.shape, value.dtype)])[0]

    def pack(self):
        arrays, free = self.arrays()
        self.halves, = self.order(self.kernel, arrays, [self.shape(2)], free=free)
        if self.net.quick:
            self.got = self.net.fetch(self.halves)
            return
        every = lax.all_gather(self.halves, NODES, axis=1, tiled=True)
        if self.stacked:
            own = self.half[0]
            every = every.reshape(2, -1, own, 2, D).swapaxes(2, 3).swapaxes(0, 1)
            every = every.reshape(2, 2, -1, D).swapaxes(1, 2).reshape(2, -1, 2 * D)
        self.parts = [every]

    def swap(self):
        if not self.net.quick:
            return
        self.fetched = self.take(self.got)
        self.got = self.net.swap(self.fetched, 1)

    def near(self):
        if not self.net.quick:
            return
        near, every = self.order(
            near_kernel, [self.halves, self.fetched, self.got], [self.shape(4), self.shape(6)]
        )
        self.parts = [every, self.net.swap(near, 2), self.net.cores(every), None]

    def core(self):
        if not self.net.quick:
            return
        self.parts[2] = self.take(self.parts[2])

    def far(self):
        if not self.net.quick:
            return
        self.parts[1] = self.take(self.parts[1])
        self.parts[3] = self.net.cores(self.parts[1])


class Reduction:
    def __init__(self, net, order):
        self.net, self.order = net, order
        self.riders = 0
        self.cut = 1

    def begin(self, keep, send):
        self.unit = keep.shape[2:]
        self.held, self.got = keep, self.net.cores(send)

    def shape(self, *lead):
        return pinned((*lead, *self.unit), BF16)

    def one(self):
        def sum_one(held_ref, got_ref, away_ref, out_ref):
            away_ref[...] = held_ref[2:] + got_ref[2:]
            out_ref[...] = held_ref[:2] + got_ref[:2]

        outs = [self.shape(2, self.net.chips)] * 2
        away, self.held = self.order(sum_one, [self.held, self.got], outs)
        self.got = self.net.swap(away, 1)

    def two(self):
        def sum_two(held_ref, got_ref, away_ref, out_ref):
            away_ref[...] = held_ref[1] + got_ref[1]
            out_ref[...] = held_ref[0] + got_ref[0]

        outs = [self.shape(self.net.chips)] * 2
        away, self.held = self.order(sum_two, [self.held, self.got], outs)
        self.got = self.net.swap(away, 2)

    def chip(self, step=1, rider=()):
        own = self.unit[0]
        if rider:
            self.riders = rider[0].shape[0]
            self.cut = own // rider[0].shape[1]
            self.unit = rider[0].shape[1:]
        count = self.net.chips // step
        riders, cut = self.riders, self.cut

        def sum_chips(held_ref, got_ref, *refs):
            away_ref, out_ref = refs[-2:]
            for k in range(count):
                target = away_ref if k % 2 else out_ref
                for part in range(cut):
                    if rider:
                        rows = slice(part * own // cut, (part + 1) * own // cut)
                        total = held_ref[k, rows] + got_ref[k, rows]
                    else:
                        total = held_ref[k * cut + part] + got_ref[k * cut + part]
                    target[k // 2 * cut + part] = total
            for k in range(riders):
                if rider:
                    total = refs[0][k] + refs[1][k]
                else:
                    total = held_ref[count * cut + k] + got_ref[count * cut + k]
                away_ref[count // 2 * cut + k] = total
                out_ref[count // 2 * cut + k] = total

        outs = [self.shape(count // 2 * cut + riders)] * 2
        away, self.held = self.order(sum_chips, [self.held, self.got, *rider], outs)
        self.got = self.net.across(away, step)

    def chips(self):
        step = 2
        while step < self.net.chips:
            self.chip(step)
            step *= 2

    def three(self):
        outs = [self.shape(self.cut + self.riders)]
        self.held, = self.order(sum_kernel, [self.held, self.got], outs)
        self.got = self.net.swap(self.held, 2)

    def four(self):
        riders, cut = self.riders, self.cut

        def join_quarters(held_ref, got_ref, out_ref):
            for k in range(cut):
                out_ref[k] = held_ref[k]
                out_ref[cut + k] = got_ref[k]
            for k in range(riders):
                out_ref[2 * cut + k] = held_ref[cut + k] + got_ref[cut + k]

        outs = [self.shape(2 * cut + riders)]
        self.held, = self.order(join_quarters, [self.held, self.got], outs)
        self.got = self.net.swap(self.held, 1)


def update_call(order, reduction, spots, arrays, more=(), more_grads=None):
    count = len(arrays) + len(more)
    cut = reduction.cut

    def update_weights(pair_ref, got_ref, *refs):
        ins, targets, scratch = refs[:count], refs[count : 2 * count], refs[2 * count :]
        pairs = list(zip(scratch[:count], targets))
        sems = scratch[count]
        sends = update_quarters(spots, cut, pair_ref, got_ref, ins, pairs, sems)
        if more:
            first = 2 * cut
            riders = pair_ref[first:].astype(F32) + got_ref[first:].astype(F32)
            grads = more_grads(riders, *scratch[count + 1 :])
            width = grads.shape[1] // 4
            for k in range(4):
                at = (slice(None), slice(k * width, (k + 1) * width))
                values = adamw(*(ref[at] for ref in ins[len(arrays) :]), grads[at])
                for j, value in enumerate(values, len(arrays)):
                    scratch[j][at] = value
                    sends.append(pltpu.make_async_copy(
                        scratch[j].at[at], targets[j].at[at], sems.at[j, k]
                    ))
                    sends[-1].start()
        for send in sends:
            send.wait()

    every = [*arrays, *more]
    scratch = [pltpu.VMEM(a.shape, F32) for a in every]
    scratch.append(pltpu.SemaphoreType.DMA((count, 4 * cut)))
    if more:
        scratch.append(pltpu.VMEM((8, 5 * D), F32))
        scratch.append(pltpu.VMEM((reduction.riders, *reduction.unit), F32))
    return order(
        update_weights, [reduction.held, reduction.got, *every],
        [jax.ShapeDtypeStruct(a.shape, F32) for a in every], scratch,
        mib=12, free=range(2, 2 + count), whole=range(count),
    )


class Held:
    pass


def per_device(
    inputs, sigma, neighbours, cotangent,
    inward_weight, inward_first, inward_second,
    outward_weight, outward_first, outward_second,
    expand_weight, expand_first, expand_second,
    contract_weight, contract_first, contract_second,
    modulate_weight, modulate_first, modulate_second,
):
    net = Net()
    order = Order()
    h = Held()
    states = inputs[0]
    cot = cotangent[0]
    rows = states.shape[0]
    own, hidden = expand_weight.shape
    chips = net.chips
    low = lambda *shape: pinned(shape, BF16)
    full = lambda *shape: pinned(shape, F32)
    split = rows // 2
    slab = (own, 3 * D // 4)
    rider_slab = (own // 2 if own % 32 == 0 else own, 3 * D // 4)
    riders = -(-net.noise * RIDER_ROWS // rider_slab[0])
    cond = fourier(sigma).astype(BF16)

    w_in = Gathering(
        net, order, pack_inward_kernel, lambda: ([inward_weight], (0,)), (own, 3 * D // 2)
    )
    w_exp = Gathering(
        net, order, pack_expand_kernel, lambda: ([h.expand, h.outward], ()),
        (own, hidden // 2 + D // 2),
    )
    w_con = Gathering(
        net, order, pack_contract_kernel, lambda: ([h.contract], ()), (own, 2 * D), stacked=True
    )
    g_in, g_exp, g_con = (Reduction(net, order) for _ in range(3))

    def load_arrays(kernel, arrays):
        return order(
            kernel, arrays, [pinned(a.shape, a.dtype) for a in arrays],
            [pltpu.SemaphoreType.DMA((len(arrays),))], loose=range(len(arrays)),
        )

    def load():
        h.expand, h.outward, h.contract = load_arrays(
            load_kernel, [expand_weight, outward_weight, contract_weight]
        )

    def load_more():
        h.modulate, h.neighbours, h.states, h.cot = load_arrays(
            load_more_kernel, [modulate_weight, neighbours[0].T, states, cot]
        )

    def mod():
        if not net.quick:
            h.mod, = order(modulation_kernel, [cond, h.modulate], [full(1, 4 * D)], free=(0,))
            h.mod_got = net.cores(h.mod)
            return
        wide = RIM + 16
        h.mod, core, h.edge = order(
            open_kernel, [cond, h.modulate, h.states],
            [full(1, 4 * D), low(wide, D), low(RIM, D)], [pltpu.VMEM((wide, D), F32)], free=(0,),
        )
        h.mod_got = net.cores(core)

    def mod_sum():
        h.mod, = order(sum_kernel, [h.mod, h.mod_got], [full(1, 4 * D)])

    def mod_core():
        if not net.quick:
            mod_sum()
            h.mod_got = net.across(h.mod, 1)
            return
        wide = RIM + 16
        h.mod, core_edge, send = order(
            open_core_kernel, [h.mod, h.mod_got, h.edge],
            [full(1, 4 * D), low(RIM, D), low(wide, D)], [pltpu.VMEM((wide, D), F32)],
        )
        h.edges = [core_edge]
        h.mod_got = net.beside(send)

    def mod_near():
        if net.quick:
            near, chip_edge, h.mod = order(
                open_chip_kernel, [h.mod, h.mod_got],
                [full(1, 4 * D), low(RIM, D), full(1, 4 * D)],
            )
            h.edges.append(chip_edge)
            h.mod_got = net.cores(near)
            return
        step = 2
        while step < chips:
            mod_sum()
            h.mod_got = net.across(h.mod, step)
            step *= 2

    def mod_far():
        if net.quick:
            h.mod, send = order(
                open_far_kernel, [h.mod, h.mod_got], [full(1, 4 * D), full(1, 4 * D)]
            )
            h.mod_got = net.beside(send)
            return
        core, chip = order(edges_kernel, [h.states], [low(RIM, D), low(RIM, D)])
        h.edges = [net.cores(core), net.beside(chip)]

    def counts():
        kernel = functools.partial(count_kernel, rows * net.nodes)
        h.bias, = order(kernel, [h.neighbours], [full(rows, WINDOW)])

    def first():
        h.first, h.mod = order(
            first_kernel, [h.states, *h.edges, h.mod, h.mod_got],
            [low(rows + 2 * RIM, D), full(1, 4 * D)],
        )

    def joint():
        h.q, h.kv, h.w_in, h.attended, h.probs = order(
            joint_kernel, [h.first, h.bias, *w_in.parts],
            [low(rows, D), low(rows + 2 * RIM, 2 * D), low(D, 3 * D),
             low(rows, D), low(rows, HEADS * WINDOW)],
            mib=14,
        )

    def mlp():
        h.mixed, h.second, h.swished, h.slope, h.w_out, h.w_exp = order(
            mlp_forward_kernel, [h.attended, h.states, h.mod, *w_exp.parts],
            [full(rows, D), low(rows, D), low(rows, hidden), low(rows, hidden),
             low(D, D), low(D, hidden)],
            mib=12,
        )

    def con_grad():
        slots = low(4, chips, own, D)
        g_con.begin(*order(
            contract_grads_kernel, [h.swished, h.cot], [slots, slots],
            [pltpu.VMEM((hidden, D), F32)], mib=12,
        ))

    def back_low():
        h.up_low, h.second_low, h.w_con = order(
            mlp_backward_low_kernel, [h.slope, h.cot, h.w_exp, *w_con.parts],
            [low(split, hidden), full(split, D), low(hidden, D)], mib=10,
        )

    def back_high():
        h.up_high, h.second_high = order(
            mlp_backward_high_kernel, [h.slope, h.cot, h.w_exp, h.w_con],
            [low(split, hidden), full(split, D)], mib=10,
        )

    def final():
        h.final, h.input_grad = order(
            final_kernel, [h.mixed, h.swished, h.w_con, h.input_grad],
            [jax.ShapeDtypeStruct((rows, D), BF16), jax.ShapeDtypeStruct((rows, D), F32)],
            [pltpu.VMEM((rows, D), BF16), pltpu.SemaphoreType.DMA((1 + rows // PIECE,))],
            mib=8, whole=(0, 1),
        )

    def norm():
        h.d_mixed, h.d_low, h.d_attended, h.sums_two = order(
            norm_backward_kernel,
            [h.mixed, h.second_low, h.second_high, h.cot, h.mod, h.w_out],
            [full(rows, D), low(rows, D), low(rows, D), full(8, D)], mib=8,
        )

    def exp_grad():
        slots = low(4, chips, own, hidden // 4 + D // 4)
        g_exp.begin(*order(
            expand_grads_kernel, [h.second, h.up_low, h.up_high, h.attended, h.d_low],
            [slots, slots], [pltpu.VMEM((D, hidden), F32), pltpu.VMEM((D, D), F32)], mib=12,
        ))

    def attn():
        h.dq, h.dkv, core, chip = order(
            attend_back_kernel, [h.q, h.kv, h.probs, h.d_attended],
            [low(rows, D), low(rows + 2 * RIM, 2 * D), low(RIM, 2 * D), low(RIM, 2 * D)],
            mib=12,
        )
        h.edges = [net.cores(core), net.beside(chip)]

    def edge_take():
        h.edges = [w_in.take(edge) for edge in h.edges]

    def in_grad():
        slots = low(4, chips, *slab)
        g_in.begin(*order(
            in_grads_kernel, [h.first, h.dq, h.dkv], [slots, slots],
            [pltpu.VMEM((D, 3 * D), F32)], mib=8,
        ))

    def input_step():
        kernel = functools.partial(input_grad_kernel, net.noise, net.nodes)
        h.input_grad, rider = order(
            kernel,
            [h.dq, h.dkv, *h.edges, h.states, h.d_mixed, h.mod, h.w_in, h.sums_two, cond],
            [full(rows, D), low(riders, *rider_slab)],
            [pltpu.VMEM((rows + 2 * RIM, 2 * D), BF16), pltpu.VMEM((8, 5 * D), F32),
             pltpu.VMEM((riders, *rider_slab), F32)],
            mib=10, free=(9,),
        )
        h.rider = (rider, net.cores(rider))

    def in_chip():
        g_in.chip(1, h.rider)

    def con_up():
        h.contract_new = update_call(
            order, g_con, [(slice(None), True)],
            [contract_weight, contract_first, contract_second],
        )

    def exp_up():
        cut = hidden // 4
        h.expand_new = update_call(
            order, g_exp, [(slice(None, cut), False), (slice(cut, None), False)],
            [expand_weight, expand_first, expand_second,
             outward_weight, outward_first, outward_second],
        )

    def in_up():
        h.inward_new = update_call(
            order, g_in, [(slice(None), False)], [inward_weight, inward_first, inward_second],
            (modulate_weight, modulate_first, modulate_second),
            functools.partial(modulate_grads, net.noise, own),
        )

    plan = (
        (w_in.pack, 0), (load_more, 10), (load, 0), (w_exp.pack, 1), (mod, 200), (w_in.swap, 100),
        (w_con.pack, 20), (mod_core, 0), (w_in.near, 0), (w_exp.swap, 10), (mod_near, 20),
        (counts, 0), (mod_far, 0), (w_con.swap, 30), (w_exp.near, 0), (w_in.core, 0),
        (w_in.far, 20), (w_con.near, 30), (first, 120), (joint, 20), (w_exp.core, 0),
        (w_exp.far, 200), (mlp, 200), (w_con.core, 1), (w_con.far, 0), (con_grad, 0),
        (back_low, 80), (g_con.one, 50), (back_high, 0), (norm, 120), (attn, 10), (exp_grad, 30),
        (g_con.two, 30), (in_grad, 80), (g_exp.one, 1), (g_con.chip, 200), (g_in.one, 0),
        (g_con.chips, 0), (edge_take, 0), (g_exp.two, 10), (input_step, 20), (g_con.three, 30),
        (g_in.two, 80), (g_exp.chip, 0), (final, 0), (in_chip, 120), (g_exp.chips, 5),
        (g_in.chips, 0), (g_con.four, 0), (g_exp.three, 120), (g_in.three, 30), (g_exp.four, 5),
        (g_in.four, 0), (con_up, 10), (exp_up, 0), (in_up, 100),
    )
    for step, tenths in plan:
        order.tenths = tenths
        step()

    return (
        h.final[None], h.input_grad[None], *h.inward_new[:3], *h.expand_new[3:],
        *h.expand_new[:3], *h.contract_new, *h.inward_new[3:],
    )


def solution(mesh):
    grid = P(NOISE, NODES, None)
    shard = P(NODES, None)
    return jax.shard_map(
        per_device,
        mesh=mesh,
        in_specs=(grid, P(NOISE), grid, grid) + (shard,) * 15,
        out_specs=(grid, grid) + (shard,) * 15,
        check_vma=False,
    )
```
